32 devices in a mesh: sec: 2 (over y), gz: 16 (over z, x, core).
Axes of the slice: x: 2, y: 2, z: 4, core: 2. Of those that a mesh axis runs over, the one named last changes fastest.
Arguments:
- velocity: float32 [2, 3, 32, 512, 256], P('sec', None, 'gz'), may hold values from -6 to 6
- eddy_viscosity: float32 [2, 32, 512, 256], P('sec', 'gz'), may hold values from 0.05 to 0.5
- turbine_mask: int32 [32, 512, 256], P('gz'), may hold values 0 or 1
- fringe_columns: int32 [64], replicated, may hold values from 0 to 511, as said below
Outputs:
- new_velocity: float32 [2, 3, 32, 512, 256], P('sec', None, 'gz')
The draws below stay inside these ranges and needn't reach their ends.
Inputs may be any that keep to these rules, and one draw needn't show every extreme that they name: `fringe_columns`: 64 distinct streamwise column indices.
All inputs are finite; a program needn't handle non-finite values. No bound on the sum of `turbine_mask` on one device may be relied on, other than what follows from the above.
Results may differ from the reference program's by a relative error of at most 0.0003.
Values sent between devices are 32-bit elements; how exact they have to be, the bound alone decides.
No kernel may reach another device: no remote copies, remote signals or barrier semaphores. Data moves between devices by JAX's collectives and lax.ppermute only.
A program may use at most 128 MiB of HBM per device.

```python
import math
import jax
import jax.numpy as jnp
from jax import lax

NX = 512
NY = 256
NF = 64
NZ = 32
N_SEC = 2


def draw_fringe_columns(key, part):
    return jax.random.permutation(key, NX)[:NF].astype(jnp.int32)


def with_ends(drawn, rng, least, top_value):
    place = [jax.random.randint(jax.random.fold_in(rng, axis), (), 0, length) for axis, length in enumerate(drawn.shape)]
    widest = drawn.shape.index(max(drawn.shape))
    next_to = place[:widest] + [(place[widest] + 1) % drawn.shape[widest]] + place[widest + 1:]
    return drawn.at[tuple(place)].set(least).at[tuple(next_to)].set(top_value)


def shard_levels(stream_key, dims, split, low, high):
    gain, own = 1.0, jax.random.fold_in(stream_key, 6)
    for dim, parts in split:
        draws = jnp.exp(jax.random.uniform(jax.random.fold_in(own, dim), (parts,), jnp.float32, low / len(split), high / len(split)))
        gain = gain * jnp.repeat(draws, dims[dim] // parts).reshape([-1 if axis == dim else 1 for axis in range(len(dims))])
    return gain


def noise(rng, dims, scale, reach, split=(), held_as=jnp.bfloat16):
    entries = scale * jax.random.normal(rng, dims, jnp.float32)
    if split:
        entries = entries * shard_levels(rng, dims, split, -0.22, 0.18)
    return jnp.clip(entries, -reach, reach).astype(held_as)


def setup_inputs(seed: int = 0) -> dict:
    splits = jax.random.split(jax.random.key(seed), 5)
    velocity = noise(splits[0], (N_SEC, 3, NZ, NX, NY), 1.0, 6.0, ((0, 2), (2, 16)), jnp.float32)
    eddy_viscosity = jnp.clip(jnp.exp(math.log(0.5) - 2.3025851 * jax.random.uniform(splits[1], (N_SEC, NZ, NX, NY), jnp.float32) ** shard_levels(splits[1], (N_SEC, NZ, NX, NY), ((0, 2), (1, 16)), -0.2, 0.2)), 0.05, 0.5)
    turbine_mask = with_ends((jax.random.randint(splits[2], (NZ, NX, NY), 0, 16) < 1).astype(jnp.int32), jax.random.fold_in(splits[2], 1), 0, 1)
    fringe_columns = draw_fringe_columns(jax.random.fold_in(splits[4], 71), 0)
    return {"velocity": velocity, "eddy_viscosity": eddy_viscosity, "turbine_mask": turbine_mask, "fringe_columns": fringe_columns}


step_size = 0.1
drag_coef = 0.75
cell_width = 4.0
highest = lax.Precision.HIGHEST

def derivative_table(length, cutoff):
    position = jnp.arange(length, dtype=jnp.int32)
    wavenumber = jnp.arange(1, cutoff + 1, dtype=jnp.int32)
    phases = position[:, None] * wavenumber[None, :] % length
    angles = 2.0 * math.pi / length * phases.astype(jnp.float32)
    sine_table = jnp.sin(angles)
    cosines = jnp.cos(angles)
    weight = (4.0 * math.pi / (length * length * cell_width) * wavenumber.astype(jnp.float32))[None, :]
    return jnp.dot(cosines * weight, sine_table.T, precision=highest) - jnp.dot(sine_table * weight, cosines.T, precision=highest)

def real_basis(length):
    midpoint = length // 2
    row_index = jnp.arange(length, dtype=jnp.int32)
    position = jnp.arange(length, dtype=jnp.int32)
    wavenumber = jnp.where(row_index <= midpoint, row_index, row_index - midpoint)
    phases = wavenumber[:, None] * position[None, :] % length
    angles = 2.0 * math.pi / length * phases.astype(jnp.float32)
    scales = jnp.where((row_index == 0) | (row_index == midpoint), math.sqrt(1.0 / length), math.sqrt(2.0 / length)).astype(jnp.float32)
    shapes = jnp.where((row_index <= midpoint)[:, None], jnp.cos(angles), jnp.sin(angles))
    return scales[:, None] * shapes

def wave_square(row_index, length):
    midpoint = length // 2
    wavenumber = jnp.where(row_index < midpoint, row_index, jnp.where(row_index == midpoint, 0, row_index - midpoint))
    scaled = 2.0 * math.pi / (length * cell_width) * wavenumber.astype(jnp.float32)
    return -(scaled * scaled)

def cosine_basis(length):
    mode_index = jnp.arange(length, dtype=jnp.int32)
    position = jnp.arange(length, dtype=jnp.int32)
    phases = mode_index[:, None] * (2 * position[None, :] + 1) % (4 * length)
    angles = math.pi / (2 * length) * phases.astype(jnp.float32)
    scales = jnp.where(mode_index == 0, math.sqrt(1.0 / length), math.sqrt(2.0 / length)).astype(jnp.float32)
    return scales[:, None] * jnp.cos(angles)

def vertical_eigen(mode_index, length):
    sines = jnp.sin(math.pi / (2 * length) * mode_index.astype(jnp.float32))
    return -4.0 * sines * sines

def column_inverse(height, length_x, length_y, first_column, column_count):
    mode_index = jnp.arange(height, dtype=jnp.int32)
    column = first_column + jnp.arange(column_count, dtype=jnp.int32)
    row_x = column // length_y
    row_y = column % length_y
    eigenvalue = vertical_eigen(mode_index, height)[:, None] + wave_square(row_x, length_x)[None, :] + wave_square(row_y, length_y)[None, :]
    null_x = (row_x == 0) | (row_x == length_x // 2)
    null_y = (row_y == 0) | (row_y == length_y // 2)
    null_mode = (mode_index == 0)[:, None] & (null_x & null_y)[None, :]
    return jnp.where(null_mode, 0.0, 1.0 / jnp.where(null_mode, -1.0, eigenvalue))

def tendency(current, viscosity, drag_field, dealias_x, dealias_y):
    rounded = lax.optimization_barrier(current.astype(jnp.bfloat16)).astype(jnp.float32)
    grad_x = jnp.einsum('ij,czjy->cziy', dealias_x, rounded)
    grad_y = jnp.einsum('czxj,ij->czxi', rounded, dealias_y)
    padded = jnp.pad(current, ((0, 0), (1, 1), (0, 0), (0, 0)))
    upper_plane = padded[:, 2:]
    lower_plane = padded[:, :-2]
    grad_z = 0.5 * (upper_plane - lower_plane)
    laplace = upper_plane - 2.0 * current + lower_plane
    advection = -(current[0] * grad_x + current[1] * grad_y + current[2] * grad_z)
    return advection + viscosity * laplace - drag_field * jnp.abs(current[0]) * current

def project(current, full_x, full_y, basis_x, basis_y, basis_z, inverse):
    height = current.shape[1]
    length_x = current.shape[2]
    length_y = current.shape[3]
    at_lid = (jnp.arange(height, dtype=jnp.int32) == height - 1)[:, None, None]
    w_face = jnp.where(at_lid, 0.0, current[2])
    beneath = jnp.pad(w_face, ((1, 0), (0, 0), (0, 0)))[:-1]
    divergence = jnp.einsum('ij,zjy->ziy', full_x, current[0], precision=highest) + jnp.einsum('zxj,ij->zxi', current[1], full_y, precision=highest)
    source = divergence + w_face - beneath
    partial_value = jnp.einsum('ax,zxy->zay', basis_x, source, precision=highest)
    spectra = jnp.einsum('zay,by->zab', partial_value, basis_y, precision=highest).reshape(height, length_x * length_y)
    solved = jnp.dot(basis_z, spectra, precision=highest) * inverse
    solved = jnp.dot(basis_z.T, solved, precision=highest).reshape(height, length_x, length_y)
    partial_value = jnp.einsum('ax,zab->zxb', basis_x, solved, precision=highest)
    pressure = jnp.einsum('zxb,by->zxy', partial_value, basis_y, precision=highest)
    overhead = jnp.pad(pressure, ((0, 1), (0, 0), (0, 0)))[1:]
    lift = jnp.where(at_lid, 0.0, overhead - pressure)
    new_u = current[0] - jnp.einsum('ij,zjy->ziy', full_x, pressure, precision=highest)
    new_v = current[1] - jnp.einsum('zxj,ij->zxi', pressure, full_y, precision=highest)
    return jnp.stack([new_u, new_v, w_face - lift])

def reference(velocity, eddy_viscosity, turbine_mask, fringe_columns):
    height = velocity.shape[2]
    length_x = velocity.shape[3]
    length_y = velocity.shape[4]
    dealias_x = lax.optimization_barrier(derivative_table(length_x, (length_x - 1) // 3).astype(jnp.bfloat16)).astype(jnp.float32)
    dealias_y = lax.optimization_barrier(derivative_table(length_y, (length_y - 1) // 3).astype(jnp.bfloat16)).astype(jnp.float32)
    full_x = derivative_table(length_x, length_x // 2 - 1)
    full_y = derivative_table(length_y, length_y // 2 - 1)
    basis_x = real_basis(length_x)
    basis_y = real_basis(length_y)
    basis_z = cosine_basis(height)
    inverse = column_inverse(height, length_x, length_y, jnp.int32(0), length_x * length_y)
    farm_drag = drag_coef * turbine_mask.astype(jnp.float32)
    tables = (full_x, full_y, basis_x, basis_y, basis_z, inverse)

    def inflow(precursor, farm):
        return farm.at[:, :, fringe_columns, :].set(precursor[:, :, fringe_columns, :])
    precursor_start = velocity[0]
    farm_start = inflow(velocity[0], velocity[1])
    precursor_mid = project(precursor_start + step_size * tendency(precursor_start, eddy_viscosity[0], 0.0, dealias_x, dealias_y), *tables)
    farm_mid = project(farm_start + step_size * tendency(farm_start, eddy_viscosity[1], farm_drag, dealias_x, dealias_y), *tables)
    farm_mid = inflow(precursor_mid, farm_mid)
    precursor_end = project(0.5 * (precursor_start + precursor_mid + step_size * tendency(precursor_mid, eddy_viscosity[0], 0.0, dealias_x, dealias_y)), *tables)
    farm_end = project(0.5 * (farm_start + farm_mid + step_size * tendency(farm_mid, eddy_viscosity[1], farm_drag, dealias_x, dealias_y)), *tables)
    return jnp.stack([precursor_end, farm_end])
```

```python
import functools
import math

import jax
import jax.numpy as jnp
import ml_dtypes
import numpy as np
from jax import lax
from jax.experimental import pallas as pl
from jax.experimental.pallas import tpu as pltpu
from jax.sharding import Mesh
from jax.sharding import PartitionSpec as P

step_size = 0.1
drag_coef = 0.75
cell_width = 4.0
half_type = jnp.bfloat16
full_type = jnp.float32
vmem_bytes = 56 * 1024 * 1024
levels_axis = ("chip", "core")
every_axis = ("sec", "chip", "core")


def derivative_table(length, cutoff):
    offset = np.arange(length)
    wavenumber = np.arange(1, cutoff + 1)
    phases = offset[:, None] * wavenumber[None, :] % length
    waves = np.sin(2.0 * math.pi / length * phases)
    first = -(2.0 / (cell_width * length)) * (waves @ (2.0 * math.pi / length * wavenumber))
    return first[(offset[:, None] - offset[None, :]) % length]


def real_basis(length):
    midpoint = length // 2
    row = np.arange(length)
    wavenumber = np.where(row <= midpoint, row, row - midpoint)
    angles = 2.0 * math.pi / length * (wavenumber[:, None] * row[None, :] % length)
    scales = np.where((row == 0) | (row == midpoint), math.sqrt(1.0 / length), math.sqrt(2.0 / length))
    return scales[:, None] * np.where((row <= midpoint)[:, None], np.cos(angles), np.sin(angles))


def wave_square(length):
    midpoint = length // 2
    row = np.arange(length)
    wavenumber = np.where(row < midpoint, row, np.where(row == midpoint, 0, row - midpoint))
    return (2.0 * math.pi / (length * cell_width) * wavenumber) ** 2


def high_low(table):
    table = np.asarray(table, np.float32)
    high = table.astype(ml_dtypes.bfloat16)
    low = (table - high.astype(np.float32)).astype(ml_dtypes.bfloat16)
    return np.stack([high, low], axis=-3)


def build_tables(length_x, length_y):
    mid = length_x // 2
    full_x = derivative_table(length_x, length_x // 2 - 1)
    full_y = derivative_table(length_y, length_y // 2 - 1)
    basis_x = real_basis(length_x)
    basis_y = real_basis(length_y)
    left_part, right_part = full_x[:mid, :mid], full_x[:mid, mid:]
    derived = full_x @ basis_x.T
    squares = wave_square(length_x)[:, None] + wave_square(length_y)[None, :]
    decay = 2.0 * np.arcsinh(0.5 * np.sqrt(squares))
    return {
        "dealias_x": derivative_table(length_x, (length_x - 1) // 3).astype(ml_dtypes.bfloat16),
        "dealias_y": derivative_table(length_y, (length_y - 1) // 3).T.astype(ml_dtypes.bfloat16),
        "slope_x": high_low(np.stack([left_part + right_part, left_part - right_part])),
        "slope_y": high_low(full_y.T),
        "into_x": high_low(np.stack([basis_x[0::2, :mid], basis_x[1::2, :mid]])),
        "into_y": high_low(basis_y.T),
        "from_x": high_low(np.stack([basis_x[0::2, :mid].T, basis_x[1::2, :mid].T])),
        "from_y": high_low(basis_y),
        "from_slope_x": high_low(np.stack([derived[:mid, 0::2], derived[:mid, 1::2]])),
        "from_slope_y": high_low(basis_y @ full_y.T),
        "decay": np.stack([decay[0::2], decay[1::2]]).astype(np.float32),
    }


def product(one, other):
    return jnp.dot(one, other, preferred_element_type=full_type)


def halves(block):
    high = block.astype(half_type)
    return high, (block - high.astype(full_type)).astype(half_type)


def from_left(table, block):
    high, low = halves(block)
    return product(table[0], high) + product(table[0], low) + product(table[1], high)


def from_right(block, table):
    high, low = halves(block)
    return product(high, table[0]) + product(low, table[0]) + product(high, table[1])


def vmem():
    return pl.BlockSpec(memory_space=pltpu.VMEM)


def smem():
    return pl.BlockSpec(memory_space=pltpu.SMEM)


def hbm():
    return pl.BlockSpec(memory_space=pl.ANY)


def call(kernel, outs, in_specs, scratch, flops, args):
    moved = sum(math.prod(a.shape) * 4 for a in (*outs, *args))
    return pl.pallas_call(
        kernel,
        out_shape=outs,
        in_specs=in_specs,
        out_specs=tuple(vmem() for _ in outs),
        scratch_shapes=scratch,
        compiler_params=pltpu.CompilerParams(vmem_limit_bytes=vmem_bytes),
        cost_estimate=pl.CostEstimate(flops=int(flops), bytes_accessed=moved, transcendentals=0),
    )(*args)


def shaped(*dims, kind=full_type):
    return jax.ShapeDtypeStruct(dims, kind)


def insert_columns(target, columns, low, high, index, depth):
    def one(i, carry):
        row = pl.ds(index[i], 1)
        here = pl.ds(i, 1)
        for c in range(3):
            target[c, 0, row, :] = low[c, here, :]
            for z in range(depth):
                target[c, 1 + z, row, :] = columns[c, z, here, :]
            target[c, 1 + depth, row, :] = high[c, here, :]
        return carry

    lax.fori_loop(0, index.shape[0], one, 0)


def tendency_steps(state, rounded, viscosity, mask, drag, dealias_x, dealias_y, put):
    depth = state.shape[1] - 2
    length_x = state.shape[2]
    rows = length_x // 2

    def level(z, carry):
        for c in range(3):
            rounded[c] = state[c, z + 1].astype(half_type)

        def block(b, inner):
            part = pl.ds(pl.multiple_of(b * rows, rows), rows)
            u, v, w = (state[c, z + 1, part, :] for c in range(3))
            slow = drag * mask[z, part, :].astype(full_type) * jnp.abs(u)
            nu = viscosity[z, part, :]
            for c in range(3):
                center = state[c, z + 1, part, :]
                upper = state[c, z + 2, part, :]
                lower = state[c, z, part, :]
                grad_x = product(dealias_x[part, :], rounded[c])
                grad_y = product(rounded[c, part, :], dealias_y[...])
                advected = u * grad_x + v * grad_y + w * (0.5 * (upper - lower))
                change = nu * (upper - 2.0 * center + lower) - advected - slow * center
                put(c, z, part, center, change)
            return inner

        lax.fori_loop(0, length_x // rows, block, 0)
        return carry

    lax.fori_loop(0, depth, level, 0)


def folded(block, sign):
    mid = block.shape[0] // 2
    return block[:mid] + sign * block[mid:]


def source_spectra(state, parts, core, slope_x, slope_y, into_x, into_y, sources):
    depth = state.shape[1]
    for slot, out in enumerate(parts):
        half = core if slot == 0 else 1 - core
        sign = (1 - 2 * half).astype(full_type)

        def level(z, carry, half=half, sign=sign):
            w = folded(state[2, z], sign)
            below = folded(state[2, jnp.maximum(z - 1, 0)], sign)
            spread = from_left(slope_x[half], folded(state[0, z], sign))
            spread += from_right(folded(state[1, z], sign), slope_y)
            sources[z] = spread + w - jnp.where(z > 0, below, 0.0)
            return carry

        lax.fori_loop(0, depth, level, 0)
        sources[depth] = folded(state[2, depth - 1], sign)

        def transform(i, carry, half=half, out=out):
            out[i] = from_right(from_left(into_x[half], sources[i]), into_y)
            return carry

        lax.fori_loop(0, depth + 1, transform, 0)


def first_kernel(
    flags, index, velocity, low, high, columns, columns_low, columns_high, viscosity, mask,
    dealias_x, dealias_y, slope_x, slope_y, into_x, into_y,
    middle, upward, downward, mine, theirs,
    state, rounded, sources, slopes, sems,
):
    depth = middle.shape[1]
    mid = middle.shape[2] // 2
    is_farm, core, is_lid = flags[0], flags[1], flags[3]
    copies = [
        pltpu.make_async_copy(velocity, state.at[:, pl.ds(1, depth)], sems.at[0]),
        pltpu.make_async_copy(low, state.at[:, 0], sems.at[1]),
        pltpu.make_async_copy(high, state.at[:, depth + 1], sems.at[2]),
    ]
    for copy in copies:
        copy.start()
    for copy in copies:
        copy.wait()

    @pl.when(is_farm == 1)
    def _():
        insert_columns(state, columns, columns_low, columns_high, index, depth)

    drag = drag_coef * is_farm.astype(full_type)

    def put(c, z, part, center, change):
        moved = center + step_size * change
        if c == 2:
            moved = jnp.where((is_lid == 1) & (z == depth - 1), 0.0, moved)
        middle[c, z, part, :] = moved

    tendency_steps(state, rounded, viscosity, mask, drag, dealias_x, dealias_y, put)
    source_spectra(middle, (mine, theirs), core, slope_x, slope_y, into_x, into_y, sources)
    downward[0] = middle[0, 0]
    downward[1] = middle[1, 0]
    top = depth - 1
    for half in range(2):
        slopes[half] = from_left(slope_x[half], folded(middle[2, top], 1.0 - 2.0 * half))
    upward[0, :mid] = middle[0, top, :mid] + 0.5 * (slopes[0] + slopes[1])
    upward[0, mid:] = middle[0, top, mid:] + 0.5 * (slopes[0] - slopes[1])
    upward[1] = middle[1, top] + from_right(middle[2, top], slope_y)


def second_kernel(
    flags, index, extended, columns, velocity, start_columns, viscosity, mask,
    dealias_x, dealias_y, slope_x, slope_y, into_x, into_y,
    final, mine, theirs,
    state, start, rounded, sources, sems,
):
    depth = final.shape[1]
    is_farm, core, is_lid = flags[0], flags[1], flags[3]
    copies = [
        pltpu.make_async_copy(extended, state, sems.at[0]),
        pltpu.make_async_copy(velocity, start, sems.at[1]),
    ]
    for copy in copies:
        copy.start()
    for copy in copies:
        copy.wait()

    @pl.when(is_farm == 1)
    def _():
        def one(i, carry):
            row = pl.ds(index[i], 1)
            here = pl.ds(i, 1)
            for c in range(3):
                for z in range(depth + 2):
                    state[c, z, row, :] = columns[c, z, here, :]
                for z in range(depth):
                    start[c, z, row, :] = start_columns[c, z, here, :]
            return carry

        lax.fori_loop(0, index.shape[0], one, 0)

    drag = drag_coef * is_farm.astype(full_type)

    def put(c, z, part, center, change):
        moved = 0.5 * (start[c, z, part, :] + center + step_size * change)
        if c == 2:
            moved = jnp.where((is_lid == 1) & (z == depth - 1), 0.0, moved)
        final[c, z, part, :] = moved

    tendency_steps(state, rounded, viscosity, mask, drag, dealias_x, dealias_y, put)
    source_spectra(final, (mine, theirs), core, slope_x, slope_y, into_x, into_y, sources)


def chip_levels(core, mine, other, depth):
    is_low = core == 0
    low = [jnp.where(is_low, mine[i], other[i]) for i in range(depth + 1)]
    high = [jnp.where(is_low, other[i], mine[i]) for i in range(depth + 1)]
    levels = low[:depth] + [high[0] - low[depth]] + high[1:depth]
    return levels, low[depth], high[depth]


class Coefficients:
    def __init__(self, stacked, count):
        self.mu = lambda: stacked[0]
        self.phi = lambda i: stacked[1 + i]
        self.psi = lambda i: stacked[2 + count + i]
        self.flux_low = lambda i: stacked[3 + 2 * count + i]
        self.flux_high = lambda i: stacked[3 + 3 * count + i]
        self.entry = lambda: stacked[4 + 4 * count]
        self.scale = lambda: stacked[5 + 4 * count]


def gather_kernel(flags, mine, other, stacked, out, work):
    core = flags[1]
    depth = mine.shape[0] - 1
    count = 2 * depth
    tables = Coefficients(stacked, count)
    levels, _, top = chip_levels(core, mine, other, depth)
    mu = tables.mu()
    forward = tables.phi(0) * levels[0]
    for i in range(1, count):
        forward = mu * forward + tables.phi(i) * levels[i]
    work[0] = mu * forward - tables.phi(count) * top
    backward = -tables.psi(count) * top
    for i in reversed(range(count)):
        backward = tables.psi(i) * levels[i] + mu * backward
    work[1] = backward
    chips = out.shape[0]
    rows = out.shape[1] // 2
    for chip in range(chips):
        out[chip, :rows] = work[0, chip * rows : (chip + 1) * rows]
        out[chip, rows:] = work[1, chip * rows : (chip + 1) * rows]


def scan_kernel(received, ratio, out):
    chips = received.shape[0]
    rows = received.shape[1] // 2
    factor = ratio[...]
    carried = jnp.zeros_like(factor)
    for chip in range(chips):
        out[chip, :rows] = carried
        carried = factor * carried + received[chip, :rows]
    carried = jnp.zeros_like(factor)
    for chip in reversed(range(chips)):
        out[chip, rows:] = carried
        carried = factor * carried + received[chip, rows:]


def solve_kernel(flags, mine, other, stacked, scanned, own, partner, work):
    core = flags[1]
    depth = mine.shape[0] - 1
    count = 2 * depth
    tables = Coefficients(stacked, count)
    chips = scanned.shape[0]
    rows = scanned.shape[1] // 2
    for chip in range(chips):
        work[0, chip * rows : (chip + 1) * rows] = scanned[chip, :rows]
        work[1, chip * rows : (chip + 1) * rows] = scanned[chip, rows:]
    levels, between, top = chip_levels(core, mine, other, depth)
    mu = tables.mu()
    forward = [work[0] + tables.phi(0) * levels[0]]
    for i in range(1, count):
        forward.append(mu * forward[-1] + tables.phi(i) * levels[i])
    backward = [work[1] - tables.psi(count) * top]
    for i in reversed(range(1, count)):
        backward.append(tables.psi(i) * levels[i] + mu * backward[-1])
    backward.reverse()
    flux = [
        tables.flux_low(i) * forward[i] - tables.flux_high(i + 1) * backward[i]
        for i in range(count)
    ]
    under = tables.entry() * work[0] - tables.flux_high(0) * (
        tables.psi(0) * levels[0] + mu * backward[0]
    )
    pressure = [
        -tables.scale() * (tables.psi(i) * forward[i] + mu * tables.phi(i) * backward[i])
        for i in (0, depth)
    ]
    low = [pressure[0], *flux[:depth], under]
    high = [pressure[1], *flux[depth:], flux[depth - 1] - between]
    is_low = core == 0
    for i in range(depth + 2):
        own[i] = jnp.where(is_low, low[i], high[i])
        partner[i] = jnp.where(is_low, high[i], low[i])


def physical_fields(core, mine, other, from_x, from_y, from_slope_x, from_slope_y, spectra, slots, ghosts):
    depth = mine.shape[0] - 2
    pressures = depth + 2 if ghosts else depth
    first = 1 if ghosts else 0
    lifts = depth + 1 if ghosts else depth
    for half in range(2):
        chosen = [jnp.where(core == half, mine[i], other[i]) for i in range(depth + 2)]
        level = chosen[0]
        if ghosts:
            spectra[half, 0] = level - chosen[depth + 1]
        for z in range(depth):
            spectra[half, first + z] = level
            level = level + chosen[1 + z]
        if ghosts:
            spectra[half, first + depth] = level
        for z in range(lifts):
            spectra[half, pressures + z] = chosen[1 + z]

    def one(half, carry):
        def pressure(i, inner):
            block = spectra[half, i]
            slots[2 * i, half] = from_left(from_slope_x[half], from_right(block, from_y))
            slots[2 * i + 1, half] = from_left(from_x[half], from_right(block, from_slope_y))
            return inner

        lax.fori_loop(0, pressures, pressure, 0)

        def lift(i, inner):
            block = spectra[half, pressures + i]
            slots[2 * pressures + i, half] = from_left(from_x[half], from_right(block, from_y))
            return inner

        lax.fori_loop(0, lifts, lift, 0)
        return carry

    lax.fori_loop(0, 2, one, 0)


def unfolded(slots, i):
    return slots[i, 0] + slots[i, 1], slots[i, 0] - slots[i, 1]


def corrected_kernel(
    flags, mine, other, middle, from_below, from_above, slope_x, slope_y,
    from_x, from_y, from_slope_x, from_slope_y, index,
    out, columns,
    spectra, slots,
):
    core, is_floor, is_lid = flags[1], flags[2], flags[3]
    depth = middle.shape[1]
    mid = middle.shape[2] // 2
    physical_fields(
        core, mine, other, from_x, from_y, from_slope_x, from_slope_y, spectra, slots, True
    )
    pressures = depth + 2
    open_low = (1 - is_floor).astype(full_type)
    open_high = (1 - is_lid).astype(full_type)
    sides = (slice(0, mid), slice(mid, 2 * mid))
    for z in range(depth):
        for c in range(3):
            slot = 2 * (1 + z) + c if c < 2 else 2 * pressures + z
            for side, change in zip(sides, unfolded(slots, slot)):
                out[c, 1 + z, side] = middle[c, z, side] - change
    for c in range(2):
        for side, change in zip(sides, unfolded(slots, c)):
            out[c, 0, side] = open_low * (from_below[c, side] - change)
        for side, change in zip(sides, unfolded(slots, 2 * (depth + 1) + c)):
            out[c, depth + 1, side] = open_high * (from_above[c, side] - change)
    for side, change in zip(sides, unfolded(slots, 2 * pressures + depth)):
        out[2, 0, side] = -open_low * change
    for half in range(2):
        slots[0, half] = 0.5 * from_left(
            slope_x[half], folded(out[0, depth + 1], 1.0 - 2.0 * half)
        )
    for side, change in zip(sides, unfolded(slots, 0)):
        spread = change + from_right(out[1, depth + 1, side], slope_y)
        out[2, depth + 1, side] = open_high * (out[2, depth, side] - spread)

    def one(i, carry):
        row = pl.ds(index[i], 1)
        for c in range(3):
            for z in range(depth + 2):
                columns[c, z, pl.ds(i, 1), :] = out[c, z, row, :]
        return carry

    lax.fori_loop(0, index.shape[0], one, 0)


def last_kernel(
    flags, mine, other, final, from_x, from_y, from_slope_x, from_slope_y,
    out,
    spectra, slots,
):
    core = flags[1]
    depth = final.shape[1]
    mid = final.shape[2] // 2
    physical_fields(
        core, mine, other, from_x, from_y, from_slope_x, from_slope_y, spectra, slots, False
    )
    sides = (slice(0, mid), slice(mid, 2 * mid))
    for z in range(depth):
        for c in range(3):
            slot = 2 * z + c if c < 2 else 2 * depth + z
            for side, change in zip(sides, unfolded(slots, slot)):
                out[c, z, side] = final[c, z, side] - change


def coefficients(decay, first_level, count, height):
    def gap(steps):
        return -jnp.expm1(-steps * decay)

    still = decay == 0.0
    below = jnp.arange(count + 1, dtype=full_type)[:, None, None] + first_level
    mu = jnp.exp(-decay)
    safe = jnp.where(still, 1.0, gap(2.0 * height))

    def ratio(steps):
        return jnp.where(still, steps / height, gap(2.0 * steps) / safe)

    share = 1.0 / (1.0 + mu)
    phi = 1.0 + jnp.exp(-(2.0 * below + 1.0) * decay)
    psi = 1.0 + jnp.exp(-(2.0 * (height - below) - 1.0) * decay)
    flux_low = mu * share * ratio(height - 1.0 - below[:count])
    flux_high = mu * share * ratio(below)
    entry = share * ratio(height - below[:1])
    scale = jnp.where(still, 0.0, mu / (jnp.where(still, 1.0, gap(2.0)) * safe))
    return jnp.concatenate([mu[None], phi, psi, flux_low, flux_high, entry, scale[None]])


def local(velocity, eddy_viscosity, turbine_mask, fringe_columns):
    current = velocity[0]
    viscosity = eddy_viscosity[0]
    _, depth, length_x, length_y = current.shape
    mid = length_x // 2
    fringe = fringe_columns.shape[0]
    chips = lax.axis_size("chip")
    devices = 2 * chips
    height = devices * depth
    count = 2 * depth
    rows = mid // chips
    section = lax.axis_index("sec")
    chip = lax.axis_index("chip")
    core = lax.axis_index("core")
    place = 2 * chip + core
    is_farm = section == 1
    flags = jnp.stack([is_farm, core, place == 0, place == devices - 1]).astype(jnp.int32)
    tables = {name: jnp.asarray(table) for name, table in build_tables(length_x, length_y).items()}

    upward_route = [(i, i + 1) for i in range(devices - 1)]
    downward_route = [(i + 1, i) for i in range(devices - 1)]
    swap = [(0, 1), (1, 0)]

    def across(shift):
        return [
            (i, devices + i + shift) for i in range(devices) if 0 <= i + shift < devices
        ]

    low = lax.ppermute(current[:, depth - 1], levels_axis, upward_route)
    high = lax.ppermute(current[:, 0], levels_axis, downward_route)
    taken = current[:, :, fringe_columns, :]
    columns = lax.ppermute(taken, every_axis, across(0))
    columns_low = lax.ppermute(taken[:, depth - 1], every_axis, across(1))
    columns_high = lax.ppermute(taken[:, 0], every_axis, across(-1))

    decay = lax.dynamic_index_in_dim(tables["decay"], core, 0, keepdims=False)
    stacked = coefficients(decay, (chip * count).astype(full_type), count, float(height))
    ratio = jnp.exp(-float(count) * lax.dynamic_slice_in_dim(decay, chip * rows, rows, 0))

    block = length_x * length_y * 2
    spectrum = shaped(depth + 1, mid, length_y)
    solved = shaped(depth + 2, mid, length_y)
    message = shaped(chips, 2 * rows, length_y)
    tendency_tables = [tables["dealias_x"], tables["dealias_y"]]
    source_tables = [tables[n] for n in ("slope_x", "slope_y", "into_x", "into_y")]
    pressure_tables = [tables[n] for n in ("from_x", "from_y", "from_slope_x", "from_slope_y")]

    def solve(mine, theirs):
        other = lax.ppermute(theirs, "core", swap)
        (sums,) = call(
            gather_kernel, (message,), [smem(), vmem(), vmem(), vmem()],
            [pltpu.VMEM((2, mid, length_y), full_type)], 8 * count * block,
            (flags, mine, other, stacked),
        )
        sums = lax.all_to_all(sums, "chip", split_axis=0, concat_axis=0, tiled=True)
        (sums,) = call(scan_kernel, (message,), [vmem(), vmem()], [], 4 * block, (sums, ratio))
        sums = lax.all_to_all(sums, "chip", split_axis=0, concat_axis=0, tiled=True)
        own, partner = call(
            solve_kernel, (solved, solved), [smem()] + [vmem()] * 4,
            [pltpu.VMEM((2, mid, length_y), full_type)], 16 * count * block,
            (flags, mine, other, stacked, sums),
        )
        return own, lax.ppermute(partner, "core", swap)

    state_shape = (3, depth + 2, length_x, length_y)
    sources = pltpu.VMEM((depth + 1, mid, length_y), full_type)
    rounded = pltpu.VMEM((3, length_x, length_y), half_type)
    own_shape = shaped(3, depth, length_x, length_y)
    edge = shaped(2, length_x, length_y)
    tendency_flops = 3 * depth * block * (length_x + length_y)
    source_flops = 3 * depth * block * (length_x + 2 * length_y)

    middle, upward, downward, mine, theirs = call(
        first_kernel,
        (own_shape, edge, edge, spectrum, spectrum),
        [smem(), smem()] + [hbm()] * 3 + [vmem()] * 11,
        [
            pltpu.VMEM(state_shape, full_type), rounded, sources,
            pltpu.VMEM((2, mid, length_y), full_type), pltpu.SemaphoreType.DMA((3,)),
        ],
        tendency_flops + source_flops,
        (flags, fringe_columns, current, low, high, columns, columns_low, columns_high,
         viscosity, turbine_mask, *tendency_tables, *source_tables),
    )
    own, partner = solve(mine, theirs)
    from_below = lax.ppermute(upward, levels_axis, upward_route)
    from_above = lax.ppermute(downward, levels_axis, downward_route)
    fields = 3 * depth + 5
    extended, bands = call(
        corrected_kernel,
        (shaped(*state_shape), shaped(3, depth + 2, fringe, length_y)),
        [smem()] + [vmem()] * 11 + [smem()],
        [
            pltpu.VMEM((2, 2 * depth + 3, mid, length_y), full_type),
            pltpu.VMEM((fields, 2, mid, length_y), full_type),
        ],
        3 * fields * block * (length_x // 2 + length_y),
        (flags, own, partner, middle, from_below, from_above, tables["slope_x"],
         tables["slope_y"], *pressure_tables, fringe_columns),
    )
    bands = lax.ppermute(bands, "sec", [(0, 1)])
    final, mine, theirs = call(
        second_kernel,
        (own_shape, spectrum, spectrum),
        [smem(), smem(), hbm(), vmem(), hbm()] + [vmem()] * 9,
        [
            pltpu.VMEM(state_shape, full_type), pltpu.VMEM(own_shape.shape, full_type),
            rounded, sources, pltpu.SemaphoreType.DMA((2,)),
        ],
        tendency_flops + source_flops,
        (flags, fringe_columns, extended, bands, current, columns, viscosity, turbine_mask,
         *tendency_tables, *source_tables),
    )
    own, partner = solve(mine, theirs)
    fields = 3 * depth
    (new,) = call(
        last_kernel,
        (own_shape,),
        [smem()] + [vmem()] * 7,
        [
            pltpu.VMEM((2, 2 * depth, mid, length_y), full_type),
            pltpu.VMEM((fields, 2, mid, length_y), full_type),
        ],
        3 * fields * block * (length_x // 2 + length_y),
        (flags, own, partner, final, *pressure_tables),
    )
    return new[None]


def solution(mesh):
    sections, devices = mesh.devices.shape
    fine = Mesh(mesh.devices.reshape(sections, devices // 2, 2), every_axis)
    placed = (
        P("sec", None, levels_axis, None, None),
        P("sec", levels_axis, None, None),
        P(levels_axis, None, None),
        P(),
    )
    return jax.shard_map(
        local,
        mesh=fine,
        in_specs=placed,
        out_specs=P("sec", None, levels_axis, None, None),
        check_vma=False,
    )
```

```python
import functools
import math

import jax
import jax.numpy as jnp
import ml_dtypes
import numpy as np
from jax import lax
from jax.experimental import pallas as pl
from jax.experimental.pallas import tpu as pltpu
from jax.sharding import Mesh
from jax.sharding import PartitionSpec as P

step_size = 0.1
drag_coef = 0.75
cell_width = 4.0
half_type = jnp.bfloat16
full_type = jnp.float32
vmem_bytes = 40 * 1024 * 1024
levels_axis = ("chip", "core")
every_axis = ("sec", "chip", "core")


def derivative_table(length, cutoff):
    offset = np.arange(length)
    wavenumber = np.arange(1, cutoff + 1)
    phases = offset[:, None] * wavenumber[None, :] % length
    waves = np.sin(2.0 * math.pi / length * phases)
    first = -(2.0 / (cell_width * length)) * (waves @ (2.0 * math.pi / length * wavenumber))
    return first[(offset[:, None] - offset[None, :]) % length]


def real_basis(length):
    midpoint = length // 2
    row = np.arange(length)
    wavenumber = np.where(row <= midpoint, row, row - midpoint)
    angles = 2.0 * math.pi / length * (wavenumber[:, None] * row[None, :] % length)
    scales = np.where((row == 0) | (row == midpoint), math.sqrt(1.0 / length), math.sqrt(2.0 / length))
    return scales[:, None] * np.where((row <= midpoint)[:, None], np.cos(angles), np.sin(angles))


def wave_square(length):
    midpoint = length // 2
    row = np.arange(length)
    wavenumber = np.where(row < midpoint, row, np.where(row == midpoint, 0, row - midpoint))
    return (2.0 * math.pi / (length * cell_width) * wavenumber) ** 2


def high_low(table):
    table = np.asarray(table, np.float32)
    high = table.astype(ml_dtypes.bfloat16)
    low = (table - high.astype(np.float32)).astype(ml_dtypes.bfloat16)
    return np.stack([high, low], axis=-3)


def build_tables(length_x, length_y):
    mid = length_x // 2
    full_x = derivative_table(length_x, length_x // 2 - 1)
    full_y = derivative_table(length_y, length_y // 2 - 1)
    basis_x = real_basis(length_x)
    basis_y = real_basis(length_y)
    left_part, right_part = full_x[:mid, :mid], full_x[:mid, mid:]
    derived = full_x @ basis_x.T
    squares = wave_square(length_x)[:, None] + wave_square(length_y)[None, :]
    decay = 2.0 * np.arcsinh(0.5 * np.sqrt(squares))
    return {
        "dealias_x": derivative_table(length_x, (length_x - 1) // 3).astype(ml_dtypes.bfloat16),
        "dealias_y": derivative_table(length_y, (length_y - 1) // 3).T.astype(ml_dtypes.bfloat16),
        "slope_x": high_low(np.stack([left_part + right_part, left_part - right_part])),
        "slope_y": high_low(full_y.T),
        "into_x": high_low(np.stack([basis_x[0::2, :mid], basis_x[1::2, :mid]])),
        "into_y": high_low(basis_y.T),
        "from_x": high_low(np.stack([basis_x[0::2, :mid].T, basis_x[1::2, :mid].T])),
        "from_y": high_low(basis_y),
        "from_slope_x": high_low(np.stack([derived[:mid, 0::2], derived[:mid, 1::2]])),
        "from_slope_y": high_low(basis_y @ full_y.T),
        "decay": np.stack([decay[0::2], decay[1::2]]).astype(np.float32),
    }


def product(one, other):
    return jnp.dot(one, other, preferred_element_type=full_type)


def halves(block):
    high = block.astype(half_type)
    return high, (block - high.astype(full_type)).astype(half_type)


def from_left(table, block):
    high, low = halves(block)
    return product(table[0], high) + product(table[0], low) + product(table[1], high)


def from_right(block, table):
    high, low = halves(block)
    return product(high, table[0]) + product(low, table[0]) + product(high, table[1])


def vmem():
    return pl.BlockSpec(memory_space=pltpu.VMEM)


def smem():
    return pl.BlockSpec(memory_space=pltpu.SMEM)


def hbm():
    return pl.BlockSpec(memory_space=pl.ANY)


def call(kernel, outs, in_specs, scratch, flops, args):
    moved = sum(math.prod(a.shape) * 4 for a in (*outs, *args))
    return pl.pallas_call(
        kernel,
        out_shape=outs,
        in_specs=in_specs,
        out_specs=tuple(vmem() for _ in outs),
        scratch_shapes=scratch,
        compiler_params=pltpu.CompilerParams(vmem_limit_bytes=vmem_bytes),
        cost_estimate=pl.CostEstimate(flops=int(flops), bytes_accessed=moved, transcendentals=0),
    )(*args)


def shaped(*dims, kind=full_type):
    return jax.ShapeDtypeStruct(dims, kind)


def tendency_steps(state, rounded, viscosity, mask, drag, dealias_x, dealias_y, put):
    depth = state.shape[1] - 2
    length_x = state.shape[2]
    rows = length_x // 2
    for z in range(depth):
        for c in range(3):
            rounded[c, z] = state[c, z + 1].astype(half_type)
    for z in range(depth):
        for b in range(length_x // rows):
            part = pl.ds(b * rows, rows)
            u, v, w = (state[c, z + 1, part, :] for c in range(3))
            slow = drag * mask[z, part, :].astype(full_type) * jnp.abs(u)
            nu = viscosity[z, part, :]
            for c in range(3):
                center = state[c, z + 1, part, :]
                upper = state[c, z + 2, part, :]
                lower = state[c, z, part, :]
                grad_x = product(dealias_x[part, :], rounded[c, z])
                grad_y = product(rounded[c, z, part, :], dealias_y[...])
                advected = u * grad_x + v * grad_y + w * (0.5 * (upper - lower))
                change = nu * (upper - 2.0 * center + lower) - advected - slow * center
                put(c, z, part, center, change)


def folded(block, sign):
    mid = block.shape[0] // 2
    return block[:mid] + sign * block[mid:]


def source_spectra(state, parts, core, slope_x, slope_y, into_x, into_y):
    depth = state.shape[1]
    for slot, out in enumerate(parts):
        half = core if slot == 0 else 1 - core
        sign = (1 - 2 * half).astype(full_type)
        slope, into = slope_x[half], into_x[half]
        lifted = [folded(state[2, z], sign) for z in range(depth)]
        sources = []
        for z in range(depth):
            spread = from_left(slope, folded(state[0, z], sign))
            spread += from_right(folded(state[1, z], sign), slope_y)
            sources.append(spread + lifted[z] - (lifted[z - 1] if z else 0.0))
        sources.append(lifted[depth - 1])
        for z, source in enumerate(sources):
            out[z] = from_right(from_left(into, source), into_y)


def prepare_kernel(index, velocity, held, low, high, columns, columns_low, columns_high, sems):
    depth = held.shape[1]
    copies = [
        pltpu.make_async_copy(velocity.at[:, depth - 1], low, sems.at[0]),
        pltpu.make_async_copy(velocity.at[:, 0], high, sems.at[1]),
    ]
    for copy in copies:
        copy.start()

    def one(i, carry):
        row = pl.ds(index[i], 1)
        here = pl.ds(i, 1)
        for c in range(3):
            for z in range(depth):
                taken = held[c, z, row, :]
                columns[c, z, here, :] = taken
                if z == depth - 1:
                    columns_low[c, here, :] = taken
                if z == 0:
                    columns_high[c, here, :] = taken
        return carry

    lax.fori_loop(0, index.shape[0], one, 0)
    for copy in copies:
        copy.wait()


def inner_kernel(
    flags, index, velocity, columns, viscosity, mask, dealias_x, dealias_y,
    partial, weights,
    state, rounded, sems,
):
    depth = partial.shape[1]
    is_farm = flags[0]
    copy = pltpu.make_async_copy(velocity, state.at[:, pl.ds(1, depth)], sems.at[0])
    copy.start()
    state[:, 0] = jnp.zeros_like(state[:, 0])
    state[:, depth + 1] = jnp.zeros_like(state[:, 0])
    copy.wait()

    @pl.when(is_farm == 1)
    def _():
        def one(i, carry):
            row = pl.ds(index[i], 1)
            for c in range(3):
                for z in range(depth):
                    state[c, 1 + z, row, :] = columns[c, z, pl.ds(i, 1), :]
            return carry

        lax.fori_loop(0, index.shape[0], one, 0)

    drag = drag_coef * is_farm.astype(full_type)

    def put(c, z, part, center, change):
        partial[c, z, part, :] = center + step_size * change

    tendency_steps(state, rounded, viscosity, mask, drag, dealias_x, dealias_y, put)
    weights[0] = step_size * (viscosity[0] + 0.5 * state[2, 1])
    weights[1] = step_size * (viscosity[depth - 1] - 0.5 * state[2, depth])


def first_kernel(
    flags, index, partial, weights, low, high, columns_low, columns_high,
    slope_x, slope_y, into_x, into_y,
    middle, upward, downward, mine, theirs,
    ghosts, sems,
):
    depth = middle.shape[1]
    mid = middle.shape[2] // 2
    is_farm, core, is_lid = flags[0], flags[1], flags[3]
    copies = [
        pltpu.make_async_copy(low, ghosts.at[0], sems.at[0]),
        pltpu.make_async_copy(high, ghosts.at[1], sems.at[1]),
    ]
    for copy in copies:
        copy.start()
    for copy in copies:
        copy.wait()

    @pl.when(is_farm == 1)
    def _():
        def one(i, carry):
            row = pl.ds(index[i], 1)
            here = pl.ds(i, 1)
            for c in range(3):
                ghosts[0, c, row, :] = columns_low[c, here, :]
                ghosts[1, c, row, :] = columns_high[c, here, :]
            return carry

        lax.fori_loop(0, index.shape[0], one, 0)

    for c in range(3):
        for z in range(depth):
            moved = partial[c, z]
            if z == 0:
                moved += weights[0] * ghosts[0, c]
            if z == depth - 1:
                moved += weights[1] * ghosts[1, c]
                if c == 2:
                    moved = jnp.where(is_lid == 1, 0.0, moved)
            middle[c, z] = moved
    source_spectra(middle, (mine, theirs), core, slope_x, slope_y, into_x, into_y)
    downward[0] = middle[0, 0]
    downward[1] = middle[1, 0]
    top = depth - 1
    even, odd = (
        0.5 * from_left(slope_x[half], folded(middle[2, top], 1.0 - 2.0 * half))
        for half in range(2)
    )
    upward[0, :mid] = middle[0, top, :mid] + (even + odd)
    upward[0, mid:] = middle[0, top, mid:] + (even - odd)
    upward[1] = middle[1, top] + from_right(middle[2, top], slope_y)


def second_kernel(
    flags, index, extended, columns, velocity, start_columns, viscosity, mask,
    dealias_x, dealias_y, slope_x, slope_y, into_x, into_y,
    final, mine, theirs,
    state, start, rounded, sems,
):
    depth = final.shape[1]
    is_farm, core, is_lid = flags[0], flags[1], flags[3]
    copies = [
        pltpu.make_async_copy(extended, state, sems.at[0]),
        pltpu.make_async_copy(velocity, start, sems.at[1]),
    ]
    for copy in copies:
        copy.start()
    for copy in copies:
        copy.wait()

    @pl.when(is_farm == 1)
    def _():
        def one(i, carry):
            row = pl.ds(index[i], 1)
            here = pl.ds(i, 1)
            for c in range(3):
                for z in range(depth + 2):
                    state[c, z, row, :] = columns[c, z, here, :]
                for z in range(depth):
                    start[c, z, row, :] = start_columns[c, z, here, :]
            return carry

        lax.fori_loop(0, index.shape[0], one, 0)

    drag = drag_coef * is_farm.astype(full_type)

    def put(c, z, part, center, change):
        moved = 0.5 * (start[c, z, part, :] + center + step_size * change)
        if c == 2:
            moved = jnp.where((is_lid == 1) & (z == depth - 1), 0.0, moved)
        final[c, z, part, :] = moved

    tendency_steps(state, rounded, viscosity, mask, drag, dealias_x, dealias_y, put)
    source_spectra(final, (mine, theirs), core, slope_x, slope_y, into_x, into_y)


def chip_levels(core, mine, other, depth):
    is_low = core == 0
    low = [jnp.where(is_low, mine[i], other[i]) for i in range(depth + 1)]
    high = [jnp.where(is_low, other[i], mine[i]) for i in range(depth + 1)]
    levels = low[:depth] + [high[0] - low[depth]] + high[1:depth]
    return levels, low[depth], high[depth]


class Coefficients:
    def __init__(self, stacked, count):
        self.mu = lambda: stacked[0]
        self.phi = lambda i: stacked[1 + i]
        self.psi = lambda i: stacked[2 + count + i]
        self.flux_low = lambda i: stacked[3 + 2 * count + i]
        self.flux_high = lambda i: stacked[3 + 3 * count + i]
        self.entry = lambda: stacked[4 + 4 * count]
        self.scale = lambda: stacked[5 + 4 * count]


def gather_kernel(flags, mine, other, stacked, out, work):
    core = flags[1]
    depth = mine.shape[0] - 1
    count = 2 * depth
    tables = Coefficients(stacked, count)
    levels, _, top = chip_levels(core, mine, other, depth)
    mu = tables.mu()
    forward = tables.phi(0) * levels[0]
    for i in range(1, count):
        forward = mu * forward + tables.phi(i) * levels[i]
    work[0] = mu * forward - tables.phi(count) * top
    backward = -tables.psi(count) * top
    for i in reversed(range(count)):
        backward = tables.psi(i) * levels[i] + mu * backward
    work[1] = backward
    chips = out.shape[0]
    rows = out.shape[1] // 2
    for chip in range(chips):
        out[chip, :rows] = work[0, chip * rows : (chip + 1) * rows]
        out[chip, rows:] = work[1, chip * rows : (chip + 1) * rows]


def scan_kernel(received, ratio, out):
    chips = received.shape[0]
    rows = received.shape[1] // 2
    factor = ratio[...]
    carried = jnp.zeros_like(factor)
    for chip in range(chips):
        out[chip, :rows] = carried
        carried = factor * carried + received[chip, :rows]
    carried = jnp.zeros_like(factor)
    for chip in reversed(range(chips)):
        out[chip, rows:] = carried
        carried = factor * carried + received[chip, rows:]


def solve_kernel(flags, mine, other, stacked, scanned, own, partner, work):
    core = flags[1]
    depth = mine.shape[0] - 1
    count = 2 * depth
    tables = Coefficients(stacked, count)
    chips = scanned.shape[0]
    rows = scanned.shape[1] // 2
    for chip in range(chips):
        work[0, chip * rows : (chip + 1) * rows] = scanned[chip, :rows]
        work[1, chip * rows : (chip + 1) * rows] = scanned[chip, rows:]
    levels, between, top = chip_levels(core, mine, other, depth)
    mu = tables.mu()
    forward = [work[0] + tables.phi(0) * levels[0]]
    for i in range(1, count):
        forward.append(mu * forward[-1] + tables.phi(i) * levels[i])
    backward = [work[1] - tables.psi(count) * top]
    for i in reversed(range(1, count)):
        backward.append(tables.psi(i) * levels[i] + mu * backward[-1])
    backward.reverse()
    flux = [
        tables.flux_low(i) * forward[i] - tables.flux_high(i + 1) * backward[i]
        for i in range(count)
    ]
    under = tables.entry() * work[0] - tables.flux_high(0) * (
        tables.psi(0) * levels[0] + mu * backward[0]
    )
    pressure = [
        -tables.scale() * (tables.psi(i) * forward[i] + mu * tables.phi(i) * backward[i])
        for i in (0, depth)
    ]
    low = [pressure[0], *flux[:depth], under]
    high = [pressure[1], *flux[depth:], flux[depth - 1] - between]
    is_low = core == 0
    for i in range(depth + 2):
        own[i] = jnp.where(is_low, low[i], high[i])
        partner[i] = jnp.where(is_low, high[i], low[i])


def physical_fields(core, mine, other, from_x, from_y, from_slope_x, from_slope_y, spectra, slots, ghosts):
    depth = mine.shape[0] - 2
    pressures = depth + 2 if ghosts else depth
    first = 1 if ghosts else 0
    lifts = depth + 1 if ghosts else depth
    for half in range(2):
        chosen = [jnp.where(core == half, mine[i], other[i]) for i in range(depth + 2)]
        level = chosen[0]
        if ghosts:
            spectra[half, 0] = level - chosen[depth + 1]
        for z in range(depth):
            spectra[half, first + z] = level
            level = level + chosen[1 + z]
        if ghosts:
            spectra[half, first + depth] = level
        for z in range(lifts):
            spectra[half, pressures + z] = chosen[1 + z]

    for half in range(2):
        for i in range(pressures):
            block = spectra[half, i]
            slots[2 * i, half] = from_left(from_slope_x[half], from_right(block, from_y))
            slots[2 * i + 1, half] = from_left(from_x[half], from_right(block, from_slope_y))
        for i in range(lifts):
            block = spectra[half, pressures + i]
            slots[2 * pressures + i, half] = from_left(from_x[half], from_right(block, from_y))


def unfolded(slots, i):
    return slots[i, 0] + slots[i, 1], slots[i, 0] - slots[i, 1]


def corrected_kernel(
    flags, mine, other, middle, from_below, from_above, slope_x, slope_y,
    from_x, from_y, from_slope_x, from_slope_y, index,
    out, columns,
    spectra, slots,
):
    core, is_floor, is_lid = flags[1], flags[2], flags[3]
    depth = middle.shape[1]
    mid = middle.shape[2] // 2
    physical_fields(
        core, mine, other, from_x, from_y, from_slope_x, from_slope_y, spectra, slots, True
    )
    pressures = depth + 2
    open_low = (1 - is_floor).astype(full_type)
    open_high = (1 - is_lid).astype(full_type)
    sides = (slice(0, mid), slice(mid, 2 * mid))
    for z in range(depth):
        for c in range(3):
            slot = 2 * (1 + z) + c if c < 2 else 2 * pressures + z
            for side, change in zip(sides, unfolded(slots, slot)):
                out[c, 1 + z, side] = middle[c, z, side] - change
    for c in range(2):
        for side, change in zip(sides, unfolded(slots, c)):
            out[c, 0, side] = open_low * (from_below[c, side] - change)
        for side, change in zip(sides, unfolded(slots, 2 * (depth + 1) + c)):
            out[c, depth + 1, side] = open_high * (from_above[c, side] - change)
    for side, change in zip(sides, unfolded(slots, 2 * pressures + depth)):
        out[2, 0, side] = -open_low * change
    for half in range(2):
        slots[0, half] = 0.5 * from_left(
            slope_x[half], folded(out[0, depth + 1], 1.0 - 2.0 * half)
        )
    for side, change in zip(sides, unfolded(slots, 0)):
        spread = change + from_right(out[1, depth + 1, side], slope_y)
        out[2, depth + 1, side] = open_high * (out[2, depth, side] - spread)

    def one(i, carry):
        row = pl.ds(index[i], 1)
        for c in range(3):
            for z in range(depth + 2):
                columns[c, z, pl.ds(i, 1), :] = out[c, z, row, :]
        return carry

    lax.fori_loop(0, index.shape[0], one, 0)


def last_kernel(
    flags, mine, other, final, from_x, from_y, from_slope_x, from_slope_y,
    out,
    spectra, slots,
):
    core = flags[1]
    depth = final.shape[1]
    mid = final.shape[2] // 2
    physical_fields(
        core, mine, other, from_x, from_y, from_slope_x, from_slope_y, spectra, slots, False
    )
    sides = (slice(0, mid), slice(mid, 2 * mid))
    for z in range(depth):
        for c in range(3):
            slot = 2 * z + c if c < 2 else 2 * depth + z
            for side, change in zip(sides, unfolded(slots, slot)):
                out[c, z, side] = final[c, z, side] - change


def coefficients(decay, first_level, count, height):
    def gap(steps):
        return -jnp.expm1(-steps * decay)

    still = decay == 0.0
    below = jnp.arange(count + 1, dtype=full_type)[:, None, None] + first_level
    mu = jnp.exp(-decay)
    safe = jnp.where(still, 1.0, gap(2.0 * height))

    def ratio(steps):
        return jnp.where(still, steps / height, gap(2.0 * steps) / safe)

    share = 1.0 / (1.0 + mu)
    phi = 1.0 + jnp.exp(-(2.0 * below + 1.0) * decay)
    psi = 1.0 + jnp.exp(-(2.0 * (height - below) - 1.0) * decay)
    flux_low = mu * share * ratio(height - 1.0 - below[:count])
    flux_high = mu * share * ratio(below)
    entry = share * ratio(height - below[:1])
    scale = jnp.where(still, 0.0, mu / (jnp.where(still, 1.0, gap(2.0)) * safe))
    return jnp.concatenate([mu[None], phi, psi, flux_low, flux_high, entry, scale[None]])


def local(velocity, eddy_viscosity, turbine_mask, fringe_columns):
    current = velocity[0]
    viscosity = eddy_viscosity[0]
    _, depth, length_x, length_y = current.shape
    mid = length_x // 2
    fringe = fringe_columns.shape[0]
    chips = lax.axis_size("chip")
    devices = 2 * chips
    height = devices * depth
    count = 2 * depth
    rows = mid // chips
    section = lax.axis_index("sec")
    chip = lax.axis_index("chip")
    core = lax.axis_index("core")
    place = 2 * chip + core
    is_farm = section == 1
    flags = jnp.stack([is_farm, core, place == 0, place == devices - 1]).astype(jnp.int32)
    tables = {name: jnp.asarray(table) for name, table in build_tables(length_x, length_y).items()}

    upward_route = [(i, i + 1) for i in range(devices - 1)]
    downward_route = [(i + 1, i) for i in range(devices - 1)]
    swap = [(0, 1), (1, 0)]

    def across(shift):
        return [
            (i, devices + i + shift) for i in range(devices) if 0 <= i + shift < devices
        ]

    edge_shape = shaped(3, length_x, length_y)
    band = shaped(3, fringe, length_y)
    low, high, columns, columns_low, columns_high = pl.pallas_call(
        prepare_kernel,
        out_shape=(edge_shape, edge_shape, shaped(3, depth, fringe, length_y), band, band),
        in_specs=[smem(), hbm(), vmem()],
        out_specs=(hbm(), hbm(), vmem(), vmem(), vmem()),
        scratch_shapes=[pltpu.SemaphoreType.DMA((2,))],
        compiler_params=pltpu.CompilerParams(vmem_limit_bytes=vmem_bytes),
    )(fringe_columns, current, current)
    low = lax.ppermute(low, levels_axis, upward_route)
    high = lax.ppermute(high, levels_axis, downward_route)
    columns = lax.ppermute(columns, every_axis, across(0))
    columns_low = lax.ppermute(columns_low, every_axis, across(1))
    columns_high = lax.ppermute(columns_high, every_axis, across(-1))

    decay = lax.dynamic_index_in_dim(tables["decay"], core, 0, keepdims=False)
    stacked = coefficients(decay, (chip * count).astype(full_type), count, float(height))
    ratio = jnp.exp(-float(count) * lax.dynamic_slice_in_dim(decay, chip * rows, rows, 0))

    block = length_x * length_y * 2
    spectrum = shaped(depth + 1, mid, length_y)
    solved = shaped(depth + 2, mid, length_y)
    message = shaped(chips, 2 * rows, length_y)
    tendency_tables = [tables["dealias_x"], tables["dealias_y"]]
    source_tables = [tables[n] for n in ("slope_x", "slope_y", "into_x", "into_y")]
    pressure_tables = [tables[n] for n in ("from_x", "from_y", "from_slope_x", "from_slope_y")]

    def solve(mine, theirs):
        other = lax.ppermute(theirs, "core", swap)
        (sums,) = call(
            gather_kernel, (message,), [smem(), vmem(), vmem(), vmem()],
            [pltpu.VMEM((2, mid, length_y), full_type)], 8 * count * block,
            (flags, mine, other, stacked),
        )
        sums = lax.all_to_all(sums, "chip", split_axis=0, concat_axis=0, tiled=True)
        (sums,) = call(scan_kernel, (message,), [vmem(), vmem()], [], 4 * block, (sums, ratio))
        sums = lax.all_to_all(sums, "chip", split_axis=0, concat_axis=0, tiled=True)
        own, partner = call(
            solve_kernel, (solved, solved), [smem()] + [vmem()] * 4,
            [pltpu.VMEM((2, mid, length_y), full_type)], 16 * count * block,
            (flags, mine, other, stacked, sums),
        )
        return own, lax.ppermute(partner, "core", swap)

    state_shape = (3, depth + 2, length_x, length_y)
    rounded = pltpu.VMEM((3, depth, length_x, length_y), half_type)
    own_shape = shaped(3, depth, length_x, length_y)
    edge = shaped(2, length_x, length_y)
    tendency_flops = 3 * depth * block * (length_x + length_y)
    source_flops = 3 * depth * block * (length_x + 2 * length_y)

    partial, weights = call(
        inner_kernel,
        (own_shape, edge),
        [smem(), smem(), hbm()] + [vmem()] * 5,
        [pltpu.VMEM(state_shape, full_type), rounded, pltpu.SemaphoreType.DMA((1,))],
        tendency_flops,
        (flags, fringe_columns, current, columns, viscosity, turbine_mask, *tendency_tables),
    )
    middle, upward, downward, mine, theirs = call(
        first_kernel,
        (own_shape, edge, edge, spectrum, spectrum),
        [smem(), smem()] + [vmem()] * 2 + [hbm()] * 2 + [vmem()] * 6,
        [pltpu.VMEM((2, 3, length_x, length_y), full_type), pltpu.SemaphoreType.DMA((2,))],
        source_flops,
        (flags, fringe_columns, partial, weights, low, high, columns_low, columns_high,
         *source_tables),
    )
    own, partner = solve(mine, theirs)
    from_below = lax.ppermute(upward, levels_axis, upward_route)
    from_above = lax.ppermute(downward, levels_axis, downward_route)
    fields = 3 * depth + 5
    extended, bands = call(
        corrected_kernel,
        (shaped(*state_shape), shaped(3, depth + 2, fringe, length_y)),
        [smem()] + [vmem()] * 11 + [smem()],
        [
            pltpu.VMEM((2, 2 * depth + 3, mid, length_y), full_type),
            pltpu.VMEM((fields, 2, mid, length_y), full_type),
        ],
        3 * fields * block * (length_x // 2 + length_y),
        (flags, own, partner, middle, from_below, from_above, tables["slope_x"],
         tables["slope_y"], *pressure_tables, fringe_columns),
    )
    bands = lax.ppermute(bands, "sec", [(0, 1)])
    final, mine, theirs = call(
        second_kernel,
        (own_shape, spectrum, spectrum),
        [smem(), smem(), hbm(), vmem(), hbm()] + [vmem()] * 9,
        [
            pltpu.VMEM(state_shape, full_type), pltpu.VMEM(own_shape.shape, full_type),
            rounded, pltpu.SemaphoreType.DMA((2,)),
        ],
        tendency_flops + source_flops,
        (flags, fringe_columns, extended, bands, current, columns, viscosity, turbine_mask,
         *tendency_tables, *source_tables),
    )
    own, partner = solve(mine, theirs)
    fields = 3 * depth
    (new,) = call(
        last_kernel,
        (own_shape,),
        [smem()] + [vmem()] * 7,
        [
            pltpu.VMEM((2, 2 * depth, mid, length_y), full_type),
            pltpu.VMEM((fields, 2, mid, length_y), full_type),
        ],
        3 * fields * block * (length_x // 2 + length_y),
        (flags, own, partner, final, *pressure_tables),
    )
    return new[None]


def solution(mesh):
    sections, devices = mesh.devices.shape
    fine = Mesh(mesh.devices.reshape(sections, devices // 2, 2), every_axis)
    placed = (
        P("sec", None, levels_axis, None, None),
        P("sec", levels_axis, None, None),
        P(levels_axis, None, None),
        P(),
    )
    return jax.shard_map(
        local,
        mesh=fine,
        in_specs=placed,
        out_specs=P("sec", None, levels_axis, None, None),
        check_vma=False,
    )
```

```python
import functools
import math

import jax
import jax.numpy as jnp
import ml_dtypes
import numpy as np
from jax import lax
from jax.experimental import pallas as pl
from jax.experimental.pallas import tpu as pltpu
from jax.sharding import Mesh
from jax.sharding import PartitionSpec as P

step_size = 0.1
drag_coef = 0.75
cell_width = 4.0
half_type = jnp.bfloat16
full_type = jnp.float32
vmem_bytes = 26 * 1024 * 1024
levels_axis = ("chip", "core")
every_axis = ("sec", "chip", "core")


def derivative_table(length, cutoff):
    offset = np.arange(length)
    wavenumber = np.arange(1, cutoff + 1)
    phases = offset[:, None] * wavenumber[None, :] % length
    waves = np.sin(2.0 * math.pi / length * phases)
    first = -(2.0 / (cell_width * length)) * (waves @ (2.0 * math.pi / length * wavenumber))
    return first[(offset[:, None] - offset[None, :]) % length]


def real_basis(length):
    midpoint = length // 2
    row = np.arange(length)
    wavenumber = np.where(row <= midpoint, row, row - midpoint)
    angles = 2.0 * math.pi / length * (wavenumber[:, None] * row[None, :] % length)
    scales = np.where((row == 0) | (row == midpoint), math.sqrt(1.0 / length), math.sqrt(2.0 / length))
    return scales[:, None] * np.where((row <= midpoint)[:, None], np.cos(angles), np.sin(angles))


def wave_square(length):
    midpoint = length // 2
    row = np.arange(length)
    wavenumber = np.where(row < midpoint, row, np.where(row == midpoint, 0, row - midpoint))
    return (2.0 * math.pi / (length * cell_width) * wavenumber) ** 2


def high_low(table):
    table = np.asarray(table, np.float32)
    high = table.astype(ml_dtypes.bfloat16)
    low = (table - high.astype(np.float32)).astype(ml_dtypes.bfloat16)
    return np.stack([high, low], axis=-3)


def build_tables(length_x, length_y):
    mid = length_x // 2
    full_x = derivative_table(length_x, length_x // 2 - 1)
    full_y = derivative_table(length_y, length_y // 2 - 1)
    basis_x = real_basis(length_x)
    basis_y = real_basis(length_y)
    left_part, right_part = full_x[:mid, :mid], full_x[:mid, mid:]
    derived = full_x @ basis_x.T
    squares = wave_square(length_x)[:, None] + wave_square(length_y)[None, :]
    decay = 2.0 * np.arcsinh(0.5 * np.sqrt(squares))
    return {
        "dealias_x": derivative_table(length_x, (length_x - 1) // 3).astype(ml_dtypes.bfloat16),
        "dealias_y": derivative_table(length_y, (length_y - 1) // 3).T.astype(ml_dtypes.bfloat16),
        "slope_x": high_low(np.stack([left_part + right_part, left_part - right_part])),
        "slope_y": high_low(full_y.T),
        "into_x": high_low(np.stack([basis_x[0::2, :mid], basis_x[1::2, :mid]])),
        "into_y": high_low(basis_y.T),
        "from_x": high_low(np.stack([basis_x[0::2, :mid].T, basis_x[1::2, :mid].T])),
        "from_y": high_low(basis_y),
        "from_slope_x": high_low(np.stack([derived[:mid, 0::2], derived[:mid, 1::2]])),
        "from_slope_y": high_low(basis_y @ full_y.T),
        "decay": np.stack([decay[0::2], decay[1::2]]).astype(np.float32),
    }


def product(one, other):
    return jnp.dot(one, other, preferred_element_type=full_type)


def halves(block):
    high = block.astype(half_type)
    return high, (block - high.astype(full_type)).astype(half_type)


def from_left(table, block):
    high, low = halves(block)
    return product(table[0], high) + product(table[0], low) + product(table[1], high)


def from_right(block, table):
    high, low = halves(block)
    return product(high, table[0]) + product(low, table[0]) + product(high, table[1])


def vmem():
    return pl.BlockSpec(memory_space=pltpu.VMEM)


def smem():
    return pl.BlockSpec(memory_space=pltpu.SMEM)


def hbm():
    return pl.BlockSpec(memory_space=pltpu.HBM)


def call(kernel, outs, in_specs, scratch, flops, args, out_specs=None):
    moved = sum(math.prod(a.shape) * 4 for a in (*outs, *args))
    return pl.pallas_call(
        kernel,
        out_shape=outs,
        in_specs=in_specs,
        out_specs=out_specs or tuple(vmem() for _ in outs),
        scratch_shapes=scratch,
        compiler_params=pltpu.CompilerParams(vmem_limit_bytes=vmem_bytes),
        cost_estimate=pl.CostEstimate(flops=int(flops), bytes_accessed=moved, transcendentals=0),
    )(*args)


def shaped(*dims, kind=full_type):
    return jax.ShapeDtypeStruct(dims, kind)


def tendency_steps(state, rounded, viscosity, mask, drag, dealias_x, dealias_y, put):
    depth = state.shape[1] - 2
    length_x = state.shape[2]
    rows = length_x // 2
    for z in range(depth):
        for c in range(3):
            rounded[c, z] = state[c, z + 1].astype(half_type)
    for z in range(depth):
        for b in range(length_x // rows):
            part = pl.ds(b * rows, rows)
            u, v, w = (state[c, z + 1, part, :] for c in range(3))
            slow = drag * mask[z, part, :].astype(full_type) * jnp.abs(u)
            nu = viscosity[z, part, :]
            for c in range(3):
                center = state[c, z + 1, part, :]
                upper = state[c, z + 2, part, :]
                lower = state[c, z, part, :]
                grad_x = product(dealias_x[part, :], rounded[c, z])
                grad_y = product(rounded[c, z, part, :], dealias_y[...])
                advected = u * grad_x + v * grad_y + w * (0.5 * (upper - lower))
                change = nu * (upper - 2.0 * center + lower) - advected - slow * center
                put(c, z, part, center, change)


def folded(block, sign):
    mid = block.shape[0] // 2
    return block[:mid] + sign * block[mid:]


def source_spectra(state, out, half, slope_x, slope_y, into_x, into_y):
    depth = state.shape[1]
    sign = (1 - 2 * half).astype(full_type)
    slope, into = slope_x[half], into_x[half]
    lifted = [folded(state[2, z], sign) for z in range(depth)]
    sources = []
    for z in range(depth):
        spread = from_left(slope, folded(state[0, z], sign))
        spread += from_right(folded(state[1, z], sign), slope_y)
        sources.append(spread + lifted[z] - (lifted[z - 1] if z else 0.0))
    sources.append(lifted[depth - 1])
    for z, source in enumerate(sources):
        out[z] = from_right(from_left(into, source), into_y)


def edges_kernel(velocity, low, high):
    depth = velocity.shape[1]
    low[...] = velocity[:, depth - 1]
    high[...] = velocity[:, 0]


def columns_kernel(index, velocity, columns, columns_low, columns_high):
    depth = velocity.shape[1]

    def one(i, carry):
        row = pl.ds(index[i], 1)
        here = pl.ds(i, 1)
        for c in range(3):
            for z in range(depth):
                taken = velocity[c, z, row, :]
                columns[c, z, here, :] = taken
                if z == depth - 1:
                    columns_low[c, here, :] = taken
                if z == 0:
                    columns_high[c, here, :] = taken
        return carry

    lax.fori_loop(0, index.shape[0], one, 0)


def insert_rows(index, pairs):
    def one(i, carry):
        row = pl.ds(index[i], 1)
        for target, rows in pairs:
            for c in range(3):
                target[c, row, :] = rows[c, pl.ds(i, 1), :]
        return carry

    lax.fori_loop(0, index.shape[0], one, 0)


def inner_kernel(
    flags, index, velocity, columns, *refs,
):
    depth = velocity.shape[1]
    is_second = len(refs) == 12
    if is_second:
        earlier, earlier_columns, *refs, start = refs
    viscosity, mask, dealias_x, dealias_y, partial, weights, state, rounded, sems, *_ = refs
    is_farm = flags[0]
    copies = [pltpu.make_async_copy(velocity, state.at[:, pl.ds(1, depth)], sems.at[0])]
    if is_second:
        copies.append(pltpu.make_async_copy(earlier, start, sems.at[1]))
    for copy in copies:
        copy.start()
    state[:, 0] = jnp.zeros_like(state[:, 0])
    state[:, depth + 1] = jnp.zeros_like(state[:, 0])
    for copy in copies:
        copy.wait()

    @pl.when(is_farm == 1)
    def _():
        pairs = [(state.at[:, 1 + z], columns.at[:, z]) for z in range(depth)]
        if is_second:
            pairs += [(start.at[:, z], earlier_columns.at[:, z]) for z in range(depth)]
        insert_rows(index, pairs)

    drag = drag_coef * is_farm.astype(full_type)
    share = 0.5 if is_second else 1.0

    def put(c, z, part, center, change):
        moved = center + step_size * change
        if is_second:
            moved = 0.5 * (start[c, z, part, :] + moved)
        partial[c, z, part, :] = moved

    tendency_steps(state, rounded, viscosity, mask, drag, dealias_x, dealias_y, put)
    weights[0] = share * step_size * (viscosity[0] + 0.5 * state[2, 1])
    weights[1] = share * step_size * (viscosity[depth - 1] - 0.5 * state[2, depth])


def outer_kernel(
    flags, index, partial, weights, low, high, columns_low, columns_high,
    slope_x, slope_y, into_x, into_y,
    middle, theirs,
    ghosts, sems,
):
    depth = middle.shape[1]
    is_farm, core, is_lid = flags[0], flags[1], flags[3]
    copies = [
        pltpu.make_async_copy(low, ghosts.at[0], sems.at[0]),
        pltpu.make_async_copy(high, ghosts.at[1], sems.at[1]),
    ]
    for copy in copies:
        copy.start()
    for copy in copies:
        copy.wait()

    @pl.when(is_farm == 1)
    def _():
        insert_rows(index, [(ghosts.at[0], columns_low), (ghosts.at[1], columns_high)])

    for c in range(3):
        for z in range(depth):
            moved = partial[c, z]
            if z == 0:
                moved += weights[0] * ghosts[0, c]
            if z == depth - 1:
                moved += weights[1] * ghosts[1, c]
                if c == 2:
                    moved = jnp.where(is_lid == 1, 0.0, moved)
            middle[c, z] = moved
    source_spectra(middle, theirs, 1 - core, slope_x, slope_y, into_x, into_y)


def own_spectra_kernel(flags, middle, slope_x, slope_y, into_x, into_y, mine, *edges):
    depth = middle.shape[1]
    mid = middle.shape[2] // 2
    source_spectra(middle, mine, flags[1], slope_x, slope_y, into_x, into_y)
    if not edges:
        return
    upward, downward = edges
    downward[0] = middle[0, 0]
    downward[1] = middle[1, 0]
    top = depth - 1
    even, odd = (
        0.5 * from_left(slope_x[half], folded(middle[2, top], 1.0 - 2.0 * half))
        for half in range(2)
    )
    upward[0, :mid] = middle[0, top, :mid] + (even + odd)
    upward[0, mid:] = middle[0, top, mid:] + (even - odd)
    upward[1] = middle[1, top] + from_right(middle[2, top], slope_y)


def chip_levels(core, mine, other, depth):
    is_low = core == 0
    low = [jnp.where(is_low, mine[i], other[i]) for i in range(depth + 1)]
    high = [jnp.where(is_low, other[i], mine[i]) for i in range(depth + 1)]
    levels = low[:depth] + [high[0] - low[depth]] + high[1:depth]
    return levels, low[depth], high[depth]


class Coefficients:
    def __init__(self, stacked, count):
        self.mu = lambda: stacked[0]
        self.phi = lambda i: stacked[1 + i]
        self.psi = lambda i: stacked[2 + count + i]
        self.flux_low = lambda i: stacked[3 + 2 * count + i]
        self.flux_high = lambda i: stacked[3 + 3 * count + i]
        self.entry = lambda: stacked[4 + 4 * count]
        self.scale = lambda: stacked[5 + 4 * count]


def gather_kernel(flags, mine, other, stacked, out, work, packed, sems):
    core = flags[1]
    depth = mine.shape[0] - 1
    count = 2 * depth
    tables = Coefficients(stacked, count)
    levels, _, top = chip_levels(core, mine, other, depth)
    mu = tables.mu()
    forward = tables.phi(0) * levels[0]
    for i in range(1, count):
        forward = mu * forward + tables.phi(i) * levels[i]
    work[0] = mu * forward - tables.phi(count) * top
    backward = -tables.psi(count) * top
    for i in reversed(range(count)):
        backward = tables.psi(i) * levels[i] + mu * backward
    work[1] = backward
    chips = out.shape[0]
    rows = out.shape[1] // 2
    for chip in range(chips):
        packed[chip, :rows] = work[0, chip * rows : (chip + 1) * rows]
        packed[chip, rows:] = work[1, chip * rows : (chip + 1) * rows]
    copy = pltpu.make_async_copy(packed, out, sems.at[0])
    copy.start()
    copy.wait()


def scan_kernel(received, ratio, out, taken, packed, sems):
    chips = received.shape[0]
    rows = received.shape[1] // 2
    copy = pltpu.make_async_copy(received, taken, sems.at[0])
    copy.start()
    factor = ratio[...]
    copy.wait()
    carried = jnp.zeros_like(factor)
    for chip in range(chips):
        packed[chip, :rows] = carried
        carried = factor * carried + taken[chip, :rows]
    carried = jnp.zeros_like(factor)
    for chip in reversed(range(chips)):
        packed[chip, rows:] = carried
        carried = factor * carried + taken[chip, rows:]
    copy = pltpu.make_async_copy(packed, out, sems.at[1])
    copy.start()
    copy.wait()


def solve_kernel(flags, mine, other, stacked, received, own, partner, work, scanned, sems):
    core = flags[1]
    depth = mine.shape[0] - 1
    count = 2 * depth
    tables = Coefficients(stacked, count)
    chips = scanned.shape[0]
    rows = scanned.shape[1] // 2
    copy = pltpu.make_async_copy(received, scanned, sems.at[0])
    copy.start()
    copy.wait()
    for chip in range(chips):
        work[0, chip * rows : (chip + 1) * rows] = scanned[chip, :rows]
        work[1, chip * rows : (chip + 1) * rows] = scanned[chip, rows:]
    levels, between, top = chip_levels(core, mine, other, depth)
    mu = tables.mu()
    forward = [work[0] + tables.phi(0) * levels[0]]
    for i in range(1, count):
        forward.append(mu * forward[-1] + tables.phi(i) * levels[i])
    backward = [work[1] - tables.psi(count) * top]
    for i in reversed(range(1, count)):
        backward.append(tables.psi(i) * levels[i] + mu * backward[-1])
    backward.reverse()
    flux = [
        tables.flux_low(i) * forward[i] - tables.flux_high(i + 1) * backward[i]
        for i in range(count)
    ]
    under = tables.entry() * work[0] - tables.flux_high(0) * (
        tables.psi(0) * levels[0] + mu * backward[0]
    )
    pressure = [
        -tables.scale() * (tables.psi(i) * forward[i] + mu * tables.phi(i) * backward[i])
        for i in (0, depth)
    ]
    low = [pressure[0], *flux[:depth], under]
    high = [pressure[1], *flux[depth:], flux[depth - 1] - between]
    is_low = core == 0
    for i in range(own.shape[0]):
        own[i] = jnp.where(is_low, low[i], high[i])
        partner[i] = jnp.where(is_low, high[i], low[i])


def physical_half(fields, half, ghosts, from_x, from_y, from_slope_x, from_slope_y, slots):
    depth = fields.shape[0] - (2 if ghosts else 1)
    level = fields[0]
    pressures = [level - fields[depth + 1]] if ghosts else []
    for z in range(depth):
        pressures.append(level)
        level = level + fields[1 + z]
    if ghosts:
        pressures.append(level)
    for i, block in enumerate(pressures):
        slots[2 * i] = from_left(from_slope_x[half], from_right(block, from_y))
        slots[2 * i + 1] = from_left(from_x[half], from_right(block, from_slope_y))
    for i in range(fields.shape[0] - 1):
        block = from_right(fields[1 + i], from_y)
        slots[2 * len(pressures) + i] = from_left(from_x[half], block)


def own_half_kernel(flags, mine, from_x, from_y, from_slope_x, from_slope_y, slots, *, ghosts):
    physical_half(mine, flags[1], ghosts, from_x, from_y, from_slope_x, from_slope_y, slots)


def unfolded(core, mine, other, i):
    sign = (1 - 2 * core).astype(full_type)
    return mine[i] + other[i], sign * (mine[i] - other[i])


def fringe_kernel(
    flags, index, mine, other, middle, rows_x, rows_slope_x, from_y, from_slope_y,
    columns, columns_low, columns_high,
):
    core = flags[1]
    depth = middle.shape[1]
    fields = [
        [jnp.where(core == half, mine[i], other[i]) for i in range(mine.shape[0])]
        for half in range(2)
    ]
    pressure = [fields[half][0] for half in range(2)]
    for z in range(depth):
        slope = sum(from_left(rows_slope_x[half], pressure[half]) for half in range(2))
        plain = sum(from_left(rows_x[half], pressure[half]) for half in range(2))
        lift = sum(from_left(rows_x[half], fields[half][1 + z]) for half in range(2))
        columns[0, z] = from_right(slope, from_y)
        columns[1, z] = from_right(plain, from_slope_y)
        columns[2, z] = from_right(lift, from_y)
        pressure = [pressure[half] + fields[half][1 + z] for half in range(2)]

    def one(i, carry):
        row = pl.ds(index[i], 1)
        here = pl.ds(i, 1)
        for c in range(3):
            for z in range(depth):
                value = middle[c, z, row, :] - columns[c, z, here, :]
                columns[c, z, here, :] = value
                if z == depth - 1:
                    columns_low[c, here, :] = value
                if z == 0:
                    columns_high[c, here, :] = value
        return carry

    lax.fori_loop(0, index.shape[0], one, 0)


def corrected_kernel(
    flags, slots, fields, middle, from_below, from_above, slope_x, slope_y,
    from_x, from_y, from_slope_x, from_slope_y,
    out, low, high,
    others,
):
    core, is_floor, is_lid = flags[1], flags[2], flags[3]
    depth = middle.shape[1]
    mid = middle.shape[2] // 2
    physical_half(
        fields, 1 - core, True, from_x, from_y, from_slope_x, from_slope_y, others
    )
    pressures = depth + 2
    open_low = (1 - is_floor).astype(full_type)
    open_high = (1 - is_lid).astype(full_type)
    sides = (slice(0, mid), slice(mid, 2 * mid))
    for z in range(depth):
        for c in range(3):
            slot = 2 * (1 + z) + c if c < 2 else 2 * pressures + z
            for side, change in zip(sides, unfolded(core, slots, others, slot)):
                out[c, z, side] = middle[c, z, side] - change
    for c in range(2):
        for side, change in zip(sides, unfolded(core, slots, others, c)):
            low[c, side] = open_low * (from_below[c, side] - change)
        slot = 2 * (depth + 1) + c
        for side, change in zip(sides, unfolded(core, slots, others, slot)):
            high[c, side] = open_high * (from_above[c, side] - change)
    slot = 2 * pressures + depth
    for side, change in zip(sides, unfolded(core, slots, others, slot)):
        low[2, side] = -open_low * change
    even, odd = (
        0.5 * from_left(slope_x[half], folded(high[0], 1.0 - 2.0 * half)) for half in range(2)
    )
    for side, change in zip(sides, (even + odd, even - odd)):
        spread = change + from_right(high[1, side], slope_y)
        high[2, side] = open_high * (out[2, depth - 1, side] - spread)


def last_kernel(
    flags, slots, fields, final, from_x, from_y, from_slope_x, from_slope_y,
    out,
    others,
):
    core = flags[1]
    depth = final.shape[1]
    mid = final.shape[2] // 2
    physical_half(
        fields, 1 - core, False, from_x, from_y, from_slope_x, from_slope_y, others
    )
    sides = (slice(0, mid), slice(mid, 2 * mid))
    for z in range(depth):
        for c in range(3):
            slot = 2 * z + c if c < 2 else 2 * depth + z
            for side, change in zip(sides, unfolded(core, slots, others, slot)):
                out[c, z, side] = final[c, z, side] - change


def coefficients(decay, first_level, count, height):
    def gap(steps):
        return -jnp.expm1(-steps * decay)

    still = decay == 0.0
    below = jnp.arange(count + 1, dtype=full_type)[:, None, None] + first_level
    mu = jnp.exp(-decay)
    safe = jnp.where(still, 1.0, gap(2.0 * height))

    def ratio(steps):
        return jnp.where(still, steps / height, gap(2.0 * steps) / safe)

    share = 1.0 / (1.0 + mu)
    phi = 1.0 + jnp.exp(-(2.0 * below + 1.0) * decay)
    psi = 1.0 + jnp.exp(-(2.0 * (height - below) - 1.0) * decay)
    flux_low = mu * share * ratio(height - 1.0 - below[:count])
    flux_high = mu * share * ratio(below)
    entry = share * ratio(height - below[:1])
    scale = jnp.where(still, 0.0, mu / (jnp.where(still, 1.0, gap(2.0)) * safe))
    return jnp.concatenate([mu[None], phi, psi, flux_low, flux_high, entry, scale[None]])


def local(velocity, eddy_viscosity, turbine_mask, fringe_columns):
    current = velocity[0]
    viscosity = eddy_viscosity[0]
    _, depth, length_x, length_y = current.shape
    mid = length_x // 2
    fringe = fringe_columns.shape[0]
    chips = lax.axis_size("chip")
    devices = 2 * chips
    height = devices * depth
    count = 2 * depth
    rows = mid // chips
    section = lax.axis_index("sec")
    chip = lax.axis_index("chip")
    core = lax.axis_index("core")
    place = 2 * chip + core
    is_farm = section == 1
    flags = jnp.stack([is_farm, core, place == 0, place == devices - 1]).astype(jnp.int32)
    tables = {name: jnp.asarray(table) for name, table in build_tables(length_x, length_y).items()}

    upward_route = [(i, i + 1) for i in range(devices - 1)]
    downward_route = [(i + 1, i) for i in range(devices - 1)]
    swap = [(0, 1), (1, 0)]

    def across(shift):
        return [
            (i, devices + i + shift) for i in range(devices) if 0 <= i + shift < devices
        ]

    state_shape = (3, depth + 2, length_x, length_y)
    own_shape = shaped(3, depth, length_x, length_y)
    edge = shaped(2, length_x, length_y)
    whole_edge = shaped(3, length_x, length_y)
    band = shaped(3, fringe, length_y)
    bands = (shaped(3, depth, fringe, length_y), band, band)
    decay = lax.dynamic_index_in_dim(tables["decay"], core, 0, keepdims=False)
    stacked = coefficients(decay, (chip * count).astype(full_type), count, float(height))
    ratio = jnp.exp(-float(count) * lax.dynamic_slice_in_dim(decay, chip * rows, rows, 0))

    low, high = call(edges_kernel, (whole_edge, whole_edge), [vmem()], [], 0, (current,))
    low, high, held = lax.optimization_barrier((low, high, current))
    low = lax.ppermute(low, levels_axis, upward_route)
    high = lax.ppermute(high, levels_axis, downward_route)
    farm_downward = [(devices + i + 1, devices + i) for i in range(devices - 1)]

    held, stacked = lax.optimization_barrier((held, stacked))
    taken = call(columns_kernel, bands, [smem(), vmem()], [], 0, (fringe_columns, held))
    columns = lax.ppermute(taken[0], every_axis, across(0))
    columns_low = lax.ppermute(taken[1], every_axis, across(1))
    columns_high = lax.ppermute(columns[:, 0], every_axis, farm_downward)
    away = jnp.where(fringe_columns < mid, 1.0, -1.0)[:, None]
    signs = jnp.stack([jnp.ones_like(away), away])[:, None].astype(half_type)
    rows_x, rows_slope_x = (
        jnp.take(tables[name], fringe_columns % mid, axis=2) * signs
        for name in ("from_x", "from_slope_x")
    )

    block = length_x * length_y * 2
    spectrum = shaped(depth + 1, mid, length_y)
    message = shaped(chips, 2 * rows, length_y)
    tendency_tables = [tables["dealias_x"], tables["dealias_y"]]
    source_tables = [tables[n] for n in ("slope_x", "slope_y", "into_x", "into_y")]
    pressure_tables = [tables[n] for n in ("from_x", "from_y", "from_slope_x", "from_slope_y")]

    packed = pltpu.VMEM(message.shape, full_type)
    halved = pltpu.VMEM((2, mid, length_y), full_type)

    def solve(mine, other, fields, beside=()):
        (sums,) = call(
            gather_kernel, (message,), [smem(), vmem(), vmem(), vmem()],
            [halved, packed, pltpu.SemaphoreType.DMA((1,))], 8 * count * block,
            (flags, mine, other, stacked), (hbm(),),
        )
        sums = lax.all_to_all(sums, "chip", split_axis=0, concat_axis=0, tiled=True)
        (sums,) = call(
            scan_kernel, (message,), [hbm(), vmem()],
            [packed, packed, pltpu.SemaphoreType.DMA((2,))], 4 * block, (sums, ratio), (hbm(),),
        )
        sums, *beside = lax.optimization_barrier((sums, *beside))
        sums = lax.all_to_all(sums, "chip", split_axis=0, concat_axis=0, tiled=True)
        solved = shaped(fields, mid, length_y)
        own, partner = call(
            solve_kernel, (solved, solved), [smem()] + [vmem()] * 3 + [hbm()],
            [halved, packed, pltpu.SemaphoreType.DMA((1,))], 16 * count * block,
            (flags, mine, other, stacked, sums),
        )
        partner = lax.ppermute(partner, "core", swap)
        ghosts = bool(beside)
        half_fields = 3 * depth + (5 if ghosts else 0)
        (slots,) = call(
            functools.partial(own_half_kernel, ghosts=ghosts),
            (shaped(half_fields, mid, length_y),), [smem()] + [vmem()] * 5, [],
            3 * half_fields * block * (length_x // 2 + length_y) // 2,
            (flags, own, *pressure_tables),
        )
        return own, partner, slots, *beside

    rounded = pltpu.VMEM((3, depth, length_x, length_y), half_type)
    state = pltpu.VMEM(state_shape, full_type)
    tendency_flops = 3 * depth * block * (length_x + length_y)
    source_flops = 3 * depth * block * (length_x + 2 * length_y)

    ghosts = pltpu.VMEM((2, 3, length_x, length_y), full_type)
    partial, weights = call(
        inner_kernel,
        (own_shape, edge),
        [smem(), smem(), hbm()] + [vmem()] * 5,
        [state, rounded, pltpu.SemaphoreType.DMA((1,))],
        tendency_flops,
        (flags, fringe_columns, current, columns, viscosity, turbine_mask, *tendency_tables),
    )
    partial, stacked, ratio, rows_x, rows_slope_x = lax.optimization_barrier(
        (partial, stacked, ratio, rows_x, rows_slope_x)
    )

    def spectra(partial, weights, low, high, columns_low, columns_high, edges):
        middle, theirs = call(
            outer_kernel,
            (own_shape, spectrum),
            [smem(), smem()] + [vmem()] * 2 + [hbm()] * 2 + [vmem()] * 6,
            [ghosts, pltpu.SemaphoreType.DMA((2,))],
            source_flops // 2,
            (flags, fringe_columns, partial, weights, low, high, columns_low, columns_high,
             *source_tables),
        )
        other = lax.ppermute(theirs, "core", swap)
        mine, *edges = call(
            own_spectra_kernel,
            (spectrum, *edges),
            [smem()] + [vmem()] * 5,
            [],
            source_flops // 2,
            (flags, middle, *source_tables),
        )
        return middle, mine, other, *edges

    middle, mine, other, upward, downward = spectra(
        partial, weights, low, high, columns_low, columns_high, (edge, edge)
    )
    from_below = lax.ppermute(upward, levels_axis, upward_route)
    from_above = lax.ppermute(downward, levels_axis, downward_route)
    own, partner, slots, from_below, from_above = solve(
        mine, other, depth + 2, (from_below, from_above)
    )
    taken = call(
        fringe_kernel, bands, [smem(), smem()] + [vmem()] * 7, [],
        9 * depth * block * (length_x + length_y) // 8,
        (flags, fringe_columns, own, partner, middle, rows_x, rows_slope_x,
         tables["from_y"], tables["from_slope_y"]),
    )
    partner, *taken = lax.optimization_barrier((partner, *taken))
    new_columns = lax.ppermute(taken[0], every_axis, across(0))
    new_columns_low = lax.ppermute(taken[1], every_axis, across(1))
    half_fields = 3 * depth + 5
    corrected, low, high = call(
        corrected_kernel,
        (own_shape, whole_edge, whole_edge),
        [smem()] + [vmem()] * 11,
        [pltpu.VMEM((half_fields, mid, length_y), full_type)],
        3 * half_fields * block * (length_x // 2 + length_y) // 2,
        (flags, slots, partner, middle, from_below, from_above, tables["slope_x"],
         tables["slope_y"], *pressure_tables),
    )
    new_columns, corrected = lax.optimization_barrier((new_columns, corrected))
    new_columns_high = lax.ppermute(new_columns[:, 0], every_axis, farm_downward)
    partial, weights = call(
        inner_kernel,
        (own_shape, edge),
        [smem(), smem(), hbm(), vmem(), hbm()] + [vmem()] * 5,
        [state, rounded, pltpu.SemaphoreType.DMA((2,)), pltpu.VMEM(own_shape.shape, full_type)],
        tendency_flops,
        (flags, fringe_columns, corrected, new_columns, current, columns, viscosity, turbine_mask,
         *tendency_tables),
    )
    final, mine, other = spectra(
        partial, weights, low, high, new_columns_low, new_columns_high, ()
    )
    _, partner, slots = solve(mine, other, depth + 1)
    half_fields = 3 * depth
    (new,) = call(
        last_kernel,
        (own_shape,),
        [smem()] + [vmem()] * 7,
        [pltpu.VMEM((half_fields, mid, length_y), full_type)],
        3 * half_fields * block * (length_x // 2 + length_y) // 2,
        (flags, slots, partner, final, *pressure_tables),
    )
    return new[None]


def solution(mesh):
    sections, devices = mesh.devices.shape
    fine = Mesh(mesh.devices.reshape(sections, devices // 2, 2), every_axis)
    placed = (
        P("sec", None, levels_axis, None, None),
        P("sec", levels_axis, None, None),
        P(levels_axis, None, None),
        P(),
    )
    return jax.shard_map(
        local,
        mesh=fine,
        in_specs=placed,
        out_specs=P("sec", None, levels_axis, None, None),
        check_vma=False,
    )
```

```python
import functools
import math

import jax
import jax.numpy as jnp
import ml_dtypes
import numpy as np
from jax import lax
from jax.experimental import pallas as pl
from jax.experimental.pallas import tpu as pltpu
from jax.sharding import Mesh
from jax.sharding import PartitionSpec as P

step_size = 0.1
drag_coef = 0.75
cell_width = 4.0
half_type = jnp.bfloat16
full_type = jnp.float32
vmem_bytes = 26 * 1024 * 1024
levels_axis = ("chip", "core")
every_axis = ("sec", "chip", "core")


def derivative_table(length, cutoff):
    offset = np.arange(length)
    wavenumber = np.arange(1, cutoff + 1)
    phases = offset[:, None] * wavenumber[None, :] % length
    waves = np.sin(2.0 * math.pi / length * phases)
    first = -(2.0 / (cell_width * length)) * (waves @ (2.0 * math.pi / length * wavenumber))
    return first[(offset[:, None] - offset[None, :]) % length]


def real_basis(length):
    midpoint = length // 2
    row = np.arange(length)
    wavenumber = np.where(row <= midpoint, row, row - midpoint)
    angles = 2.0 * math.pi / length * (wavenumber[:, None] * row[None, :] % length)
    scales = np.where((row == 0) | (row == midpoint), math.sqrt(1.0 / length), math.sqrt(2.0 / length))
    return scales[:, None] * np.where((row <= midpoint)[:, None], np.cos(angles), np.sin(angles))


def wave_square(length):
    midpoint = length // 2
    row = np.arange(length)
    wavenumber = np.where(row < midpoint, row, np.where(row == midpoint, 0, row - midpoint))
    return (2.0 * math.pi / (length * cell_width) * wavenumber) ** 2


def high_low(table):
    table = np.asarray(table, np.float32)
    high = table.astype(ml_dtypes.bfloat16)
    low = (table - high.astype(np.float32)).astype(ml_dtypes.bfloat16)
    return np.stack([high, low], axis=-3)


def build_tables(length_x, length_y):
    mid = length_x // 2
    full_x = derivative_table(length_x, length_x // 2 - 1)
    full_y = derivative_table(length_y, length_y // 2 - 1)
    basis_x = real_basis(length_x)
    basis_y = real_basis(length_y)
    left_part, right_part = full_x[:mid, :mid], full_x[:mid, mid:]
    derived = full_x @ basis_x.T
    squares = wave_square(length_x)[:, None] + wave_square(length_y)[None, :]
    decay = 2.0 * np.arcsinh(0.5 * np.sqrt(squares))
    return {
        "dealias_x": derivative_table(length_x, (length_x - 1) // 3).astype(ml_dtypes.bfloat16),
        "dealias_y": derivative_table(length_y, (length_y - 1) // 3).T.astype(ml_dtypes.bfloat16),
        "slope_x": high_low(np.stack([left_part + right_part, left_part - right_part])),
        "slope_y": high_low(full_y.T),
        "into_x": high_low(np.stack([basis_x[0::2, :mid], basis_x[1::2, :mid]])),
        "into_y": high_low(basis_y.T),
        "from_x": high_low(np.stack([basis_x[0::2, :mid].T, basis_x[1::2, :mid].T])),
        "from_y": high_low(basis_y),
        "from_slope_x": high_low(np.stack([derived[:mid, 0::2], derived[:mid, 1::2]])),
        "from_slope_y": high_low(basis_y @ full_y.T),
        "decay": np.stack([decay[0::2], decay[1::2]]).astype(np.float32),
    }


def product(one, other):
    return jnp.dot(one, other, preferred_element_type=full_type)


def halves(block):
    high = block.astype(half_type)
    return high, (block - high.astype(full_type)).astype(half_type)


def from_left(table, block):
    high, low = halves(block)
    return product(table[0], high) + product(table[0], low) + product(table[1], high)


def from_right(block, table):
    high, low = halves(block)
    return product(high, table[0]) + product(low, table[0]) + product(high, table[1])


def vmem():
    return pl.BlockSpec(memory_space=pltpu.VMEM)


def smem():
    return pl.BlockSpec(memory_space=pltpu.SMEM)


def hbm():
    return pl.BlockSpec(memory_space=pltpu.HBM)


def call(kernel, outs, in_specs, scratch, flops, args, out_specs=None):
    moved = sum(math.prod(a.shape) * 4 for a in (*outs, *args))
    return pl.pallas_call(
        kernel,
        out_shape=outs,
        in_specs=in_specs,
        out_specs=out_specs or tuple(vmem() for _ in outs),
        scratch_shapes=scratch,
        compiler_params=pltpu.CompilerParams(vmem_limit_bytes=vmem_bytes),
        cost_estimate=pl.CostEstimate(flops=int(flops), bytes_accessed=moved, transcendentals=0),
    )(*args)


def shaped(*dims, kind=full_type):
    return jax.ShapeDtypeStruct(dims, kind)


def tendency_steps(state, rounded, viscosity, mask, drag, dealias_x, dealias_y, put):
    depth = state.shape[1]
    length_x = state.shape[2]
    rows = length_x // 2
    for z in range(depth):
        for c in range(3):
            rounded[c, z] = state[c, z].astype(half_type)
    for z in range(depth):
        for b in range(length_x // rows):
            part = pl.ds(b * rows, rows)
            u, v, w = (state[c, z, part, :] for c in range(3))
            slow = drag * mask[z, part, :].astype(full_type) * jnp.abs(u)
            nu = viscosity[z, part, :]
            still = 2.0 * nu + slow
            rising = nu - 0.5 * w if z < depth - 1 else None
            sinking = nu + 0.5 * w if z > 0 else None
            for c in range(3):
                center = state[c, z, part, :]
                grad_x = product(dealias_x[part, :], rounded[c, z])
                grad_y = product(rounded[c, z, part, :], dealias_y[...])
                change = -(u * grad_x + v * grad_y + still * center)
                if rising is not None:
                    change += rising * state[c, z + 1, part, :]
                if sinking is not None:
                    change += sinking * state[c, z - 1, part, :]
                put(c, z, part, center, change)


def folded(block, sign):
    mid = block.shape[0] // 2
    return block[:mid] + sign * block[mid:]


def source_spectra(state, out, half, slope_x, slope_y, into_x, into_y):
    depth = state.shape[1]
    sign = (1 - 2 * half).astype(full_type)
    slope, into = slope_x[half], into_x[half]
    lifted = [folded(state[2, z], sign) for z in range(depth)]
    sources = []
    for z in range(depth):
        spread = from_left(slope, folded(state[0, z], sign))
        spread += from_right(folded(state[1, z], sign), slope_y)
        sources.append(spread + lifted[z] - (lifted[z - 1] if z else 0.0))
    sources.append(lifted[depth - 1])
    for z, source in enumerate(sources):
        out[z] = from_right(from_left(into, source), into_y)


def edges_kernel(velocity, low, high):
    depth = velocity.shape[1]
    low[...] = velocity[:, depth - 1]
    high[...] = velocity[:, 0]


def columns_kernel(index, velocity, columns, columns_low, columns_high):
    depth = velocity.shape[1]

    def one(i, carry):
        row = pl.ds(index[i], 1)
        here = pl.ds(i, 1)
        for c in range(3):
            for z in range(depth):
                taken = velocity[c, z, row, :]
                columns[c, z, here, :] = taken
                if z == depth - 1:
                    columns_low[c, here, :] = taken
                if z == 0:
                    columns_high[c, here, :] = taken
        return carry

    lax.fori_loop(0, index.shape[0], one, 0, unroll=8)


def insert_rows(index, pairs):
    def one(i, carry):
        row = pl.ds(index[i], 1)
        for target, rows in pairs:
            for c in range(3):
                target[c, row, :] = rows[c, pl.ds(i, 1), :]
        return carry

    lax.fori_loop(0, index.shape[0], one, 0, unroll=8)


def inner_kernel(flags, index, given, columns, viscosity, mask, dealias_x, dealias_y, *refs):
    depth = given.shape[1]
    earlier = refs[0] if len(refs) == 5 else None
    partial, weights, state, rounded = refs[-4:]
    is_farm = flags[0]
    state[...] = given[...]

    @pl.when(is_farm == 1)
    def _():
        insert_rows(index, [(state.at[:, z], columns.at[:, z]) for z in range(depth)])

    drag = drag_coef * is_farm.astype(full_type)
    share = 1.0 if earlier is None else 0.5

    def put(c, z, part, center, change):
        moved = center + step_size * change
        if earlier is not None:
            moved = 0.5 * (earlier[c, z, part, :] + moved)
        partial[c, z, part, :] = moved

    tendency_steps(state, rounded, viscosity, mask, drag, dealias_x, dealias_y, put)
    weights[0] = share * step_size * (viscosity[0] + 0.5 * state[2, 0])
    weights[1] = share * step_size * (viscosity[depth - 1] - 0.5 * state[2, depth - 1])


def outer_kernel(
    flags, index, partial, weights, low, high, columns_low, columns_high,
    slope_x, slope_y, into_x, into_y,
    middle, theirs,
):
    depth = middle.shape[1]
    is_farm, core, is_lid = flags[0], flags[1], flags[3]
    for c in range(3):
        for z in range(depth):
            moved = partial[c, z]
            if z == 0:
                moved += weights[0] * low[c]
            if z == depth - 1:
                moved += weights[1] * high[c]
                if c == 2:
                    moved = jnp.where(is_lid == 1, 0.0, moved)
            middle[c, z] = moved

    @pl.when(is_farm == 1)
    def _():
        def one(i, carry):
            row = pl.ds(index[i], 1)
            here = pl.ds(i, 1)
            for c in range(3):
                lag = columns_low[c, here, :] - low[c, row, :]
                middle[c, 0, row, :] += weights[0, row, :] * lag
                lag = columns_high[c, here, :] - high[c, row, :]
                middle[c, depth - 1, row, :] += weights[1, row, :] * lag
            return carry

        lax.fori_loop(0, index.shape[0], one, 0, unroll=8)

    source_spectra(middle, theirs, 1 - core, slope_x, slope_y, into_x, into_y)


def own_spectra_kernel(flags, middle, slope_x, slope_y, into_x, into_y, mine, *edges):
    depth = middle.shape[1]
    mid = middle.shape[2] // 2
    source_spectra(middle, mine, flags[1], slope_x, slope_y, into_x, into_y)
    if not edges:
        return
    upward, downward = edges
    downward[0] = middle[0, 0]
    downward[1] = middle[1, 0]
    top = depth - 1
    even, odd = (
        0.5 * from_left(slope_x[half], folded(middle[2, top], 1.0 - 2.0 * half))
        for half in range(2)
    )
    upward[0, :mid] = middle[0, top, :mid] + (even + odd)
    upward[0, mid:] = middle[0, top, mid:] + (even - odd)
    upward[1] = middle[1, top] + from_right(middle[2, top], slope_y)


def chip_levels(core, mine, other, depth):
    is_low = core == 0
    low = [jnp.where(is_low, mine[i], other[i]) for i in range(depth + 1)]
    high = [jnp.where(is_low, other[i], mine[i]) for i in range(depth + 1)]
    levels = low[:depth] + [high[0] - low[depth]] + high[1:depth]
    return levels, low[depth], high[depth]


class Coefficients:
    def __init__(self, stacked, count):
        self.mu = lambda: stacked[0]
        self.phi = lambda i: stacked[1 + i]
        self.psi = lambda i: stacked[2 + count + i]
        self.flux_low = lambda i: stacked[3 + 2 * count + i]
        self.flux_high = lambda i: stacked[3 + 3 * count + i]
        self.entry = lambda: stacked[4 + 4 * count]
        self.scale = lambda: stacked[5 + 4 * count]


def gather_kernel(flags, mine, other, stacked, out, work, packed, sems):
    core = flags[1]
    depth = mine.shape[0] - 1
    count = 2 * depth
    tables = Coefficients(stacked, count)
    levels, _, top = chip_levels(core, mine, other, depth)
    mu = tables.mu()
    forward = tables.phi(0) * levels[0]
    for i in range(1, count):
        forward = mu * forward + tables.phi(i) * levels[i]
    work[0] = mu * forward - tables.phi(count) * top
    backward = -tables.psi(count) * top
    for i in reversed(range(count)):
        backward = tables.psi(i) * levels[i] + mu * backward
    work[1] = backward
    chips = out.shape[0]
    rows = out.shape[1] // 2
    for chip in range(chips):
        packed[chip, :rows] = work[0, chip * rows : (chip + 1) * rows]
        packed[chip, rows:] = work[1, chip * rows : (chip + 1) * rows]
    copy = pltpu.make_async_copy(packed, out, sems.at[0])
    copy.start()
    copy.wait()


def scan_kernel(received, ratio, out, taken, packed, sems):
    chips = received.shape[0]
    rows = received.shape[1] // 2
    copy = pltpu.make_async_copy(received, taken, sems.at[0])
    copy.start()
    factor = ratio[...]
    copy.wait()
    carried = jnp.zeros_like(factor)
    for chip in range(chips):
        packed[chip, :rows] = carried
        carried = factor * carried + taken[chip, :rows]
    carried = jnp.zeros_like(factor)
    for chip in reversed(range(chips)):
        packed[chip, rows:] = carried
        carried = factor * carried + taken[chip, rows:]
    copy = pltpu.make_async_copy(packed, out, sems.at[1])
    copy.start()
    copy.wait()


def solve_kernel(flags, mine, other, stacked, received, own, partner, work, scanned, sems):
    core = flags[1]
    depth = mine.shape[0] - 1
    count = 2 * depth
    tables = Coefficients(stacked, count)
    chips = scanned.shape[0]
    rows = scanned.shape[1] // 2
    copy = pltpu.make_async_copy(received, scanned, sems.at[0])
    copy.start()
    copy.wait()
    for chip in range(chips):
        work[0, chip * rows : (chip + 1) * rows] = scanned[chip, :rows]
        work[1, chip * rows : (chip + 1) * rows] = scanned[chip, rows:]
    levels, between, top = chip_levels(core, mine, other, depth)
    mu = tables.mu()
    forward = [work[0] + tables.phi(0) * levels[0]]
    for i in range(1, count):
        forward.append(mu * forward[-1] + tables.phi(i) * levels[i])
    backward = [work[1] - tables.psi(count) * top]
    for i in reversed(range(1, count)):
        backward.append(tables.psi(i) * levels[i] + mu * backward[-1])
    backward.reverse()
    flux = [
        tables.flux_low(i) * forward[i] - tables.flux_high(i + 1) * backward[i]
        for i in range(count)
    ]
    under = tables.entry() * work[0] - tables.flux_high(0) * (
        tables.psi(0) * levels[0] + mu * backward[0]
    )
    pressure = [
        -tables.scale() * (tables.psi(i) * forward[i] + mu * tables.phi(i) * backward[i])
        for i in (0, depth)
    ]
    low = [pressure[0], *flux[:depth], under]
    high = [pressure[1], *flux[depth:], flux[depth - 1] - between]
    is_low = core == 0
    for i in range(own.shape[0]):
        own[i] = jnp.where(is_low, low[i], high[i])
        partner[i] = jnp.where(is_low, high[i], low[i])


def physical_half(fields, half, ghosts, from_x, from_y, from_slope_x, from_slope_y, slots):
    depth = fields.shape[0] - (2 if ghosts else 1)
    level = fields[0]
    pressures = [level - fields[depth + 1]] if ghosts else []
    for z in range(depth):
        pressures.append(level)
        level = level + fields[1 + z]
    if ghosts:
        pressures.append(level)
    for i, block in enumerate(pressures):
        slots[2 * i] = from_left(from_slope_x[half], from_right(block, from_y))
        slots[2 * i + 1] = from_left(from_x[half], from_right(block, from_slope_y))
    for i in range(fields.shape[0] - 1):
        block = from_right(fields[1 + i], from_y)
        slots[2 * len(pressures) + i] = from_left(from_x[half], block)


def own_half_kernel(flags, mine, from_x, from_y, from_slope_x, from_slope_y, slots, *, ghosts):
    physical_half(mine, flags[1], ghosts, from_x, from_y, from_slope_x, from_slope_y, slots)


def unfolded(core, mine, other, i):
    sign = (1 - 2 * core).astype(full_type)
    return mine[i] + other[i], sign * (mine[i] - other[i])


def fringe_kernel(
    flags, index, mine, other, middle, rows_x, rows_slope_x, from_y, from_slope_y,
    columns, columns_low, columns_high,
):
    core = flags[1]
    depth = middle.shape[1]
    count = rows_x.shape[2]
    slopes = [0.0] * depth
    plains = [0.0] * depth
    lifts = [0.0] * depth
    for half in range(2):
        fields = [jnp.where(core == half, mine[i], other[i]) for i in range(1 + depth)]
        single = jnp.concatenate([rows_x[half, 0], rows_x[half, 1]])
        both = jnp.concatenate([rows_slope_x[half, 0], single, rows_slope_x[half, 1]])
        level = fields[0]
        for z in range(depth):
            high, low = halves(level)
            by_high = product(both, high)
            by_low = product(both[: 2 * count], low)
            slopes[z] += by_high[:count] + by_high[3 * count :] + by_low[:count]
            plains[z] += by_high[count : 2 * count] + by_high[2 * count : 3 * count]
            plains[z] += by_low[count:]
            high, low = halves(fields[1 + z])
            by_high = product(single, high)
            lifts[z] += by_high[:count] + by_high[count:] + product(single[:count], low)
            level = level + fields[1 + z]
    through = from_right(jnp.concatenate(slopes + lifts), from_y)
    across = from_right(jnp.concatenate(plains), from_slope_y)
    for z in range(depth):
        columns[0, z] = through[z * count : (z + 1) * count]
        columns[1, z] = across[z * count : (z + 1) * count]
        columns[2, z] = through[(depth + z) * count : (depth + z + 1) * count]

    def one(i, carry):
        row = pl.ds(index[i], 1)
        here = pl.ds(i, 1)
        for c in range(3):
            for z in range(depth):
                value = middle[c, z, row, :] - columns[c, z, here, :]
                columns[c, z, here, :] = value
                if z == depth - 1:
                    columns_low[c, here, :] = value
                if z == 0:
                    columns_high[c, here, :] = value
        return carry

    lax.fori_loop(0, index.shape[0], one, 0, unroll=8)


def corrected_kernel(
    flags, slots, fields, middle, from_x, from_y, from_slope_x, from_slope_y,
    out, low_change, high_change,
    others,
):
    core = flags[1]
    depth = middle.shape[1]
    mid = middle.shape[2] // 2
    physical_half(
        fields, 1 - core, True, from_x, from_y, from_slope_x, from_slope_y, others
    )
    pressures = depth + 2
    sides = (slice(0, mid), slice(mid, 2 * mid))
    for z in range(depth):
        for c in range(3):
            slot = 2 * (1 + z) + c if c < 2 else 2 * pressures + z
            for side, change in zip(sides, unfolded(core, slots, others, slot)):
                out[c, z, side] = middle[c, z, side] - change
    for c in range(3):
        slot = c if c < 2 else 2 * pressures + depth
        for side, change in zip(sides, unfolded(core, slots, others, slot)):
            low_change[c, side] = change
    for c in range(2):
        slot = 2 * (depth + 1) + c
        for side, change in zip(sides, unfolded(core, slots, others, slot)):
            high_change[c, side] = change


def ghost_kernel(
    flags, out, low_change, high_change, from_below, from_above, slope_x, slope_y,
    low, high,
):
    is_floor, is_lid = flags[2], flags[3]
    depth = out.shape[1]
    mid = out.shape[2] // 2
    open_low = (1 - is_floor).astype(full_type)
    open_high = (1 - is_lid).astype(full_type)
    for c in range(2):
        low[c] = open_low * (from_below[c] - low_change[c])
        high[c] = open_high * (from_above[c] - high_change[c])
    low[2] = -open_low * low_change[2]
    even, odd = (
        0.5 * from_left(slope_x[half], folded(high[0], 1.0 - 2.0 * half)) for half in range(2)
    )
    sides = (slice(0, mid), slice(mid, 2 * mid))
    for side, change in zip(sides, (even + odd, even - odd)):
        spread = change + from_right(high[1, side], slope_y)
        high[2, side] = open_high * (out[2, depth - 1, side] - spread)


def last_kernel(
    flags, slots, fields, final, from_x, from_y, from_slope_x, from_slope_y,
    out,
    others,
):
    core = flags[1]
    depth = final.shape[1]
    mid = final.shape[2] // 2
    physical_half(
        fields, 1 - core, False, from_x, from_y, from_slope_x, from_slope_y, others
    )
    sides = (slice(0, mid), slice(mid, 2 * mid))
    for z in range(depth):
        for c in range(3):
            slot = 2 * z + c if c < 2 else 2 * depth + z
            for side, change in zip(sides, unfolded(core, slots, others, slot)):
                out[c, z, side] = final[c, z, side] - change


def coefficients(decay, first_level, count, height):
    def gap(steps):
        return -jnp.expm1(-steps * decay)

    still = decay == 0.0
    below = jnp.arange(count + 1, dtype=full_type)[:, None, None] + first_level
    mu = jnp.exp(-decay)
    safe = jnp.where(still, 1.0, gap(2.0 * height))

    def ratio(steps):
        return jnp.where(still, steps / height, gap(2.0 * steps) / safe)

    share = 1.0 / (1.0 + mu)
    phi = 1.0 + jnp.exp(-(2.0 * below + 1.0) * decay)
    psi = 1.0 + jnp.exp(-(2.0 * (height - below) - 1.0) * decay)
    flux_low = mu * share * ratio(height - 1.0 - below[:count])
    flux_high = mu * share * ratio(below)
    entry = share * ratio(height - below[:1])
    scale = jnp.where(still, 0.0, mu / (jnp.where(still, 1.0, gap(2.0)) * safe))
    return jnp.concatenate([mu[None], phi, psi, flux_low, flux_high, entry, scale[None]])


def local(velocity, eddy_viscosity, turbine_mask, fringe_columns):
    current = velocity[0]
    viscosity = eddy_viscosity[0]
    _, depth, length_x, length_y = current.shape
    mid = length_x // 2
    fringe = fringe_columns.shape[0]
    chips = lax.axis_size("chip")
    devices = 2 * chips
    height = devices * depth
    count = 2 * depth
    rows = mid // chips
    section = lax.axis_index("sec")
    chip = lax.axis_index("chip")
    core = lax.axis_index("core")
    place = 2 * chip + core
    is_farm = section == 1
    flags = jnp.stack([is_farm, core, place == 0, place == devices - 1]).astype(jnp.int32)
    tables = {name: jnp.asarray(table) for name, table in build_tables(length_x, length_y).items()}

    upward_route = [(i, i + 1) for i in range(devices - 1)]
    downward_route = [(i + 1, i) for i in range(devices - 1)]
    swap = [(0, 1), (1, 0)]

    def across(shift):
        return [
            (i, devices + i + shift) for i in range(devices) if 0 <= i + shift < devices
        ]

    state_shape = (3, depth + 2, length_x, length_y)
    own_shape = shaped(3, depth, length_x, length_y)
    edge = shaped(2, length_x, length_y)
    whole_edge = shaped(3, length_x, length_y)
    band = shaped(3, fringe, length_y)
    bands = (shaped(3, depth, fringe, length_y), band, band)
    decay = lax.dynamic_index_in_dim(tables["decay"], core, 0, keepdims=False)
    stacked = coefficients(decay, (chip * count).astype(full_type), count, float(height))
    ratio = jnp.exp(-float(count) * lax.dynamic_slice_in_dim(decay, chip * rows, rows, 0))

    low, high = call(edges_kernel, (whole_edge, whole_edge), [vmem()], [], 0, (current,))
    low, high, held = lax.optimization_barrier((low, high, current))
    low = lax.ppermute(low, levels_axis, upward_route)
    high = lax.ppermute(high, levels_axis, downward_route)
    farm_downward = [(devices + i + 1, devices + i) for i in range(devices - 1)]

    held, stacked = lax.optimization_barrier((held, stacked))
    taken = [*call(columns_kernel, bands, [smem(), vmem()], [], 0, (fringe_columns, held))]
    columns = lax.ppermute(taken[0], every_axis, across(0))
    away = jnp.where(fringe_columns < mid, 1.0, -1.0)[:, None]
    signs = jnp.stack([jnp.ones_like(away), away])[:, None].astype(half_type)
    rows_x, rows_slope_x = (
        jnp.take(tables[name], fringe_columns % mid, axis=2) * signs
        for name in ("from_x", "from_slope_x")
    )

    rows_x, taken[1] = lax.optimization_barrier((rows_x, taken[1]))
    columns_low = lax.ppermute(taken[1], every_axis, across(1))
    columns_high = lax.ppermute(columns[:, 0], every_axis, farm_downward)
    block = length_x * length_y * 2
    spectrum = shaped(depth + 1, mid, length_y)
    message = shaped(chips, 2 * rows, length_y)
    tendency_tables = [tables["dealias_x"], tables["dealias_y"]]
    source_tables = [tables[n] for n in ("slope_x", "slope_y", "into_x", "into_y")]
    pressure_tables = [tables[n] for n in ("from_x", "from_y", "from_slope_x", "from_slope_y")]

    packed = pltpu.VMEM(message.shape, full_type)
    halved = pltpu.VMEM((2, mid, length_y), full_type)

    def solve(mine, other, fields, beside=()):
        (sums,) = call(
            gather_kernel, (message,), [smem(), vmem(), vmem(), vmem()],
            [halved, packed, pltpu.SemaphoreType.DMA((1,))], 8 * count * block,
            (flags, mine, other, stacked), (hbm(),),
        )
        sums = lax.all_to_all(sums, "chip", split_axis=0, concat_axis=0, tiled=True)
        (sums,) = call(
            scan_kernel, (message,), [hbm(), vmem()],
            [packed, packed, pltpu.SemaphoreType.DMA((2,))], 4 * block, (sums, ratio), (hbm(),),
        )
        sums = lax.all_to_all(sums, "chip", split_axis=0, concat_axis=0, tiled=True)
        solved = shaped(fields, mid, length_y)
        own, partner = call(
            solve_kernel, (solved, solved), [smem()] + [vmem()] * 3 + [hbm()],
            [halved, packed, pltpu.SemaphoreType.DMA((1,))], 16 * count * block,
            (flags, mine, other, stacked, sums),
        )
        own, *beside = lax.optimization_barrier((own, *beside))
        partner = lax.ppermute(partner, "core", swap)
        ghosts = bool(beside)
        half_fields = 3 * depth + (5 if ghosts else 0)
        (slots,) = call(
            functools.partial(own_half_kernel, ghosts=ghosts),
            (shaped(half_fields, mid, length_y),), [smem()] + [vmem()] * 5, [],
            3 * half_fields * block * (length_x // 2 + length_y) // 2,
            (flags, own, *pressure_tables),
        )
        return own, partner, slots, *beside

    rounded = pltpu.VMEM((3, depth, length_x, length_y), half_type)
    state = pltpu.VMEM(state_shape, full_type)
    tendency_flops = 3 * depth * block * (length_x + length_y)
    source_flops = 3 * depth * block * (length_x + 2 * length_y)

    def inner(state, columns, earlier):
        kept = () if earlier else (own_shape,)
        return call(
            inner_kernel,
            (own_shape, edge, *kept),
            [smem(), smem()] + [vmem()] * (6 + len(earlier)),
            ([pltpu.VMEM(own_shape.shape, full_type)] if earlier else []) + [rounded],
            tendency_flops,
            (flags, fringe_columns, state, columns, viscosity, turbine_mask, *tendency_tables,
             *earlier),
        )

    partial, weights, start = inner(current, columns, ())
    partial, stacked, ratio, rows_x, rows_slope_x = lax.optimization_barrier(
        (partial, stacked, ratio, rows_x, rows_slope_x)
    )

    def spectra(partial, weights, low, high, columns_low, columns_high, edges):
        middle, theirs = call(
            outer_kernel,
            (own_shape, spectrum),
            [smem(), smem()] + [vmem()] * 10,
            [],
            source_flops // 2,
            (flags, fringe_columns, partial, weights, low, high, columns_low, columns_high,
             *source_tables),
        )
        other = lax.ppermute(theirs, "core", swap)
        mine, *edges = call(
            own_spectra_kernel,
            (spectrum, *edges),
            [smem()] + [vmem()] * 5,
            [],
            source_flops // 2,
            (flags, middle, *source_tables),
        )
        return middle, mine, other, *edges

    middle, mine, other, upward, downward = spectra(
        partial, weights, low, high, columns_low, columns_high, (edge, edge)
    )
    own, partner, slots, upward, downward = solve(mine, other, depth + 2, (upward, downward))
    from_below = lax.ppermute(upward, levels_axis, upward_route)
    from_above = lax.ppermute(downward, levels_axis, downward_route)
    taken = call(
        fringe_kernel, bands, [smem(), smem()] + [vmem()] * 7, [],
        9 * depth * block * (length_x + length_y) // 8,
        (flags, fringe_columns, own, partner, middle, rows_x, rows_slope_x,
         tables["from_y"], tables["from_slope_y"]),
    )
    partner, *taken = lax.optimization_barrier((partner, *taken))
    new_columns = lax.ppermute(taken[0], every_axis, across(0))
    slots, *taken[1:] = lax.optimization_barrier((slots, *taken[1:]))
    new_columns_low = lax.ppermute(taken[1], every_axis, across(1))
    new_columns_high = lax.ppermute(taken[2], every_axis, across(-1))
    half_fields = 3 * depth + 5
    corrected, low_change, high_change = call(
        corrected_kernel,
        (own_shape, whole_edge, edge),
        [smem()] + [vmem()] * 7,
        [pltpu.VMEM((half_fields, mid, length_y), full_type)],
        3 * half_fields * block * (length_x // 2 + length_y) // 2,
        (flags, slots, partner, middle, *pressure_tables),
    )
    new_columns, corrected = lax.optimization_barrier((new_columns, corrected))
    partial, weights = inner(corrected, new_columns, (start,))
    partial, from_below, from_above = lax.optimization_barrier((partial, from_below, from_above))
    low, high = call(
        ghost_kernel, (whole_edge, whole_edge), [smem()] + [vmem()] * 7, [],
        3 * block * (length_x // 2 + length_y),
        (flags, corrected, low_change, high_change, from_below, from_above, tables["slope_x"],
         tables["slope_y"]),
    )
    final, mine, other = spectra(
        partial, weights, low, high, new_columns_low, new_columns_high, ()
    )
    _, partner, slots = solve(mine, other, depth + 1)
    half_fields = 3 * depth
    (new,) = call(
        last_kernel,
        (own_shape,),
        [smem()] + [vmem()] * 7,
        [pltpu.VMEM((half_fields, mid, length_y), full_type)],
        3 * half_fields * block * (length_x // 2 + length_y) // 2,
        (flags, slots, partner, final, *pressure_tables),
    )
    return new[None]


def solution(mesh):
    sections, devices = mesh.devices.shape
    fine = Mesh(mesh.devices.reshape(sections, devices // 2, 2), every_axis)
    placed = (
        P("sec", None, levels_axis, None, None),
        P("sec", levels_axis, None, None),
        P(levels_axis, None, None),
        P(),
    )
    return jax.shard_map(
        local,
        mesh=fine,
        in_specs=placed,
        out_specs=P("sec", None, levels_axis, None, None),
        check_vma=False,
    )
```

```python
import functools
import math

import jax
import jax.numpy as jnp
import ml_dtypes
import numpy as np
from jax import lax
from jax.experimental import pallas as pl
from jax.experimental.pallas import tpu as pltpu
from jax.sharding import Mesh
from jax.sharding import PartitionSpec as P

step_size = 0.1
drag_coef = 0.75
cell_width = 4.0
half_type = jnp.bfloat16
full_type = jnp.float32
vmem_bytes = 26 * 1024 * 1024
levels_axis = ("chip", "core")
every_axis = ("sec", "chip", "core")


def derivative_table(length, cutoff):
    offset = np.arange(length)
    wavenumber = np.arange(1, cutoff + 1)
    phases = offset[:, None] * wavenumber[None, :] % length
    waves = np.sin(2.0 * math.pi / length * phases)
    first = -(2.0 / (cell_width * length)) * (waves @ (2.0 * math.pi / length * wavenumber))
    return first[(offset[:, None] - offset[None, :]) % length]


def real_basis(length):
    midpoint = length // 2
    row = np.arange(length)
    wavenumber = np.where(row <= midpoint, row, row - midpoint)
    angles = 2.0 * math.pi / length * (wavenumber[:, None] * row[None, :] % length)
    scales = np.where((row == 0) | (row == midpoint), math.sqrt(1.0 / length), math.sqrt(2.0 / length))
    return scales[:, None] * np.where((row <= midpoint)[:, None], np.cos(angles), np.sin(angles))


def wave_square(length):
    midpoint = length // 2
    row = np.arange(length)
    wavenumber = np.where(row < midpoint, row, np.where(row == midpoint, 0, row - midpoint))
    return (2.0 * math.pi / (length * cell_width) * wavenumber) ** 2


def high_low(table):
    table = np.asarray(table, np.float32)
    high = table.astype(ml_dtypes.bfloat16)
    low = (table - high.astype(np.float32)).astype(ml_dtypes.bfloat16)
    return np.stack([high, low], axis=-3)


def build_tables(length_x, length_y):
    mid = length_x // 2
    full_x = derivative_table(length_x, length_x // 2 - 1)
    full_y = derivative_table(length_y, length_y // 2 - 1)
    basis_x = real_basis(length_x)
    basis_y = real_basis(length_y)
    left_part, right_part = full_x[:mid, :mid], full_x[:mid, mid:]
    derived = full_x @ basis_x.T
    squares = wave_square(length_x)[:, None] + wave_square(length_y)[None, :]
    decay = 2.0 * np.arcsinh(0.5 * np.sqrt(squares))
    return {
        "dealias_x": derivative_table(length_x, (length_x - 1) // 3).astype(ml_dtypes.bfloat16),
        "dealias_y": derivative_table(length_y, (length_y - 1) // 3).T.astype(ml_dtypes.bfloat16),
        "slope_x": high_low(np.stack([left_part + right_part, left_part - right_part])),
        "slope_y": high_low(full_y.T),
        "into_x": high_low(np.stack([basis_x[0::2, :mid], basis_x[1::2, :mid]])),
        "into_y": high_low(basis_y.T),
        "from_x": high_low(np.stack([basis_x[0::2, :mid].T, basis_x[1::2, :mid].T])),
        "from_y": high_low(basis_y),
        "from_slope_x": high_low(np.stack([derived[:mid, 0::2], derived[:mid, 1::2]])),
        "from_slope_y": high_low(basis_y @ full_y.T),
        "decay": np.stack([decay[0::2], decay[1::2]]).astype(np.float32),
    }


def product(one, other):
    return jnp.dot(one, other, preferred_element_type=full_type)


def halves(block):
    high = block.astype(half_type)
    return high, (block - high.astype(full_type)).astype(half_type)


def from_left(table, block):
    high, low = halves(block)
    return product(table[0], high) + product(table[0], low) + product(table[1], high)


def from_right(block, table):
    high, low = halves(block)
    return product(high, table[0]) + product(low, table[0]) + product(high, table[1])


def vmem():
    return pl.BlockSpec(memory_space=pltpu.VMEM)


def smem():
    return pl.BlockSpec(memory_space=pltpu.SMEM)


def hbm():
    return pl.BlockSpec(memory_space=pltpu.HBM)


def call(kernel, outs, in_specs, scratch, flops, args, out_specs=None):
    moved = sum(math.prod(a.shape) * 4 for a in (*outs, *args))
    return pl.pallas_call(
        kernel,
        out_shape=outs,
        in_specs=in_specs,
        out_specs=out_specs or tuple(vmem() for _ in outs),
        scratch_shapes=scratch,
        compiler_params=pltpu.CompilerParams(vmem_limit_bytes=vmem_bytes),
        cost_estimate=pl.CostEstimate(flops=int(flops), bytes_accessed=moved, transcendentals=0),
    )(*args)


def shaped(*dims, kind=full_type):
    return jax.ShapeDtypeStruct(dims, kind)


def tendency_steps(state, rounded, viscosity, mask, drag, dealias_x, dealias_y, put):
    depth = state.shape[1]
    length_x = state.shape[2]
    rows = length_x // 2
    for z in range(depth):
        for c in range(3):
            rounded[c, z] = state[c, z].astype(half_type)
    for z in range(depth):
        for b in range(length_x // rows):
            part = pl.ds(b * rows, rows)
            u, v, w = (state[c, z, part, :] for c in range(3))
            slow = drag * mask[z, part, :].astype(full_type) * jnp.abs(u)
            nu = viscosity[z, part, :]
            still = 2.0 * nu + slow
            rising = nu - 0.5 * w if z < depth - 1 else None
            sinking = nu + 0.5 * w if z > 0 else None
            for c in range(3):
                center = state[c, z, part, :]
                grad_x = product(dealias_x[part, :], rounded[c, z])
                grad_y = product(rounded[c, z, part, :], dealias_y[...])
                change = -(u * grad_x + v * grad_y + still * center)
                if rising is not None:
                    change += rising * state[c, z + 1, part, :]
                if sinking is not None:
                    change += sinking * state[c, z - 1, part, :]
                put(c, z, part, center, change)


def folded(block, sign):
    mid = block.shape[0] // 2
    return block[:mid] + sign * block[mid:]


def source_spectra(state, out, half, slope_x, slope_y, into_x, into_y):
    depth = state.shape[1]
    sign = (1 - 2 * half).astype(full_type)
    slope, into = slope_x[half], into_x[half]
    lifted = [folded(state[2, z], sign) for z in range(depth)]
    sources = []
    for z in range(depth):
        spread = from_left(slope, folded(state[0, z], sign))
        spread += from_right(folded(state[1, z], sign), slope_y)
        sources.append(spread + lifted[z] - (lifted[z - 1] if z else 0.0))
    sources.append(lifted[depth - 1])
    for z, source in enumerate(sources):
        out[z] = from_right(from_left(into, source), into_y)


def edges_kernel(velocity, low, high):
    depth = velocity.shape[1]
    low[...] = velocity[:, depth - 1]
    high[...] = velocity[:, 0]


def columns_kernel(index, velocity, columns, columns_low, columns_high):
    depth = velocity.shape[1]

    def one(i, carry):
        row = pl.ds(index[i], 1)
        here = pl.ds(i, 1)
        for c in range(3):
            for z in range(depth):
                taken = velocity[c, z, row, :]
                columns[c, z, here, :] = taken
                if z == depth - 1:
                    columns_low[c, here, :] = taken
                if z == 0:
                    columns_high[c, here, :] = taken
        return carry

    lax.fori_loop(0, index.shape[0], one, 0, unroll=8)


def insert_rows(index, pairs):
    def one(i, carry):
        row = pl.ds(index[i], 1)
        for target, rows in pairs:
            for c in range(3):
                target[c, row, :] = rows[c, pl.ds(i, 1), :]
        return carry

    lax.fori_loop(0, index.shape[0], one, 0, unroll=8)


def inner_kernel(flags, index, given, columns, viscosity, mask, dealias_x, dealias_y, *refs):
    depth = given.shape[1]
    earlier = refs[0] if len(refs) == 5 else None
    partial, weights, state, rounded = refs[-4:]
    is_farm = flags[0]
    state[...] = given[...]

    @pl.when(is_farm == 1)
    def _():
        insert_rows(index, [(state.at[:, z], columns.at[:, z]) for z in range(depth)])

    drag = drag_coef * is_farm.astype(full_type)
    share = 1.0 if earlier is None else 0.5

    def put(c, z, part, center, change):
        moved = center + step_size * change
        if earlier is not None:
            moved = 0.5 * (earlier[c, z, part, :] + moved)
        partial[c, z, part, :] = moved

    tendency_steps(state, rounded, viscosity, mask, drag, dealias_x, dealias_y, put)
    weights[0] = share * step_size * (viscosity[0] + 0.5 * state[2, 0])
    weights[1] = share * step_size * (viscosity[depth - 1] - 0.5 * state[2, depth - 1])


def add_ghosts(
    flags, index, partial, weights, low, high, columns_low, columns_high, middle,
):
    depth = middle.shape[1]
    is_farm, is_lid = flags[0], flags[3]
    for c in range(3):
        for z in range(depth):
            moved = partial[c, z]
            if z == 0:
                moved += weights[0] * low[c]
            if z == depth - 1:
                moved += weights[1] * high[c]
                if c == 2:
                    moved = jnp.where(is_lid == 1, 0.0, moved)
            middle[c, z] = moved

    @pl.when(is_farm == 1)
    def _():
        def one(i, carry):
            row = pl.ds(index[i], 1)
            here = pl.ds(i, 1)
            for c in range(3):
                lag = columns_low[c, here, :] - low[c, row, :]
                middle[c, 0, row, :] += weights[0, row, :] * lag
                lag = columns_high[c, here, :] - high[c, row, :]
                middle[c, depth - 1, row, :] += weights[1, row, :] * lag
            return carry

        lax.fori_loop(0, index.shape[0], one, 0, unroll=8)


def outer_kernel(
    flags, index, partial, weights, low, high, columns_low, columns_high,
    slope_x, slope_y, into_x, into_y,
    middle, theirs, downward,
):
    add_ghosts(
        flags, index, partial, weights, low, high, columns_low, columns_high, middle
    )
    downward[0] = middle[0, 0]
    downward[1] = middle[1, 0]
    source_spectra(middle, theirs, 1 - flags[1], slope_x, slope_y, into_x, into_y)


def second_outer_kernel(
    flags, index, partial, weights, low_change, high_change, columns_low, columns_high,
    slope_x, slope_y, into_x, into_y, corrected, from_below, from_above,
    middle, theirs,
    low, high,
):
    ghost_levels(
        flags, corrected, low_change, high_change, from_below, from_above, slope_x, slope_y,
        low, high,
    )
    add_ghosts(
        flags, index, partial, weights, low, high, columns_low, columns_high, middle
    )
    source_spectra(middle, theirs, 1 - flags[1], slope_x, slope_y, into_x, into_y)


def own_spectra_kernel(flags, middle, slope_x, slope_y, into_x, into_y, mine, *edges):
    depth = middle.shape[1]
    mid = middle.shape[2] // 2
    source_spectra(middle, mine, flags[1], slope_x, slope_y, into_x, into_y)
    if not edges:
        return
    (upward,) = edges
    top = depth - 1
    even, odd = (
        0.5 * from_left(slope_x[half], folded(middle[2, top], 1.0 - 2.0 * half))
        for half in range(2)
    )
    upward[0, :mid] = middle[0, top, :mid] + (even + odd)
    upward[0, mid:] = middle[0, top, mid:] + (even - odd)
    upward[1] = middle[1, top] + from_right(middle[2, top], slope_y)


def chip_levels(core, mine, other, depth):
    is_low = core == 0
    low = [jnp.where(is_low, mine[i], other[i]) for i in range(depth + 1)]
    high = [jnp.where(is_low, other[i], mine[i]) for i in range(depth + 1)]
    levels = low[:depth] + [high[0] - low[depth]] + high[1:depth]
    return levels, low[depth], high[depth]


class Coefficients:
    def __init__(self, stacked, count):
        self.mu = lambda: stacked[0]
        self.phi = lambda i: stacked[1 + i]
        self.psi = lambda i: stacked[2 + count + i]
        self.flux_low = lambda i: stacked[3 + 2 * count + i]
        self.flux_high = lambda i: stacked[3 + 3 * count + i]
        self.entry = lambda: stacked[4 + 4 * count]
        self.scale = lambda: stacked[5 + 4 * count]


def gather_kernel(flags, mine, other, stacked, out, work, packed, sems):
    core = flags[1]
    depth = mine.shape[0] - 1
    count = 2 * depth
    tables = Coefficients(stacked, count)
    levels, _, top = chip_levels(core, mine, other, depth)
    mu = tables.mu()
    forward = tables.phi(0) * levels[0]
    for i in range(1, count):
        forward = mu * forward + tables.phi(i) * levels[i]
    work[0] = mu * forward - tables.phi(count) * top
    backward = -tables.psi(count) * top
    for i in reversed(range(count)):
        backward = tables.psi(i) * levels[i] + mu * backward
    work[1] = backward
    chips = out.shape[0]
    rows = out.shape[1] // 2
    for chip in range(chips):
        packed[chip, :rows] = work[0, chip * rows : (chip + 1) * rows]
        packed[chip, rows:] = work[1, chip * rows : (chip + 1) * rows]
    copy = pltpu.make_async_copy(packed, out, sems.at[0])
    copy.start()
    copy.wait()


def scan_kernel(received, ratio, out, taken, packed, sems):
    chips = received.shape[0]
    rows = received.shape[1] // 2
    copy = pltpu.make_async_copy(received, taken, sems.at[0])
    copy.start()
    factor = ratio[...]
    copy.wait()
    carried = jnp.zeros_like(factor)
    for chip in range(chips):
        packed[chip, :rows] = carried
        carried = factor * carried + taken[chip, :rows]
    carried = jnp.zeros_like(factor)
    for chip in reversed(range(chips)):
        packed[chip, rows:] = carried
        carried = factor * carried + taken[chip, rows:]
    copy = pltpu.make_async_copy(packed, out, sems.at[1])
    copy.start()
    copy.wait()


def solve_kernel(flags, mine, other, stacked, received, own, partner, work, scanned, sems):
    core = flags[1]
    depth = mine.shape[0] - 1
    count = 2 * depth
    tables = Coefficients(stacked, count)
    chips = scanned.shape[0]
    rows = scanned.shape[1] // 2
    copy = pltpu.make_async_copy(received, scanned, sems.at[0])
    copy.start()
    copy.wait()
    for chip in range(chips):
        work[0, chip * rows : (chip + 1) * rows] = scanned[chip, :rows]
        work[1, chip * rows : (chip + 1) * rows] = scanned[chip, rows:]
    levels, between, top = chip_levels(core, mine, other, depth)
    mu = tables.mu()
    forward = [work[0] + tables.phi(0) * levels[0]]
    for i in range(1, count):
        forward.append(mu * forward[-1] + tables.phi(i) * levels[i])
    backward = [work[1] - tables.psi(count) * top]
    for i in reversed(range(1, count)):
        backward.append(tables.psi(i) * levels[i] + mu * backward[-1])
    backward.reverse()
    flux = [
        tables.flux_low(i) * forward[i] - tables.flux_high(i + 1) * backward[i]
        for i in range(count)
    ]
    under = tables.entry() * work[0] - tables.flux_high(0) * (
        tables.psi(0) * levels[0] + mu * backward[0]
    )
    pressure = [
        -tables.scale() * (tables.psi(i) * forward[i] + mu * tables.phi(i) * backward[i])
        for i in (0, depth)
    ]
    low = [pressure[0], *flux[:depth], under]
    high = [pressure[1], *flux[depth:], flux[depth - 1] - between]
    is_low = core == 0
    for i in range(own.shape[0]):
        own[i] = jnp.where(is_low, low[i], high[i])
        partner[i] = jnp.where(is_low, high[i], low[i])


def physical_half(fields, half, ghosts, from_x, from_y, from_slope_x, from_slope_y, slots):
    depth = fields.shape[0] - (2 if ghosts else 1)
    level = fields[0]
    pressures = [level - fields[depth + 1]] if ghosts else []
    for z in range(depth):
        pressures.append(level)
        level = level + fields[1 + z]
    if ghosts:
        pressures.append(level)
    for i, block in enumerate(pressures):
        slots[2 * i] = from_left(from_slope_x[half], from_right(block, from_y))
        slots[2 * i + 1] = from_left(from_x[half], from_right(block, from_slope_y))
    for i in range(fields.shape[0] - 1):
        block = from_right(fields[1 + i], from_y)
        slots[2 * len(pressures) + i] = from_left(from_x[half], block)


def own_half_kernel(flags, mine, from_x, from_y, from_slope_x, from_slope_y, slots, *, ghosts):
    physical_half(mine, flags[1], ghosts, from_x, from_y, from_slope_x, from_slope_y, slots)


def unfolded(core, mine, other, i):
    sign = (1 - 2 * core).astype(full_type)
    return mine[i] + other[i], sign * (mine[i] - other[i])


def fringe_kernel(
    flags, index, mine, other, middle, rows_x, rows_slope_x, from_y, from_slope_y,
    columns, columns_low, columns_high,
):
    core = flags[1]
    depth = middle.shape[1]
    count = rows_x.shape[2]
    slopes = [0.0] * depth
    plains = [0.0] * depth
    lifts = [0.0] * depth
    for half in range(2):
        fields = [jnp.where(core == half, mine[i], other[i]) for i in range(1 + depth)]
        single = jnp.concatenate([rows_x[half, 0], rows_x[half, 1]])
        both = jnp.concatenate([rows_slope_x[half, 0], single, rows_slope_x[half, 1]])
        level = fields[0]
        for z in range(depth):
            high, low = halves(level)
            by_high = product(both, high)
            by_low = product(both[: 2 * count], low)
            slopes[z] += by_high[:count] + by_high[3 * count :] + by_low[:count]
            plains[z] += by_high[count : 2 * count] + by_high[2 * count : 3 * count]
            plains[z] += by_low[count:]
            high, low = halves(fields[1 + z])
            by_high = product(single, high)
            lifts[z] += by_high[:count] + by_high[count:] + product(single[:count], low)
            level = level + fields[1 + z]
    through = from_right(jnp.concatenate(slopes + lifts), from_y)
    across = from_right(jnp.concatenate(plains), from_slope_y)
    for z in range(depth):
        columns[0, z] = through[z * count : (z + 1) * count]
        columns[1, z] = across[z * count : (z + 1) * count]
        columns[2, z] = through[(depth + z) * count : (depth + z + 1) * count]

    def one(i, carry):
        row = pl.ds(index[i], 1)
        here = pl.ds(i, 1)
        for c in range(3):
            for z in range(depth):
                value = middle[c, z, row, :] - columns[c, z, here, :]
                columns[c, z, here, :] = value
                if z == depth - 1:
                    columns_low[c, here, :] = value
                if z == 0:
                    columns_high[c, here, :] = value
        return carry

    lax.fori_loop(0, index.shape[0], one, 0, unroll=8)


def corrected_kernel(
    flags, slots, fields, middle, from_x, from_y, from_slope_x, from_slope_y,
    out, low_change, high_change,
    others,
):
    core = flags[1]
    depth = middle.shape[1]
    mid = middle.shape[2] // 2
    physical_half(
        fields, 1 - core, True, from_x, from_y, from_slope_x, from_slope_y, others
    )
    pressures = depth + 2
    sides = (slice(0, mid), slice(mid, 2 * mid))
    for z in range(depth):
        for c in range(3):
            slot = 2 * (1 + z) + c if c < 2 else 2 * pressures + z
            for side, change in zip(sides, unfolded(core, slots, others, slot)):
                out[c, z, side] = middle[c, z, side] - change
    for c in range(3):
        slot = c if c < 2 else 2 * pressures + depth
        for side, change in zip(sides, unfolded(core, slots, others, slot)):
            low_change[c, side] = change
    for c in range(2):
        slot = 2 * (depth + 1) + c
        for side, change in zip(sides, unfolded(core, slots, others, slot)):
            high_change[c, side] = change


def ghost_levels(
    flags, out, low_change, high_change, from_below, from_above, slope_x, slope_y,
    low, high,
):
    is_floor, is_lid = flags[2], flags[3]
    depth = out.shape[1]
    mid = out.shape[2] // 2
    open_low = (1 - is_floor).astype(full_type)
    open_high = (1 - is_lid).astype(full_type)
    for c in range(2):
        low[c] = open_low * (from_below[c] - low_change[c])
        high[c] = open_high * (from_above[c] - high_change[c])
    low[2] = -open_low * low_change[2]
    even, odd = (
        0.5 * from_left(slope_x[half], folded(high[0], 1.0 - 2.0 * half)) for half in range(2)
    )
    sides = (slice(0, mid), slice(mid, 2 * mid))
    for side, change in zip(sides, (even + odd, even - odd)):
        spread = change + from_right(high[1, side], slope_y)
        high[2, side] = open_high * (out[2, depth - 1, side] - spread)


def last_kernel(
    flags, slots, fields, final, from_x, from_y, from_slope_x, from_slope_y,
    out,
    others,
):
    core = flags[1]
    depth = final.shape[1]
    mid = final.shape[2] // 2
    physical_half(
        fields, 1 - core, False, from_x, from_y, from_slope_x, from_slope_y, others
    )
    sides = (slice(0, mid), slice(mid, 2 * mid))
    for z in range(depth):
        for c in range(3):
            slot = 2 * z + c if c < 2 else 2 * depth + z
            for side, change in zip(sides, unfolded(core, slots, others, slot)):
                out[c, z, side] = final[c, z, side] - change


def coefficients(decay, first_level, count, height):
    def gap(steps):
        return -jnp.expm1(-steps * decay)

    still = decay == 0.0
    below = jnp.arange(count + 1, dtype=full_type)[:, None, None] + first_level
    mu = jnp.exp(-decay)
    safe = jnp.where(still, 1.0, gap(2.0 * height))

    def ratio(steps):
        return jnp.where(still, steps / height, gap(2.0 * steps) / safe)

    share = 1.0 / (1.0 + mu)
    phi = 1.0 + jnp.exp(-(2.0 * below + 1.0) * decay)
    psi = 1.0 + jnp.exp(-(2.0 * (height - below) - 1.0) * decay)
    flux_low = mu * share * ratio(height - 1.0 - below[:count])
    flux_high = mu * share * ratio(below)
    entry = share * ratio(height - below[:1])
    scale = jnp.where(still, 0.0, mu / (jnp.where(still, 1.0, gap(2.0)) * safe))
    return jnp.concatenate([mu[None], phi, psi, flux_low, flux_high, entry, scale[None]])


def local(velocity, eddy_viscosity, turbine_mask, fringe_columns):
    current = velocity[0]
    viscosity = eddy_viscosity[0]
    _, depth, length_x, length_y = current.shape
    mid = length_x // 2
    fringe = fringe_columns.shape[0]
    chips = lax.axis_size("chip")
    devices = 2 * chips
    height = devices * depth
    count = 2 * depth
    rows = mid // chips
    section = lax.axis_index("sec")
    chip = lax.axis_index("chip")
    core = lax.axis_index("core")
    place = 2 * chip + core
    is_farm = section == 1
    flags = jnp.stack([is_farm, core, place == 0, place == devices - 1]).astype(jnp.int32)
    tables = {name: jnp.asarray(table) for name, table in build_tables(length_x, length_y).items()}

    upward_route = [(i, i + 1) for i in range(devices - 1)]
    downward_route = [(i + 1, i) for i in range(devices - 1)]
    swap = [(0, 1), (1, 0)]

    def across(shift):
        return [
            (i, devices + i + shift) for i in range(devices) if 0 <= i + shift < devices
        ]

    state_shape = (3, depth + 2, length_x, length_y)
    own_shape = shaped(3, depth, length_x, length_y)
    edge = shaped(2, length_x, length_y)
    whole_edge = shaped(3, length_x, length_y)
    band = shaped(3, fringe, length_y)
    bands = (shaped(3, depth, fringe, length_y), band, band)
    decay = lax.dynamic_index_in_dim(tables["decay"], core, 0, keepdims=False)
    stacked = coefficients(decay, (chip * count).astype(full_type), count, float(height))
    ratio = jnp.exp(-float(count) * lax.dynamic_slice_in_dim(decay, chip * rows, rows, 0))

    low, high = call(edges_kernel, (whole_edge, whole_edge), [vmem()], [], 0, (current,))
    low, high, held = lax.optimization_barrier((low, high, current))
    low = lax.ppermute(low, levels_axis, upward_route)
    high = lax.ppermute(high, levels_axis, downward_route)
    farm_downward = [(devices + i + 1, devices + i) for i in range(devices - 1)]

    held, stacked = lax.optimization_barrier((held, stacked))
    taken = [*call(columns_kernel, bands, [smem(), vmem()], [], 0, (fringe_columns, held))]
    columns = lax.ppermute(taken[0], every_axis, across(0))
    away = jnp.where(fringe_columns < mid, 1.0, -1.0)[:, None]
    signs = jnp.stack([jnp.ones_like(away), away])[:, None].astype(half_type)
    rows_x, rows_slope_x = (
        jnp.take(tables[name], fringe_columns % mid, axis=2) * signs
        for name in ("from_x", "from_slope_x")
    )

    rows_x, taken[1] = lax.optimization_barrier((rows_x, taken[1]))
    columns_low = lax.ppermute(taken[1], every_axis, across(1))
    columns_high = lax.ppermute(columns[:, 0], every_axis, farm_downward)
    block = length_x * length_y * 2
    spectrum = shaped(depth + 1, mid, length_y)
    message = shaped(chips, 2 * rows, length_y)
    tendency_tables = [tables["dealias_x"], tables["dealias_y"]]
    source_tables = [tables[n] for n in ("slope_x", "slope_y", "into_x", "into_y")]
    pressure_tables = [tables[n] for n in ("from_x", "from_y", "from_slope_x", "from_slope_y")]

    packed = pltpu.VMEM(message.shape, full_type)
    halved = pltpu.VMEM((2, mid, length_y), full_type)

    def solve(mine, other, fields, beside=()):
        (sums,) = call(
            gather_kernel, (message,), [smem(), vmem(), vmem(), vmem()],
            [halved, packed, pltpu.SemaphoreType.DMA((1,))], 8 * count * block,
            (flags, mine, other, stacked), (hbm(),),
        )
        sums = lax.all_to_all(sums, "chip", split_axis=0, concat_axis=0, tiled=True)
        (sums,) = call(
            scan_kernel, (message,), [hbm(), vmem()],
            [packed, packed, pltpu.SemaphoreType.DMA((2,))], 4 * block, (sums, ratio), (hbm(),),
        )
        if beside:
            upward, from_above = beside
            sums, from_above = lax.optimization_barrier((sums, from_above))
            beside = (upward, from_above)
        sums = lax.all_to_all(sums, "chip", split_axis=0, concat_axis=0, tiled=True)
        solved = shaped(fields, mid, length_y)
        own, partner = call(
            solve_kernel, (solved, solved), [smem()] + [vmem()] * 3 + [hbm()],
            [halved, packed, pltpu.SemaphoreType.DMA((1,))], 16 * count * block,
            (flags, mine, other, stacked, sums),
        )
        own, *beside = lax.optimization_barrier((own, *beside))
        partner = lax.ppermute(partner, "core", swap)
        ghosts = bool(beside)
        half_fields = 3 * depth + (5 if ghosts else 0)
        (slots,) = call(
            functools.partial(own_half_kernel, ghosts=ghosts),
            (shaped(half_fields, mid, length_y),), [smem()] + [vmem()] * 5, [],
            3 * half_fields * block * (length_x // 2 + length_y) // 2,
            (flags, own, *pressure_tables),
        )
        return own, partner, slots, *beside

    rounded = pltpu.VMEM((3, depth, length_x, length_y), half_type)
    state = pltpu.VMEM(state_shape, full_type)
    tendency_flops = 3 * depth * block * (length_x + length_y)
    source_flops = 3 * depth * block * (length_x + 2 * length_y)

    def inner(state, columns, earlier):
        kept = () if earlier else (own_shape,)
        return call(
            inner_kernel,
            (own_shape, edge, *kept),
            [smem(), smem()] + [vmem()] * (6 + len(earlier)),
            ([pltpu.VMEM(own_shape.shape, full_type)] if earlier else []) + [rounded],
            tendency_flops,
            (flags, fringe_columns, state, columns, viscosity, turbine_mask, *tendency_tables,
             *earlier),
        )

    partial, weights, start = inner(current, columns, ())
    partial, stacked, ratio, rows_x, rows_slope_x = lax.optimization_barrier(
        (partial, stacked, ratio, rows_x, rows_slope_x)
    )

    def spectra(partial, weights, low, high, columns_low, columns_high, more=()):
        middle, theirs, *downward = call(
            second_outer_kernel if more else outer_kernel,
            (own_shape, spectrum) if more else (own_shape, spectrum, edge),
            [smem(), smem()] + [vmem()] * (10 + len(more)),
            [pltpu.VMEM(whole_edge.shape, full_type)] * 2 if more else [],
            source_flops // 2,
            (flags, fringe_columns, partial, weights, low, high, columns_low, columns_high,
             *source_tables, *more),
        )
        other = lax.ppermute(theirs, "core", swap)
        mine, *upward = call(
            own_spectra_kernel,
            (spectrum,) if more else (spectrum, edge),
            [smem()] + [vmem()] * 5,
            [],
            source_flops // 2,
            (flags, middle, *source_tables),
        )
        return middle, mine, other, *upward, *downward

    middle, mine, other, upward, downward = spectra(
        partial, weights, low, high, columns_low, columns_high
    )
    from_above = lax.ppermute(downward, levels_axis, downward_route)
    own, partner, slots, upward, from_above = solve(mine, other, depth + 2, (upward, from_above))
    from_below = lax.ppermute(upward, levels_axis, upward_route)
    taken = call(
        fringe_kernel, bands, [smem(), smem()] + [vmem()] * 7, [],
        9 * depth * block * (length_x + length_y) // 8,
        (flags, fringe_columns, own, partner, middle, rows_x, rows_slope_x,
         tables["from_y"], tables["from_slope_y"]),
    )
    partner, *taken = lax.optimization_barrier((partner, *taken))
    new_columns = lax.ppermute(taken[0], every_axis, across(0))
    new_columns_low = lax.ppermute(taken[1], every_axis, across(1))
    new_columns_high = lax.ppermute(taken[2], every_axis, across(-1))
    half_fields = 3 * depth + 5
    corrected, low_change, high_change = call(
        corrected_kernel,
        (own_shape, whole_edge, edge),
        [smem()] + [vmem()] * 7,
        [pltpu.VMEM((half_fields, mid, length_y), full_type)],
        3 * half_fields * block * (length_x // 2 + length_y) // 2,
        (flags, slots, partner, middle, *pressure_tables),
    )
    new_columns, corrected = lax.optimization_barrier((new_columns, corrected))
    partial, weights = inner(corrected, new_columns, (start,))
    partial, from_below, from_above = lax.optimization_barrier((partial, from_below, from_above))
    final, mine, other = spectra(
        partial, weights, low_change, high_change, new_columns_low, new_columns_high,
        (corrected, from_below, from_above),
    )
    _, partner, slots = solve(mine, other, depth + 1)
    half_fields = 3 * depth
    (new,) = call(
        last_kernel,
        (own_shape,),
        [smem()] + [vmem()] * 7,
        [pltpu.VMEM((half_fields, mid, length_y), full_type)],
        3 * half_fields * block * (length_x // 2 + length_y) // 2,
        (flags, slots, partner, final, *pressure_tables),
    )
    return new[None]


def solution(mesh):
    sections, devices = mesh.devices.shape
    fine = Mesh(mesh.devices.reshape(sections, devices // 2, 2), every_axis)
    placed = (
        P("sec", None, levels_axis, None, None),
        P("sec", levels_axis, None, None),
        P(levels_axis, None, None),
        P(),
    )
    return jax.shard_map(
        local,
        mesh=fine,
        in_specs=placed,
        out_specs=P("sec", None, levels_axis, None, None),
        check_vma=False,
    )
```

```python
import functools
import math

import jax
import jax.numpy as jnp
import ml_dtypes
import numpy as np
from jax import lax
from jax.experimental import pallas as pl
from jax.experimental.pallas import tpu as pltpu
from jax.sharding import Mesh
from jax.sharding import PartitionSpec as P

step_size = 0.1
drag_coef = 0.75
cell_width = 4.0
half_type = jnp.bfloat16
full_type = jnp.float32
vmem_bytes = 26 * 1024 * 1024
levels_axis = ("chip", "core")
every_axis = ("sec", "chip", "core")


def derivative_table(length, cutoff):
    offset = np.arange(length)
    wavenumber = np.arange(1, cutoff + 1)
    phases = offset[:, None] * wavenumber[None, :] % length
    waves = np.sin(2.0 * math.pi / length * phases)
    first = -(2.0 / (cell_width * length)) * (waves @ (2.0 * math.pi / length * wavenumber))
    return first[(offset[:, None] - offset[None, :]) % length]


def real_basis(length):
    midpoint = length // 2
    row = np.arange(length)
    wavenumber = np.where(row <= midpoint, row, row - midpoint)
    angles = 2.0 * math.pi / length * (wavenumber[:, None] * row[None, :] % length)
    scales = np.where((row == 0) | (row == midpoint), math.sqrt(1.0 / length), math.sqrt(2.0 / length))
    return scales[:, None] * np.where((row <= midpoint)[:, None], np.cos(angles), np.sin(angles))


def wave_square(length):
    midpoint = length // 2
    row = np.arange(length)
    wavenumber = np.where(row < midpoint, row, np.where(row == midpoint, 0, row - midpoint))
    return (2.0 * math.pi / (length * cell_width) * wavenumber) ** 2


def high_low(table):
    table = np.asarray(table, np.float32)
    high = table.astype(ml_dtypes.bfloat16)
    low = (table - high.astype(np.float32)).astype(ml_dtypes.bfloat16)
    return np.stack([high, low], axis=-3)


def build_tables(length_x, length_y):
    mid = length_x // 2
    full_x = derivative_table(length_x, length_x // 2 - 1)
    full_y = derivative_table(length_y, length_y // 2 - 1)
    basis_x = real_basis(length_x)
    basis_y = real_basis(length_y)
    left_part, right_part = full_x[:mid, :mid], full_x[:mid, mid:]
    derived = full_x @ basis_x.T
    squares = wave_square(length_x)[:, None] + wave_square(length_y)[None, :]
    decay = 2.0 * np.arcsinh(0.5 * np.sqrt(squares))
    return {
        "dealias_x": derivative_table(length_x, (length_x - 1) // 3).astype(ml_dtypes.bfloat16),
        "dealias_y": derivative_table(length_y, (length_y - 1) // 3).T.astype(ml_dtypes.bfloat16),
        "slope_x": high_low(np.stack([left_part + right_part, left_part - right_part])),
        "slope_y": high_low(full_y.T),
        "into_x": high_low(np.stack([basis_x[0::2, :mid], basis_x[1::2, :mid]])),
        "into_y": high_low(basis_y.T),
        "from_x": high_low(np.stack([basis_x[0::2, :mid].T, basis_x[1::2, :mid].T])),
        "from_y": high_low(basis_y),
        "from_slope_x": high_low(np.stack([derived[:mid, 0::2], derived[:mid, 1::2]])),
        "from_slope_y": high_low(basis_y @ full_y.T),
        "decay": np.stack([decay[0::2], decay[1::2]]).astype(np.float32),
    }


def product(one, other):
    return jnp.dot(one, other, preferred_element_type=full_type)


def halves(block):
    high = block.astype(half_type)
    return high, (block - high.astype(full_type)).astype(half_type)


def from_left(table, block):
    high, low = halves(block)
    return product(table[0], high) + product(table[0], low) + product(table[1], high)


def from_right(block, table):
    high, low = halves(block)
    return product(high, table[0]) + product(low, table[0]) + product(high, table[1])


def vmem():
    return pl.BlockSpec(memory_space=pltpu.VMEM)


def smem():
    return pl.BlockSpec(memory_space=pltpu.SMEM)


def hbm():
    return pl.BlockSpec(memory_space=pltpu.HBM)


def call(kernel, outs, in_specs, scratch, flops, args, out_specs=None):
    moved = sum(math.prod(a.shape) * 4 for a in (*outs, *args))
    return pl.pallas_call(
        kernel,
        out_shape=outs,
        in_specs=in_specs,
        out_specs=out_specs or tuple(vmem() for _ in outs),
        scratch_shapes=scratch,
        compiler_params=pltpu.CompilerParams(vmem_limit_bytes=vmem_bytes),
        cost_estimate=pl.CostEstimate(flops=int(flops), bytes_accessed=moved, transcendentals=0),
    )(*args)


def shaped(*dims, kind=full_type):
    return jax.ShapeDtypeStruct(dims, kind)


def tendency_steps(state, rounded, viscosity, mask, drag, dealias_x, dealias_y, put):
    depth = state.shape[1]
    length_x = state.shape[2]
    rows = length_x // 2
    for z in range(depth):
        for c in range(3):
            rounded[c, z] = state[c, z].astype(half_type)
    for z in range(depth):
        for b in range(length_x // rows):
            part = pl.ds(b * rows, rows)
            u, v, w = (state[c, z, part, :] for c in range(3))
            slow = drag * mask[z, part, :].astype(full_type) * jnp.abs(u)
            nu = viscosity[z, part, :]
            still = 2.0 * nu + slow
            rising = nu - 0.5 * w if z < depth - 1 else None
            sinking = nu + 0.5 * w if z > 0 else None
            for c in range(3):
                center = state[c, z, part, :]
                grad_x = product(dealias_x[part, :], rounded[c, z])
                grad_y = product(rounded[c, z, part, :], dealias_y[...])
                change = -(u * grad_x + v * grad_y + still * center)
                if rising is not None:
                    change += rising * state[c, z + 1, part, :]
                if sinking is not None:
                    change += sinking * state[c, z - 1, part, :]
                put(c, z, part, center, change)


def folded(block, sign):
    mid = block.shape[0] // 2
    return block[:mid] + sign * block[mid:]


def source_spectra(state, out, half, slope_x, slope_y, into_x, into_y):
    depth = state.shape[1]
    sign = (1 - 2 * half).astype(full_type)
    slope, into = slope_x[half], into_x[half]
    lifted = [folded(state[2, z], sign) for z in range(depth)]
    sources = []
    for z in range(depth):
        spread = from_left(slope, folded(state[0, z], sign))
        spread += from_right(folded(state[1, z], sign), slope_y)
        sources.append(spread + lifted[z] - (lifted[z - 1] if z else 0.0))
    sources.append(lifted[depth - 1])
    for z, source in enumerate(sources):
        out[z] = from_right(from_left(into, source), into_y)


def edges_kernel(velocity, low, high):
    depth = velocity.shape[1]
    low[...] = velocity[:, depth - 1]
    high[...] = velocity[:, 0]


def columns_kernel(index, velocity, columns, columns_low, columns_high):
    depth = velocity.shape[1]

    def one(i, carry):
        row = pl.ds(index[i], 1)
        here = pl.ds(i, 1)
        for c in range(3):
            for z in range(depth):
                taken = velocity[c, z, row, :]
                columns[c, z, here, :] = taken
                if z == depth - 1:
                    columns_low[c, here, :] = taken
                if z == 0:
                    columns_high[c, here, :] = taken
        return carry

    lax.fori_loop(0, index.shape[0], one, 0, unroll=8)


def insert_rows(index, pairs):
    def one(i, carry):
        row = pl.ds(index[i], 1)
        for target, rows in pairs:
            for c in range(3):
                target[c, row, :] = rows[c, pl.ds(i, 1), :]
        return carry

    lax.fori_loop(0, index.shape[0], one, 0, unroll=8)


def inner_kernel(flags, index, given, columns, viscosity, mask, dealias_x, dealias_y, *refs):
    depth = given.shape[1]
    earlier = refs[0] if len(refs) == 5 else None
    partial, weights, state, rounded = refs[-4:]
    is_farm = flags[0]
    state[...] = given[...]

    @pl.when(is_farm == 1)
    def _():
        insert_rows(index, [(state.at[:, z], columns.at[:, z]) for z in range(depth)])

    drag = drag_coef * is_farm.astype(full_type)
    share = 1.0 if earlier is None else 0.5

    def put(c, z, part, center, change):
        moved = center + step_size * change
        if earlier is not None:
            moved = 0.5 * (earlier[c, z, part, :] + moved)
        partial[c, z, part, :] = moved

    tendency_steps(state, rounded, viscosity, mask, drag, dealias_x, dealias_y, put)
    weights[0] = share * step_size * (viscosity[0] + 0.5 * state[2, 0])
    weights[1] = share * step_size * (viscosity[depth - 1] - 0.5 * state[2, depth - 1])


def add_ghosts(
    flags, index, partial, weights, low, high, columns_low, columns_high, middle,
):
    depth = middle.shape[1]
    is_farm, is_lid = flags[0], flags[3]
    for c in range(3):
        for z in range(depth):
            moved = partial[c, z]
            if z == 0:
                moved += weights[0] * low[c]
            if z == depth - 1:
                moved += weights[1] * high[c]
                if c == 2:
                    moved = jnp.where(is_lid == 1, 0.0, moved)
            middle[c, z] = moved

    @pl.when(is_farm == 1)
    def _():
        def one(i, carry):
            row = pl.ds(index[i], 1)
            here = pl.ds(i, 1)
            for c in range(3):
                lag = columns_low[c, here, :] - low[c, row, :]
                middle[c, 0, row, :] += weights[0, row, :] * lag
                lag = columns_high[c, here, :] - high[c, row, :]
                middle[c, depth - 1, row, :] += weights[1, row, :] * lag
            return carry

        lax.fori_loop(0, index.shape[0], one, 0, unroll=8)


def outer_kernel(
    flags, index, partial, weights, low, high, columns_low, columns_high,
    slope_x, slope_y, into_x, into_y,
    middle, theirs, downward,
):
    add_ghosts(
        flags, index, partial, weights, low, high, columns_low, columns_high, middle
    )
    downward[0] = middle[0, 0]
    downward[1] = middle[1, 0]
    source_spectra(middle, theirs, 1 - flags[1], slope_x, slope_y, into_x, into_y)


def second_outer_kernel(
    flags, index, partial, weights, low_change, high_change, columns_low, columns_high,
    slope_x, slope_y, into_x, into_y, corrected, from_below, from_above,
    middle, theirs,
    low, high,
):
    ghost_levels(
        flags, corrected, low_change, high_change, from_below, from_above, slope_x, slope_y,
        low, high,
    )
    add_ghosts(
        flags, index, partial, weights, low, high, columns_low, columns_high, middle
    )
    source_spectra(middle, theirs, 1 - flags[1], slope_x, slope_y, into_x, into_y)


def own_spectra_kernel(flags, middle, slope_x, slope_y, into_x, into_y, mine, *edges):
    depth = middle.shape[1]
    mid = middle.shape[2] // 2
    source_spectra(middle, mine, flags[1], slope_x, slope_y, into_x, into_y)
    if not edges:
        return
    (upward,) = edges
    top = depth - 1
    even, odd = (
        0.5 * from_left(slope_x[half], folded(middle[2, top], 1.0 - 2.0 * half))
        for half in range(2)
    )
    upward[0, :mid] = middle[0, top, :mid] + (even + odd)
    upward[0, mid:] = middle[0, top, mid:] + (even - odd)
    upward[1] = middle[1, top] + from_right(middle[2, top], slope_y)


def chip_levels(core, mine, other, depth):
    is_low = core == 0
    low = [jnp.where(is_low, mine[i], other[i]) for i in range(depth + 1)]
    high = [jnp.where(is_low, other[i], mine[i]) for i in range(depth + 1)]
    levels = low[:depth] + [high[0] - low[depth]] + high[1:depth]
    return levels, low[depth], high[depth]


class Coefficients:
    def __init__(self, stacked, count):
        self.mu = lambda: stacked[0]
        self.phi = lambda i: stacked[1 + i]
        self.psi = lambda i: stacked[2 + count + i]
        self.flux_low = lambda i: stacked[3 + 2 * count + i]
        self.flux_high = lambda i: stacked[3 + 3 * count + i]
        self.entry = lambda: stacked[4 + 4 * count]
        self.scale = lambda: stacked[5 + 4 * count]


def gather_kernel(flags, mine, other, stacked, out, work, packed, sems):
    core = flags[1]
    depth = mine.shape[0] - 1
    count = 2 * depth
    tables = Coefficients(stacked, count)
    levels, _, top = chip_levels(core, mine, other, depth)
    mu = tables.mu()
    forward = tables.phi(0) * levels[0]
    for i in range(1, count):
        forward = mu * forward + tables.phi(i) * levels[i]
    work[0] = mu * forward - tables.phi(count) * top
    backward = -tables.psi(count) * top
    for i in reversed(range(count)):
        backward = tables.psi(i) * levels[i] + mu * backward
    work[1] = backward
    chips = out.shape[0]
    rows = out.shape[1] // 2
    for chip in range(chips):
        packed[chip, :rows] = work[0, chip * rows : (chip + 1) * rows]
        packed[chip, rows:] = work[1, chip * rows : (chip + 1) * rows]
    copy = pltpu.make_async_copy(packed, out, sems.at[0])
    copy.start()
    copy.wait()


def scan_kernel(received, ratio, out, taken, packed, sems):
    chips = received.shape[0]
    rows = received.shape[1] // 2
    copy = pltpu.make_async_copy(received, taken, sems.at[0])
    copy.start()
    factor = ratio[...]
    copy.wait()
    carried = jnp.zeros_like(factor)
    for chip in range(chips):
        packed[chip, :rows] = carried
        carried = factor * carried + taken[chip, :rows]
    carried = jnp.zeros_like(factor)
    for chip in reversed(range(chips)):
        packed[chip, rows:] = carried
        carried = factor * carried + taken[chip, rows:]
    copy = pltpu.make_async_copy(packed, out, sems.at[1])
    copy.start()
    copy.wait()


def solve_kernel(flags, mine, other, stacked, received, own, partner, work, scanned, sems):
    core = flags[1]
    depth = mine.shape[0] - 1
    count = 2 * depth
    tables = Coefficients(stacked, count)
    chips = scanned.shape[0]
    rows = scanned.shape[1] // 2
    copy = pltpu.make_async_copy(received, scanned, sems.at[0])
    copy.start()
    copy.wait()
    for chip in range(chips):
        work[0, chip * rows : (chip + 1) * rows] = scanned[chip, :rows]
        work[1, chip * rows : (chip + 1) * rows] = scanned[chip, rows:]
    levels, between, top = chip_levels(core, mine, other, depth)
    mu = tables.mu()
    forward = [work[0] + tables.phi(0) * levels[0]]
    for i in range(1, count):
        forward.append(mu * forward[-1] + tables.phi(i) * levels[i])
    backward = [work[1] - tables.psi(count) * top]
    for i in reversed(range(1, count)):
        backward.append(tables.psi(i) * levels[i] + mu * backward[-1])
    backward.reverse()
    flux = [
        tables.flux_low(i) * forward[i] - tables.flux_high(i + 1) * backward[i]
        for i in range(count)
    ]
    under = tables.entry() * work[0] - tables.flux_high(0) * (
        tables.psi(0) * levels[0] + mu * backward[0]
    )
    pressure = [
        -tables.scale() * (tables.psi(i) * forward[i] + mu * tables.phi(i) * backward[i])
        for i in (0, depth)
    ]
    low = [pressure[0], *flux[:depth], under]
    high = [pressure[1], *flux[depth:], flux[depth - 1] - between]
    is_low = core == 0
    for i in range(own.shape[0]):
        own[i] = jnp.where(is_low, low[i], high[i])
        partner[i] = jnp.where(is_low, high[i], low[i])


def physical_half(fields, half, ghosts, from_x, from_y, from_slope_x, from_slope_y, slots):
    depth = fields.shape[0] - (2 if ghosts else 1)
    level = fields[0]
    pressures = [level - fields[depth + 1]] if ghosts else []
    for z in range(depth):
        pressures.append(level)
        level = level + fields[1 + z]
    if ghosts:
        pressures.append(level)
    for i, block in enumerate(pressures):
        slots[2 * i] = from_left(from_slope_x[half], from_right(block, from_y))
        slots[2 * i + 1] = from_left(from_x[half], from_right(block, from_slope_y))
    for i in range(fields.shape[0] - 1):
        block = from_right(fields[1 + i], from_y)
        slots[2 * len(pressures) + i] = from_left(from_x[half], block)


def own_half_kernel(flags, mine, from_x, from_y, from_slope_x, from_slope_y, slots, *, ghosts):
    physical_half(mine, flags[1], ghosts, from_x, from_y, from_slope_x, from_slope_y, slots)


def unfolded(core, mine, other, i):
    sign = (1 - 2 * core).astype(full_type)
    return mine[i] + other[i], sign * (mine[i] - other[i])


def fringe_kernel(
    flags, index, mine, other, middle, rows_x, rows_slope_x, from_y, from_slope_y,
    columns, columns_low, columns_high,
):
    core = flags[1]
    depth = middle.shape[1]
    count = rows_x.shape[2]
    slopes = [0.0] * depth
    plains = [0.0] * depth
    lifts = [0.0] * depth
    for half in range(2):
        fields = [jnp.where(core == half, mine[i], other[i]) for i in range(1 + depth)]
        single = jnp.concatenate([rows_x[half, 0], rows_x[half, 1]])
        both = jnp.concatenate([rows_slope_x[half, 0], single, rows_slope_x[half, 1]])
        level = fields[0]
        for z in range(depth):
            high, low = halves(level)
            by_high = product(both, high)
            by_low = product(both[: 2 * count], low)
            slopes[z] += by_high[:count] + by_high[3 * count :] + by_low[:count]
            plains[z] += by_high[count : 2 * count] + by_high[2 * count : 3 * count]
            plains[z] += by_low[count:]
            high, low = halves(fields[1 + z])
            by_high = product(single, high)
            lifts[z] += by_high[:count] + by_high[count:] + product(single[:count], low)
            level = level + fields[1 + z]
    through = from_right(jnp.concatenate(slopes + lifts), from_y)
    across = from_right(jnp.concatenate(plains), from_slope_y)
    for z in range(depth):
        columns[0, z] = through[z * count : (z + 1) * count]
        columns[1, z] = across[z * count : (z + 1) * count]
        columns[2, z] = through[(depth + z) * count : (depth + z + 1) * count]

    def one(i, carry):
        row = pl.ds(index[i], 1)
        here = pl.ds(i, 1)
        for c in range(3):
            for z in range(depth):
                value = middle[c, z, row, :] - columns[c, z, here, :]
                columns[c, z, here, :] = value
                if z == depth - 1:
                    columns_low[c, here, :] = value
                if z == 0:
                    columns_high[c, here, :] = value
        return carry

    lax.fori_loop(0, index.shape[0], one, 0, unroll=8)


def corrected_kernel(
    flags, slots, fields, middle, from_x, from_y, from_slope_x, from_slope_y,
    out, low_change, high_change,
    others,
):
    core = flags[1]
    depth = middle.shape[1]
    mid = middle.shape[2] // 2
    physical_half(
        fields, 1 - core, True, from_x, from_y, from_slope_x, from_slope_y, others
    )
    pressures = depth + 2
    sides = (slice(0, mid), slice(mid, 2 * mid))
    for z in range(depth):
        for c in range(3):
            slot = 2 * (1 + z) + c if c < 2 else 2 * pressures + z
            for side, change in zip(sides, unfolded(core, slots, others, slot)):
                out[c, z, side] = middle[c, z, side] - change
    for c in range(3):
        slot = c if c < 2 else 2 * pressures + depth
        for side, change in zip(sides, unfolded(core, slots, others, slot)):
            low_change[c, side] = change
    for c in range(2):
        slot = 2 * (depth + 1) + c
        for side, change in zip(sides, unfolded(core, slots, others, slot)):
            high_change[c, side] = change


def ghost_levels(
    flags, out, low_change, high_change, from_below, from_above, slope_x, slope_y,
    low, high,
):
    is_floor, is_lid = flags[2], flags[3]
    depth = out.shape[1]
    mid = out.shape[2] // 2
    open_low = (1 - is_floor).astype(full_type)
    open_high = (1 - is_lid).astype(full_type)
    for c in range(2):
        low[c] = open_low * (from_below[c] - low_change[c])
        high[c] = open_high * (from_above[c] - high_change[c])
    low[2] = -open_low * low_change[2]
    even, odd = (
        0.5 * from_left(slope_x[half], folded(high[0], 1.0 - 2.0 * half)) for half in range(2)
    )
    sides = (slice(0, mid), slice(mid, 2 * mid))
    for side, change in zip(sides, (even + odd, even - odd)):
        spread = change + from_right(high[1, side], slope_y)
        high[2, side] = open_high * (out[2, depth - 1, side] - spread)


def last_kernel(
    flags, slots, fields, final, from_x, from_y, from_slope_x, from_slope_y,
    out,
    held, sems,
):
    core = flags[1]
    depth = final.shape[1]
    mid = final.shape[2] // 2
    half = 1 - core
    sign = (1 - 2 * core).astype(full_type)
    level = fields[0]
    copies = []
    for z in range(depth):
        lift = fields[1 + z]
        for c, (block, left, right) in enumerate(
            ((level, from_slope_x, from_y), (level, from_x, from_slope_y), (lift, from_x, from_y))
        ):
            other = from_left(left[half], from_right(block, right))
            mine = slots[2 * z + c if c < 2 else 2 * depth + z]
            held[c, z, :mid] = final[c, z, :mid] - (mine + other)
            held[c, z, mid:] = final[c, z, mid:] - sign * (mine - other)
            copy = pltpu.make_async_copy(held.at[c, z], out.at[c, z], sems.at[3 * z + c])
            copy.start()
            copies.append(copy)
        level = level + lift
    for copy in copies:
        copy.wait()


def coefficients(decay, first_level, count, height):
    def gap(steps):
        return -jnp.expm1(-steps * decay)

    still = decay == 0.0
    below = jnp.arange(count + 1, dtype=full_type)[:, None, None] + first_level
    mu = jnp.exp(-decay)
    safe = jnp.where(still, 1.0, gap(2.0 * height))

    def ratio(steps):
        return jnp.where(still, steps / height, gap(2.0 * steps) / safe)

    share = 1.0 / (1.0 + mu)
    phi = 1.0 + jnp.exp(-(2.0 * below + 1.0) * decay)
    psi = 1.0 + jnp.exp(-(2.0 * (height - below) - 1.0) * decay)
    flux_low = mu * share * ratio(height - 1.0 - below[:count])
    flux_high = mu * share * ratio(below)
    entry = share * ratio(height - below[:1])
    scale = jnp.where(still, 0.0, mu / (jnp.where(still, 1.0, gap(2.0)) * safe))
    return jnp.concatenate([mu[None], phi, psi, flux_low, flux_high, entry, scale[None]])


def local(velocity, eddy_viscosity, turbine_mask, fringe_columns):
    current = velocity[0]
    viscosity = eddy_viscosity[0]
    _, depth, length_x, length_y = current.shape
    mid = length_x // 2
    fringe = fringe_columns.shape[0]
    chips = lax.axis_size("chip")
    devices = 2 * chips
    height = devices * depth
    count = 2 * depth
    rows = mid // chips
    section = lax.axis_index("sec")
    chip = lax.axis_index("chip")
    core = lax.axis_index("core")
    place = 2 * chip + core
    is_farm = section == 1
    flags = jnp.stack([is_farm, core, place == 0, place == devices - 1]).astype(jnp.int32)
    tables = {name: jnp.asarray(table) for name, table in build_tables(length_x, length_y).items()}

    upward_route = [(i, i + 1) for i in range(devices - 1)]
    downward_route = [(i + 1, i) for i in range(devices - 1)]
    swap = [(0, 1), (1, 0)]

    def across(shift):
        return [
            (i, devices + i + shift) for i in range(devices) if 0 <= i + shift < devices
        ]

    state_shape = (3, depth + 2, length_x, length_y)
    own_shape = shaped(3, depth, length_x, length_y)
    edge = shaped(2, length_x, length_y)
    whole_edge = shaped(3, length_x, length_y)
    band = shaped(3, fringe, length_y)
    bands = (shaped(3, depth, fringe, length_y), band, band)
    decay = lax.dynamic_index_in_dim(tables["decay"], core, 0, keepdims=False)
    stacked = coefficients(decay, (chip * count).astype(full_type), count, float(height))
    ratio = jnp.exp(-float(count) * lax.dynamic_slice_in_dim(decay, chip * rows, rows, 0))

    low, high = call(edges_kernel, (whole_edge, whole_edge), [vmem()], [], 0, (current,))
    low, high, held = lax.optimization_barrier((low, high, current))
    low = lax.ppermute(low, levels_axis, upward_route)
    high = lax.ppermute(high, levels_axis, downward_route)
    farm_downward = [(devices + i + 1, devices + i) for i in range(devices - 1)]

    held, stacked = lax.optimization_barrier((held, stacked))
    taken = [*call(columns_kernel, bands, [smem(), vmem()], [], 0, (fringe_columns, held))]
    columns = lax.ppermute(taken[0], every_axis, across(0))
    away = jnp.where(fringe_columns < mid, 1.0, -1.0)[:, None]
    signs = jnp.stack([jnp.ones_like(away), away])[:, None].astype(half_type)
    rows_x, rows_slope_x = (
        jnp.take(tables[name], fringe_columns % mid, axis=2) * signs
        for name in ("from_x", "from_slope_x")
    )

    rows_x, taken[1] = lax.optimization_barrier((rows_x, taken[1]))
    columns_low = lax.ppermute(taken[1], every_axis, across(1))
    columns_high = lax.ppermute(columns[:, 0], every_axis, farm_downward)
    block = length_x * length_y * 2
    spectrum = shaped(depth + 1, mid, length_y)
    message = shaped(chips, 2 * rows, length_y)
    tendency_tables = [tables["dealias_x"], tables["dealias_y"]]
    source_tables = [tables[n] for n in ("slope_x", "slope_y", "into_x", "into_y")]
    pressure_tables = [tables[n] for n in ("from_x", "from_y", "from_slope_x", "from_slope_y")]

    packed = pltpu.VMEM(message.shape, full_type)
    halved = pltpu.VMEM((2, mid, length_y), full_type)

    def solve(mine, other, fields, beside=()):
        (sums,) = call(
            gather_kernel, (message,), [smem(), vmem(), vmem(), vmem()],
            [halved, packed, pltpu.SemaphoreType.DMA((1,))], 8 * count * block,
            (flags, mine, other, stacked), (hbm(),),
        )
        sums = lax.all_to_all(sums, "chip", split_axis=0, concat_axis=0, tiled=True)
        (sums,) = call(
            scan_kernel, (message,), [hbm(), vmem()],
            [packed, packed, pltpu.SemaphoreType.DMA((2,))], 4 * block, (sums, ratio), (hbm(),),
        )
        if beside:
            upward, from_above = beside
            sums, from_above = lax.optimization_barrier((sums, from_above))
            beside = (upward, from_above)
        sums = lax.all_to_all(sums, "chip", split_axis=0, concat_axis=0, tiled=True)
        solved = shaped(fields, mid, length_y)
        own, partner = call(
            solve_kernel, (solved, solved), [smem()] + [vmem()] * 3 + [hbm()],
            [halved, packed, pltpu.SemaphoreType.DMA((1,))], 16 * count * block,
            (flags, mine, other, stacked, sums),
        )
        own, *beside = lax.optimization_barrier((own, *beside))
        partner = lax.ppermute(partner, "core", swap)
        ghosts = bool(beside)
        half_fields = 3 * depth + (5 if ghosts else 0)
        (slots,) = call(
            functools.partial(own_half_kernel, ghosts=ghosts),
            (shaped(half_fields, mid, length_y),), [smem()] + [vmem()] * 5, [],
            3 * half_fields * block * (length_x // 2 + length_y) // 2,
            (flags, own, *pressure_tables),
        )
        return own, partner, slots, *beside

    rounded = pltpu.VMEM((3, depth, length_x, length_y), half_type)
    state = pltpu.VMEM(state_shape, full_type)
    tendency_flops = 3 * depth * block * (length_x + length_y)
    source_flops = 3 * depth * block * (length_x + 2 * length_y)

    def inner(state, columns, earlier):
        kept = () if earlier else (own_shape,)
        return call(
            inner_kernel,
            (own_shape, edge, *kept),
            [smem(), smem()] + [vmem()] * (6 + len(earlier)),
            ([pltpu.VMEM(own_shape.shape, full_type)] if earlier else []) + [rounded],
            tendency_flops,
            (flags, fringe_columns, state, columns, viscosity, turbine_mask, *tendency_tables,
             *earlier),
        )

    partial, weights, start = inner(current, columns, ())
    partial, stacked, ratio, rows_x, rows_slope_x = lax.optimization_barrier(
        (partial, stacked, ratio, rows_x, rows_slope_x)
    )

    def spectra(partial, weights, low, high, columns_low, columns_high, more=()):
        middle, theirs, *downward = call(
            second_outer_kernel if more else outer_kernel,
            (own_shape, spectrum) if more else (own_shape, spectrum, edge),
            [smem(), smem()] + [vmem()] * (10 + len(more)),
            [pltpu.VMEM(whole_edge.shape, full_type)] * 2 if more else [],
            source_flops // 2,
            (flags, fringe_columns, partial, weights, low, high, columns_low, columns_high,
             *source_tables, *more),
        )
        other = lax.ppermute(theirs, "core", swap)
        mine, *upward = call(
            own_spectra_kernel,
            (spectrum,) if more else (spectrum, edge),
            [smem()] + [vmem()] * 5,
            [],
            source_flops // 2,
            (flags, middle, *source_tables),
        )
        return middle, mine, other, *upward, *downward

    middle, mine, other, upward, downward = spectra(
        partial, weights, low, high, columns_low, columns_high
    )
    from_above = lax.ppermute(downward, levels_axis, downward_route)
    own, partner, slots, upward, from_above = solve(mine, other, depth + 2, (upward, from_above))
    from_below = lax.ppermute(upward, levels_axis, upward_route)
    taken = call(
        fringe_kernel, bands, [smem(), smem()] + [vmem()] * 7, [],
        9 * depth * block * (length_x + length_y) // 8,
        (flags, fringe_columns, own, partner, middle, rows_x, rows_slope_x,
         tables["from_y"], tables["from_slope_y"]),
    )
    partner, *taken = lax.optimization_barrier((partner, *taken))
    new_columns = lax.ppermute(taken[0], every_axis, across(0))
    new_columns_low = lax.ppermute(taken[1], every_axis, across(1))
    new_columns_high = lax.ppermute(taken[2], every_axis, across(-1))
    half_fields = 3 * depth + 5
    corrected, low_change, high_change = call(
        corrected_kernel,
        (own_shape, whole_edge, edge),
        [smem()] + [vmem()] * 7,
        [pltpu.VMEM((half_fields, mid, length_y), full_type)],
        3 * half_fields * block * (length_x // 2 + length_y) // 2,
        (flags, slots, partner, middle, *pressure_tables),
    )
    new_columns, corrected = lax.optimization_barrier((new_columns, corrected))
    partial, weights = inner(corrected, new_columns, (start,))
    partial, from_below, from_above = lax.optimization_barrier((partial, from_below, from_above))
    final, mine, other = spectra(
        partial, weights, low_change, high_change, new_columns_low, new_columns_high,
        (corrected, from_below, from_above),
    )
    _, partner, slots = solve(mine, other, depth + 1)
    half_fields = 3 * depth
    (new,) = call(
        last_kernel,
        (own_shape,),
        [smem()] + [vmem()] * 7,
        [pltpu.VMEM(own_shape.shape, full_type), pltpu.SemaphoreType.DMA((half_fields,))],
        3 * half_fields * block * (length_x // 2 + length_y) // 2,
        (flags, slots, partner, final, *pressure_tables),
        (hbm(),),
    )
    return new[None]


def solution(mesh):
    sections, devices = mesh.devices.shape
    fine = Mesh(mesh.devices.reshape(sections, devices // 2, 2), every_axis)
    placed = (
        P("sec", None, levels_axis, None, None),
        P("sec", levels_axis, None, None),
        P(levels_axis, None, None),
        P(),
    )
    return jax.shard_map(
        local,
        mesh=fine,
        in_specs=placed,
        out_specs=P("sec", None, levels_axis, None, None),
        check_vma=False,
    )
```

```python
import functools
import math

import jax
import jax.numpy as jnp
import ml_dtypes
import numpy as np
from jax import lax
from jax.experimental import pallas as pl
from jax.experimental.pallas import tpu as pltpu
from jax.sharding import Mesh
from jax.sharding import PartitionSpec as P

step_size = 0.1
drag_coef = 0.75
cell_width = 4.0
half_type = jnp.bfloat16
full_type = jnp.float32
vmem_bytes = 26 * 1024 * 1024
levels_axis = ("chip", "core")
every_axis = ("sec", "chip", "core")


def derivative_table(length, cutoff):
    offset = np.arange(length)
    wavenumber = np.arange(1, cutoff + 1)
    phases = offset[:, None] * wavenumber[None, :] % length
    waves = np.sin(2.0 * math.pi / length * phases)
    first = -(2.0 / (cell_width * length)) * (waves @ (2.0 * math.pi / length * wavenumber))
    return first[(offset[:, None] - offset[None, :]) % length]


def real_basis(length):
    midpoint = length // 2
    row = np.arange(length)
    wavenumber = np.where(row <= midpoint, row, row - midpoint)
    angles = 2.0 * math.pi / length * (wavenumber[:, None] * row[None, :] % length)
    scales = np.where((row == 0) | (row == midpoint), math.sqrt(1.0 / length), math.sqrt(2.0 / length))
    return scales[:, None] * np.where((row <= midpoint)[:, None], np.cos(angles), np.sin(angles))


def wave_square(length):
    midpoint = length // 2
    row = np.arange(length)
    wavenumber = np.where(row < midpoint, row, np.where(row == midpoint, 0, row - midpoint))
    return (2.0 * math.pi / (length * cell_width) * wavenumber) ** 2


def high_low(table):
    table = np.asarray(table, np.float32)
    high = table.astype(ml_dtypes.bfloat16)
    low = (table - high.astype(np.float32)).astype(ml_dtypes.bfloat16)
    return np.stack([high, low], axis=-3)


def build_tables(length_x, length_y):
    mid = length_x // 2
    full_x = derivative_table(length_x, length_x // 2 - 1)
    full_y = derivative_table(length_y, length_y // 2 - 1)
    basis_x = real_basis(length_x)
    basis_y = real_basis(length_y)
    left_part, right_part = full_x[:mid, :mid], full_x[:mid, mid:]
    derived = full_x @ basis_x.T
    squares = wave_square(length_x)[:, None] + wave_square(length_y)[None, :]
    decay = 2.0 * np.arcsinh(0.5 * np.sqrt(squares))
    return {
        "dealias_x": derivative_table(length_x, (length_x - 1) // 3).astype(ml_dtypes.bfloat16),
        "dealias_y": derivative_table(length_y, (length_y - 1) // 3).T.astype(ml_dtypes.bfloat16),
        "slope_x": high_low(np.stack([left_part + right_part, left_part - right_part])),
        "slope_y": high_low(full_y.T),
        "into_x": high_low(np.stack([basis_x[0::2, :mid], basis_x[1::2, :mid]])),
        "into_y": high_low(basis_y.T),
        "from_x": high_low(np.stack([basis_x[0::2, :mid].T, basis_x[1::2, :mid].T])),
        "from_y": high_low(basis_y),
        "from_slope_x": high_low(np.stack([derived[:mid, 0::2], derived[:mid, 1::2]])),
        "from_slope_y": high_low(basis_y @ full_y.T),
        "decay": np.stack([decay[0::2], decay[1::2]]).astype(np.float32),
    }


def product(one, other):
    return jnp.dot(one, other, preferred_element_type=full_type)


def halves(block):
    high = block.astype(half_type)
    return high, (block - high.astype(full_type)).astype(half_type)


def from_left(table, block):
    high, low = halves(block)
    return product(table[0], high) + product(table[0], low) + product(table[1], high)


def from_right(block, table):
    high, low = halves(block)
    return product(high, table[0]) + product(low, table[0]) + product(high, table[1])


def vmem():
    return pl.BlockSpec(memory_space=pltpu.VMEM)


def smem():
    return pl.BlockSpec(memory_space=pltpu.SMEM)


def hbm():
    return pl.BlockSpec(memory_space=pltpu.HBM)


def call(kernel, outs, in_specs, scratch, flops, args, out_specs=None):
    moved = sum(math.prod(a.shape) * 4 for a in (*outs, *args)) if flops else 0
    return pl.pallas_call(
        kernel,
        out_shape=outs,
        in_specs=in_specs,
        out_specs=out_specs or tuple(vmem() for _ in outs),
        scratch_shapes=scratch,
        compiler_params=pltpu.CompilerParams(vmem_limit_bytes=vmem_bytes),
        cost_estimate=pl.CostEstimate(flops=int(flops), bytes_accessed=moved, transcendentals=0),
    )(*args)


def shaped(*dims, kind=full_type):
    return jax.ShapeDtypeStruct(dims, kind)


def tendency_steps(state, rounded, viscosity, mask, drag, dealias_x, dealias_y, put):
    depth = state.shape[1]
    length_x = state.shape[2]
    rows = length_x // 2
    for z in range(depth):
        for c in range(3):
            rounded[c, z] = state[c, z].astype(half_type)
    for z in range(depth):
        for b in range(length_x // rows):
            part = pl.ds(b * rows, rows)
            u, v, w = (state[c, z, part, :] for c in range(3))
            slow = drag * mask[z, part, :].astype(full_type) * jnp.abs(u)
            nu = viscosity[z, part, :]
            still = 2.0 * nu + slow
            rising = nu - 0.5 * w if z < depth - 1 else None
            sinking = nu + 0.5 * w if z > 0 else None
            for c in range(3):
                center = state[c, z, part, :]
                grad_x = product(dealias_x[part, :], rounded[c, z])
                grad_y = product(rounded[c, z, part, :], dealias_y[...])
                change = -(u * grad_x + v * grad_y + still * center)
                if rising is not None:
                    change += rising * state[c, z + 1, part, :]
                if sinking is not None:
                    change += sinking * state[c, z - 1, part, :]
                put(c, z, part, center, change)


def folded(block, sign):
    mid = block.shape[0] // 2
    return block[:mid] + sign * block[mid:]


def source_spectra(state, out, half, slope_x, slope_y, into_x, into_y):
    depth = state.shape[1]
    sign = (1 - 2 * half).astype(full_type)
    slope, into = slope_x[half], into_x[half]
    lifted = [folded(state[2, z], sign) for z in range(depth)]
    sources = []
    for z in range(depth):
        spread = from_left(slope, folded(state[0, z], sign))
        spread += from_right(folded(state[1, z], sign), slope_y)
        sources.append(spread + lifted[z] - (lifted[z - 1] if z else 0.0))
    sources.append(lifted[depth - 1])
    for z, source in enumerate(sources):
        out[z] = from_right(from_left(into, source), into_y)


def edges_kernel(velocity, low, high):
    depth = velocity.shape[1]
    low[...] = velocity[:, depth - 1]
    high[...] = velocity[:, 0]


def columns_kernel(index, velocity, columns, columns_low, columns_high):
    depth = velocity.shape[1]

    def one(i, carry):
        row = pl.ds(index[i], 1)
        here = pl.ds(i, 1)
        for c in range(3):
            for z in range(depth):
                taken = velocity[c, z, row, :]
                columns[c, z, here, :] = taken
                if z == depth - 1:
                    columns_low[c, here, :] = taken
                if z == 0:
                    columns_high[c, here, :] = taken
        return carry

    lax.fori_loop(0, index.shape[0], one, 0, unroll=8)


def insert_rows(index, pairs):
    def one(i, carry):
        row = pl.ds(index[i], 1)
        for target, rows in pairs:
            for c in range(3):
                target[c, row, :] = rows[c, pl.ds(i, 1), :]
        return carry

    lax.fori_loop(0, index.shape[0], one, 0, unroll=8)


def inner_kernel(flags, index, given, columns, viscosity, mask, dealias_x, dealias_y, *refs):
    depth = given.shape[1]
    earlier = refs[0] if len(refs) == 5 else None
    partial, weights, state, rounded = refs[-4:]
    is_farm = flags[0]
    state[...] = given[...]

    @pl.when(is_farm == 1)
    def _():
        insert_rows(index, [(state.at[:, z], columns.at[:, z]) for z in range(depth)])

    drag = drag_coef * is_farm.astype(full_type)
    share = 1.0 if earlier is None else 0.5

    def put(c, z, part, center, change):
        moved = center + step_size * change
        if earlier is not None:
            moved = 0.5 * (earlier[c, z, part, :] + moved)
        partial[c, z, part, :] = moved

    tendency_steps(state, rounded, viscosity, mask, drag, dealias_x, dealias_y, put)
    weights[0] = share * step_size * (viscosity[0] + 0.5 * state[2, 0])
    weights[1] = share * step_size * (viscosity[depth - 1] - 0.5 * state[2, depth - 1])


def add_ghosts(
    flags, index, partial, weights, low, high, columns_low, columns_high, middle,
):
    depth = middle.shape[1]
    is_farm, is_lid = flags[0], flags[3]
    for c in range(3):
        for z in range(depth):
            moved = partial[c, z]
            if z == 0:
                moved += weights[0] * low[c]
            if z == depth - 1:
                moved += weights[1] * high[c]
                if c == 2:
                    moved = jnp.where(is_lid == 1, 0.0, moved)
            middle[c, z] = moved

    @pl.when(is_farm == 1)
    def _():
        def one(i, carry):
            row = pl.ds(index[i], 1)
            here = pl.ds(i, 1)
            for c in range(3):
                lag = columns_low[c, here, :] - low[c, row, :]
                middle[c, 0, row, :] += weights[0, row, :] * lag
                lag = columns_high[c, here, :] - high[c, row, :]
                middle[c, depth - 1, row, :] += weights[1, row, :] * lag
            return carry

        lax.fori_loop(0, index.shape[0], one, 0, unroll=8)


def outer_kernel(
    flags, index, partial, weights, low, high, columns_low, columns_high,
    slope_x, slope_y, into_x, into_y,
    middle, theirs, downward,
):
    add_ghosts(
        flags, index, partial, weights, low, high, columns_low, columns_high, middle
    )
    downward[0] = middle[0, 0]
    downward[1] = middle[1, 0]
    source_spectra(middle, theirs, 1 - flags[1], slope_x, slope_y, into_x, into_y)


def second_outer_kernel(
    flags, index, partial, weights, low_change, high_change, columns_low, columns_high,
    slope_x, slope_y, into_x, into_y, corrected, from_below, from_above,
    middle, theirs,
    low, high,
):
    ghost_levels(
        flags, corrected, low_change, high_change, from_below, from_above, slope_x, slope_y,
        low, high,
    )
    add_ghosts(
        flags, index, partial, weights, low, high, columns_low, columns_high, middle
    )
    source_spectra(middle, theirs, 1 - flags[1], slope_x, slope_y, into_x, into_y)


def own_spectra_kernel(flags, middle, slope_x, slope_y, into_x, into_y, mine, *edges):
    depth = middle.shape[1]
    mid = middle.shape[2] // 2
    source_spectra(middle, mine, flags[1], slope_x, slope_y, into_x, into_y)
    if not edges:
        return
    (upward,) = edges
    top = depth - 1
    even, odd = (
        0.5 * from_left(slope_x[half], folded(middle[2, top], 1.0 - 2.0 * half))
        for half in range(2)
    )
    upward[0, :mid] = middle[0, top, :mid] + (even + odd)
    upward[0, mid:] = middle[0, top, mid:] + (even - odd)
    upward[1] = middle[1, top] + from_right(middle[2, top], slope_y)


def chip_levels(core, mine, other, depth):
    is_low = core == 0
    low = [jnp.where(is_low, mine[i], other[i]) for i in range(depth + 1)]
    high = [jnp.where(is_low, other[i], mine[i]) for i in range(depth + 1)]
    levels = low[:depth] + [high[0] - low[depth]] + high[1:depth]
    return levels, low[depth], high[depth]


class Coefficients:
    def __init__(self, stacked, count):
        self.mu = lambda: stacked[0]
        self.phi = lambda i: stacked[1 + i]
        self.psi = lambda i: stacked[2 + count + i]
        self.flux_low = lambda i: stacked[3 + 2 * count + i]
        self.flux_high = lambda i: stacked[3 + 3 * count + i]
        self.entry = lambda: stacked[4 + 4 * count]
        self.scale = lambda: stacked[5 + 4 * count]


def gather_kernel(flags, mine, other, stacked, out, work, packed, sems):
    core = flags[1]
    depth = mine.shape[0] - 1
    count = 2 * depth
    tables = Coefficients(stacked, count)
    levels, _, top = chip_levels(core, mine, other, depth)
    mu = tables.mu()
    forward = tables.phi(0) * levels[0]
    for i in range(1, count):
        forward = mu * forward + tables.phi(i) * levels[i]
    work[0] = mu * forward - tables.phi(count) * top
    backward = -tables.psi(count) * top
    for i in reversed(range(count)):
        backward = tables.psi(i) * levels[i] + mu * backward
    work[1] = backward
    chips = out.shape[0]
    rows = out.shape[1] // 2
    for chip in range(chips):
        packed[chip, :rows] = work[0, chip * rows : (chip + 1) * rows]
        packed[chip, rows:] = work[1, chip * rows : (chip + 1) * rows]
    copy = pltpu.make_async_copy(packed, out, sems.at[0])
    copy.start()
    copy.wait()


def scan_kernel(received, ratio, out, taken, packed, sems):
    chips = received.shape[0]
    rows = received.shape[1] // 2
    copy = pltpu.make_async_copy(received, taken, sems.at[0])
    copy.start()
    factor = ratio[...]
    copy.wait()
    carried = jnp.zeros_like(factor)
    for chip in range(chips):
        packed[chip, :rows] = carried
        carried = factor * carried + taken[chip, :rows]
    carried = jnp.zeros_like(factor)
    for chip in reversed(range(chips)):
        packed[chip, rows:] = carried
        carried = factor * carried + taken[chip, rows:]
    copy = pltpu.make_async_copy(packed, out, sems.at[1])
    copy.start()
    copy.wait()


def solve_kernel(flags, mine, other, stacked, received, own, partner, work, scanned, sems):
    core = flags[1]
    depth = mine.shape[0] - 1
    count = 2 * depth
    tables = Coefficients(stacked, count)
    chips = scanned.shape[0]
    rows = scanned.shape[1] // 2
    copy = pltpu.make_async_copy(received, scanned, sems.at[0])
    copy.start()
    copy.wait()
    for chip in range(chips):
        work[0, chip * rows : (chip + 1) * rows] = scanned[chip, :rows]
        work[1, chip * rows : (chip + 1) * rows] = scanned[chip, rows:]
    levels, between, top = chip_levels(core, mine, other, depth)
    mu = tables.mu()
    forward = [work[0] + tables.phi(0) * levels[0]]
    for i in range(1, count):
        forward.append(mu * forward[-1] + tables.phi(i) * levels[i])
    backward = [work[1] - tables.psi(count) * top]
    for i in reversed(range(1, count)):
        backward.append(tables.psi(i) * levels[i] + mu * backward[-1])
    backward.reverse()
    flux = [
        tables.flux_low(i) * forward[i] - tables.flux_high(i + 1) * backward[i]
        for i in range(count)
    ]
    under = tables.entry() * work[0] - tables.flux_high(0) * (
        tables.psi(0) * levels[0] + mu * backward[0]
    )
    pressure = [
        -tables.scale() * (tables.psi(i) * forward[i] + mu * tables.phi(i) * backward[i])
        for i in (0, depth)
    ]
    low = [pressure[0], *flux[:depth], under]
    high = [pressure[1], *flux[depth:], flux[depth - 1] - between]
    is_low = core == 0
    for i in range(own.shape[0]):
        own[i] = jnp.where(is_low, low[i], high[i])
        partner[i] = jnp.where(is_low, high[i], low[i])


def physical_half(fields, half, ghosts, from_x, from_y, from_slope_x, from_slope_y, slots):
    depth = fields.shape[0] - (2 if ghosts else 1)
    level = fields[0]
    pressures = [level - fields[depth + 1]] if ghosts else []
    for z in range(depth):
        pressures.append(level)
        level = level + fields[1 + z]
    if ghosts:
        pressures.append(level)
    for i, block in enumerate(pressures):
        slots[2 * i] = from_left(from_slope_x[half], from_right(block, from_y))
        slots[2 * i + 1] = from_left(from_x[half], from_right(block, from_slope_y))
    for i in range(fields.shape[0] - 1):
        block = from_right(fields[1 + i], from_y)
        slots[2 * len(pressures) + i] = from_left(from_x[half], block)


def own_half_kernel(flags, mine, from_x, from_y, from_slope_x, from_slope_y, slots, *, ghosts):
    physical_half(mine, flags[1], ghosts, from_x, from_y, from_slope_x, from_slope_y, slots)


def unfolded(core, mine, other, i):
    sign = (1 - 2 * core).astype(full_type)
    return mine[i] + other[i], sign * (mine[i] - other[i])


def fringe_kernel(
    flags, index, mine, other, middle, rows_x, rows_slope_x, from_y, from_slope_y,
    columns, columns_low, columns_high,
):
    core = flags[1]
    depth = middle.shape[1]
    count = rows_x.shape[2]
    slopes = [0.0] * depth
    plains = [0.0] * depth
    lifts = [0.0] * depth
    for half in range(2):
        fields = [jnp.where(core == half, mine[i], other[i]) for i in range(1 + depth)]
        single = jnp.concatenate([rows_x[half, 0], rows_x[half, 1]])
        both = jnp.concatenate([rows_slope_x[half, 0], single, rows_slope_x[half, 1]])
        level = fields[0]
        for z in range(depth):
            high, low = halves(level)
            by_high = product(both, high)
            by_low = product(both[: 2 * count], low)
            slopes[z] += by_high[:count] + by_high[3 * count :] + by_low[:count]
            plains[z] += by_high[count : 2 * count] + by_high[2 * count : 3 * count]
            plains[z] += by_low[count:]
            high, low = halves(fields[1 + z])
            by_high = product(single, high)
            lifts[z] += by_high[:count] + by_high[count:] + product(single[:count], low)
            level = level + fields[1 + z]
    through = from_right(jnp.concatenate(slopes + lifts), from_y)
    across = from_right(jnp.concatenate(plains), from_slope_y)
    for z in range(depth):
        columns[0, z] = through[z * count : (z + 1) * count]
        columns[1, z] = across[z * count : (z + 1) * count]
        columns[2, z] = through[(depth + z) * count : (depth + z + 1) * count]

    def one(i, carry):
        row = pl.ds(index[i], 1)
        here = pl.ds(i, 1)
        for c in range(3):
            for z in range(depth):
                value = middle[c, z, row, :] - columns[c, z, here, :]
                columns[c, z, here, :] = value
                if z == depth - 1:
                    columns_low[c, here, :] = value
                if z == 0:
                    columns_high[c, here, :] = value
        return carry

    lax.fori_loop(0, index.shape[0], one, 0, unroll=8)


def corrected_kernel(
    flags, slots, fields, middle, from_x, from_y, from_slope_x, from_slope_y,
    out, low_change, high_change,
    others,
):
    core = flags[1]
    depth = middle.shape[1]
    mid = middle.shape[2] // 2
    physical_half(
        fields, 1 - core, True, from_x, from_y, from_slope_x, from_slope_y, others
    )
    pressures = depth + 2
    sides = (slice(0, mid), slice(mid, 2 * mid))
    for z in range(depth):
        for c in range(3):
            slot = 2 * (1 + z) + c if c < 2 else 2 * pressures + z
            for side, change in zip(sides, unfolded(core, slots, others, slot)):
                out[c, z, side] = middle[c, z, side] - change
    for c in range(3):
        slot = c if c < 2 else 2 * pressures + depth
        for side, change in zip(sides, unfolded(core, slots, others, slot)):
            low_change[c, side] = change
    for c in range(2):
        slot = 2 * (depth + 1) + c
        for side, change in zip(sides, unfolded(core, slots, others, slot)):
            high_change[c, side] = change


def ghost_levels(
    flags, out, low_change, high_change, from_below, from_above, slope_x, slope_y,
    low, high,
):
    is_floor, is_lid = flags[2], flags[3]
    depth = out.shape[1]
    mid = out.shape[2] // 2
    open_low = (1 - is_floor).astype(full_type)
    open_high = (1 - is_lid).astype(full_type)
    for c in range(2):
        low[c] = open_low * (from_below[c] - low_change[c])
        high[c] = open_high * (from_above[c] - high_change[c])
    low[2] = -open_low * low_change[2]
    even, odd = (
        0.5 * from_left(slope_x[half], folded(high[0], 1.0 - 2.0 * half)) for half in range(2)
    )
    sides = (slice(0, mid), slice(mid, 2 * mid))
    for side, change in zip(sides, (even + odd, even - odd)):
        spread = change + from_right(high[1, side], slope_y)
        high[2, side] = open_high * (out[2, depth - 1, side] - spread)


def last_kernel(
    flags, slots, fields, final, from_x, from_y, from_slope_x, from_slope_y,
    out,
    held, sems,
):
    core = flags[1]
    depth = final.shape[1]
    mid = final.shape[2] // 2
    half = 1 - core
    sign = (1 - 2 * core).astype(full_type)
    level = fields[0]
    copies = []
    for z in range(depth):
        lift = fields[1 + z]
        for c, (block, left, right) in enumerate(
            ((level, from_slope_x, from_y), (level, from_x, from_slope_y), (lift, from_x, from_y))
        ):
            other = from_left(left[half], from_right(block, right))
            mine = slots[2 * z + c if c < 2 else 2 * depth + z]
            held[c, z, :mid] = final[c, z, :mid] - (mine + other)
            held[c, z, mid:] = final[c, z, mid:] - sign * (mine - other)
            copy = pltpu.make_async_copy(held.at[c, z], out.at[c, z], sems.at[3 * z + c])
            copy.start()
            copies.append(copy)
        level = level + lift
    for copy in copies:
        copy.wait()


def coefficients(decay, first_level, count, height):
    def gap(steps):
        return -jnp.expm1(-steps * decay)

    still = decay == 0.0
    below = jnp.arange(count + 1, dtype=full_type)[:, None, None] + first_level
    mu = jnp.exp(-decay)
    safe = jnp.where(still, 1.0, gap(2.0 * height))

    def ratio(steps):
        return jnp.where(still, steps / height, gap(2.0 * steps) / safe)

    share = 1.0 / (1.0 + mu)
    phi = 1.0 + jnp.exp(-(2.0 * below + 1.0) * decay)
    psi = 1.0 + jnp.exp(-(2.0 * (height - below) - 1.0) * decay)
    flux_low = mu * share * ratio(height - 1.0 - below[:count])
    flux_high = mu * share * ratio(below)
    entry = share * ratio(height - below[:1])
    scale = jnp.where(still, 0.0, mu / (jnp.where(still, 1.0, gap(2.0)) * safe))
    return jnp.concatenate([mu[None], phi, psi, flux_low, flux_high, entry, scale[None]])


def local(velocity, eddy_viscosity, turbine_mask, fringe_columns):
    current = velocity[0]
    viscosity = eddy_viscosity[0]
    _, depth, length_x, length_y = current.shape
    mid = length_x // 2
    fringe = fringe_columns.shape[0]
    chips = lax.axis_size("chip")
    devices = 2 * chips
    height = devices * depth
    count = 2 * depth
    rows = mid // chips
    section = lax.axis_index("sec")
    chip = lax.axis_index("chip")
    core = lax.axis_index("core")
    place = 2 * chip + core
    is_farm = section == 1
    flags = jnp.stack([is_farm, core, place == 0, place == devices - 1]).astype(jnp.int32)
    tables = {name: jnp.asarray(table) for name, table in build_tables(length_x, length_y).items()}

    upward_route = [(i, i + 1) for i in range(devices - 1)]
    downward_route = [(i + 1, i) for i in range(devices - 1)]
    swap = [(0, 1), (1, 0)]

    def across(shift):
        return [
            (i, devices + i + shift) for i in range(devices) if 0 <= i + shift < devices
        ]

    state_shape = (3, depth + 2, length_x, length_y)
    own_shape = shaped(3, depth, length_x, length_y)
    edge = shaped(2, length_x, length_y)
    whole_edge = shaped(3, length_x, length_y)
    band = shaped(3, fringe, length_y)
    bands = (shaped(3, depth, fringe, length_y), band, band)
    decay = lax.dynamic_index_in_dim(tables["decay"], core, 0, keepdims=False)
    stacked = coefficients(decay, (chip * count).astype(full_type), count, float(height))
    ratio = jnp.exp(-float(count) * lax.dynamic_slice_in_dim(decay, chip * rows, rows, 0))

    low, high = call(edges_kernel, (whole_edge, whole_edge), [vmem()], [], 0, (current,))
    low, high, held = lax.optimization_barrier((low, high, current))
    low = lax.ppermute(low, levels_axis, upward_route)
    high = lax.ppermute(high, levels_axis, downward_route)
    farm_downward = [(devices + i + 1, devices + i) for i in range(devices - 1)]

    held, stacked = lax.optimization_barrier((held, stacked))
    taken = [*call(columns_kernel, bands, [smem(), vmem()], [], 0, (fringe_columns, held))]
    columns = lax.ppermute(taken[0], every_axis, across(0))
    away = jnp.where(fringe_columns < mid, 1.0, -1.0)[:, None]
    signs = jnp.stack([jnp.ones_like(away), away])[:, None].astype(half_type)
    rows_x, rows_slope_x = (
        jnp.take(tables[name], fringe_columns % mid, axis=2) * signs
        for name in ("from_x", "from_slope_x")
    )

    rows_x, taken[1] = lax.optimization_barrier((rows_x, taken[1]))
    columns_low = lax.ppermute(taken[1], every_axis, across(1))
    columns_high = lax.ppermute(columns[:, 0], every_axis, farm_downward)
    block = length_x * length_y * 2
    spectrum = shaped(depth + 1, mid, length_y)
    message = shaped(chips, 2 * rows, length_y)
    tendency_tables = [tables["dealias_x"], tables["dealias_y"]]
    source_tables = [tables[n] for n in ("slope_x", "slope_y", "into_x", "into_y")]
    pressure_tables = [tables[n] for n in ("from_x", "from_y", "from_slope_x", "from_slope_y")]

    packed = pltpu.VMEM(message.shape, full_type)
    halved = pltpu.VMEM((2, mid, length_y), full_type)

    def solve(mine, other, fields, beside=()):
        (sums,) = call(
            gather_kernel, (message,), [smem(), vmem(), vmem(), vmem()],
            [halved, packed, pltpu.SemaphoreType.DMA((1,))], 8 * count * block,
            (flags, mine, other, stacked), (hbm(),),
        )
        sums = lax.all_to_all(sums, "chip", split_axis=0, concat_axis=0, tiled=True)
        (sums,) = call(
            scan_kernel, (message,), [hbm(), vmem()],
            [packed, packed, pltpu.SemaphoreType.DMA((2,))], 4 * block, (sums, ratio), (hbm(),),
        )
        if beside:
            upward, from_above = beside
            sums, from_above = lax.optimization_barrier((sums, from_above))
            beside = (upward, from_above)
        sums = lax.all_to_all(sums, "chip", split_axis=0, concat_axis=0, tiled=True)
        solved = shaped(fields, mid, length_y)
        own, partner = call(
            solve_kernel, (solved, solved), [smem()] + [vmem()] * 3 + [hbm()],
            [halved, packed, pltpu.SemaphoreType.DMA((1,))], 16 * count * block,
            (flags, mine, other, stacked, sums),
        )
        own, *beside = lax.optimization_barrier((own, *beside))
        partner = lax.ppermute(partner, "core", swap)
        ghosts = bool(beside)
        half_fields = 3 * depth + (5 if ghosts else 0)
        (slots,) = call(
            functools.partial(own_half_kernel, ghosts=ghosts),
            (shaped(half_fields, mid, length_y),), [smem()] + [vmem()] * 5, [],
            0,
            (flags, own, *pressure_tables),
        )
        return own, partner, slots, *beside

    rounded = pltpu.VMEM((3, depth, length_x, length_y), half_type)
    state = pltpu.VMEM(state_shape, full_type)
    tendency_flops = 3 * depth * block * (length_x + length_y)
    source_flops = 3 * depth * block * (length_x + 2 * length_y)

    def inner(state, columns, earlier):
        kept = () if earlier else (own_shape,)
        return call(
            inner_kernel,
            (own_shape, edge, *kept),
            [smem(), smem()] + [vmem()] * (6 + len(earlier)),
            ([pltpu.VMEM(own_shape.shape, full_type)] if earlier else []) + [rounded],
            tendency_flops,
            (flags, fringe_columns, state, columns, viscosity, turbine_mask, *tendency_tables,
             *earlier),
        )

    partial, weights, start = inner(current, columns, ())
    partial, stacked, ratio, rows_x, rows_slope_x = lax.optimization_barrier(
        (partial, stacked, ratio, rows_x, rows_slope_x)
    )

    def spectra(partial, weights, low, high, columns_low, columns_high, more=()):
        middle, theirs, *downward = call(
            second_outer_kernel if more else outer_kernel,
            (own_shape, spectrum) if more else (own_shape, spectrum, edge),
            [smem(), smem()] + [vmem()] * (10 + len(more)),
            [pltpu.VMEM(whole_edge.shape, full_type)] * 2 if more else [],
            source_flops // 2,
            (flags, fringe_columns, partial, weights, low, high, columns_low, columns_high,
             *source_tables, *more),
        )
        other = lax.ppermute(theirs, "core", swap)
        mine, *upward = call(
            own_spectra_kernel,
            (spectrum,) if more else (spectrum, edge),
            [smem()] + [vmem()] * 5,
            [],
            source_flops // 2,
            (flags, middle, *source_tables),
        )
        return middle, mine, other, *upward, *downward

    middle, mine, other, upward, downward = spectra(
        partial, weights, low, high, columns_low, columns_high
    )
    from_above = lax.ppermute(downward, levels_axis, downward_route)
    own, partner, slots, upward, from_above = solve(mine, other, depth + 2, (upward, from_above))
    from_below = lax.ppermute(upward, levels_axis, upward_route)
    taken = call(
        fringe_kernel, bands, [smem(), smem()] + [vmem()] * 7, [],
        9 * depth * block * (length_x + length_y) // 8,
        (flags, fringe_columns, own, partner, middle, rows_x, rows_slope_x,
         tables["from_y"], tables["from_slope_y"]),
    )
    partner, *taken = lax.optimization_barrier((partner, *taken))
    new_columns = lax.ppermute(taken[0], every_axis, across(0))
    new_columns_low = lax.ppermute(taken[1], every_axis, across(1))
    new_columns_high = lax.ppermute(taken[2], every_axis, across(-1))
    half_fields = 3 * depth + 5
    corrected, low_change, high_change = call(
        corrected_kernel,
        (own_shape, whole_edge, edge),
        [smem()] + [vmem()] * 7,
        [pltpu.VMEM((half_fields, mid, length_y), full_type)],
        0,
        (flags, slots, partner, middle, *pressure_tables),
    )
    new_columns, corrected = lax.optimization_barrier((new_columns, corrected))
    partial, weights = inner(corrected, new_columns, (start,))
    partial, from_below, from_above = lax.optimization_barrier((partial, from_below, from_above))
    final, mine, other = spectra(
        partial, weights, low_change, high_change, new_columns_low, new_columns_high,
        (corrected, from_below, from_above),
    )
    _, partner, slots = solve(mine, other, depth + 1)
    half_fields = 3 * depth
    (new,) = call(
        last_kernel,
        (own_shape,),
        [smem()] + [vmem()] * 7,
        [pltpu.VMEM(own_shape.shape, full_type), pltpu.SemaphoreType.DMA((half_fields,))],
        3 * half_fields * block * (length_x // 2 + length_y) // 2,
        (flags, slots, partner, final, *pressure_tables),
        (hbm(),),
    )
    return new[None]


def solution(mesh):
    sections, devices = mesh.devices.shape
    fine = Mesh(mesh.devices.reshape(sections, devices // 2, 2), every_axis)
    placed = (
        P("sec", None, levels_axis, None, None),
        P("sec", levels_axis, None, None),
        P(levels_axis, None, None),
        P(),
    )
    return jax.shard_map(
        local,
        mesh=fine,
        in_specs=placed,
        out_specs=P("sec", None, levels_axis, None, None),
        check_vma=False,
    )
```
